256 devices in a mesh: cam: 8 (over x, y_hi), brick: 32 (over z, y_lo, core).
Axes of the slice: x: 4, y: 4 (y_hi: 2, y_lo: 2; y = y_hi * 2 + y_lo), z: 8, core: 2. Of those that a mesh axis runs over, the one named last changes fastest.
Arguments:
- raw_frames: bfloat16 [512, 256, 2048], P(('cam', 'brick')), may hold values from 2.4 to 12
- frame_order: int32 [256, 2], P(('cam', 'brick')), may hold values from 0 to 1, each once within a row
- dark_frame: bfloat16 [256, 2048], replicated, may hold values from 0 to 0.5
- flat_gain: bfloat16 [256, 2048], replicated, may hold values from 0.75 to 1.25
- stripe_band: float32 [9, 2048], replicated, may hold values from -0.015 to 0.015
- shear_offset: int32 [512], P('cam'), may hold values from 0 to 511
- shear_fraction: float32 [512], P('cam'), may hold values from 0 to 1
- band_index: int32 [512], replicated, may hold values from 0 to 7
- psf_bank: float32 [8, 13], replicated, may hold values from 0.2 to 1
- lateral_psf: float32 [9], replicated, may hold values from 0.2 to 1
Outputs:
- restored: bfloat16 [512, 256, 2048], P('cam', 'brick')
The draws below stay inside these ranges and needn't reach their ends.
Inputs may be any that keep to these rules, and one draw needn't show every extreme that they name: Each row of frame_order names every number of 0 to 1 once.
All inputs are finite; a program needn't handle non-finite values.
Results may differ from the reference program's by a relative error of at most 0.005.
Values may be sent and summed in bfloat16 or wider, within the bound.
No kernel may reach another device: no remote copies, remote signals or barrier semaphores. Data moves between devices by JAX's collectives and lax.ppermute only.
A program may use at most 128 MiB of HBM per device.

```python
import jax
import jax.numpy as jnp
from jax import lax

W = 2048
ROWS = 256
F_DEV = 2
STRIPE_HALF = 4
LAT_HALF = 4
PSF_HALF = 6
BANK = 8
SHEAR = 512
ITERS = 2
BLOCKS = 256
FRAMES = 512
N_BRICK = 32


def draw_shear_offset(key, part):
    key = jax.random.fold_in(key, 7)
    first_key, second_key = jax.random.split(key)
    offsets = jax.random.randint(first_key, (FRAMES,), 0, SHEAR, dtype=jnp.int32)
    location = jax.random.randint(second_key, (), 0, FRAMES, dtype=jnp.int32)
    offsets = offsets.at[location].set(SHEAR - 1)
    offsets = offsets.at[(location + 1) % FRAMES].set(0)
    return offsets


def draw_raw_frames(key, part):
    key = jax.random.fold_in(key, 11)
    level_key, patch_key, pixel_key = jax.random.split(key, 3)
    patch_rows = ROWS // 8
    patch_cols = W // 8
    level_draw = jax.random.uniform(level_key, (FRAMES, 1, 1, 1, 1), jnp.float32)
    patch_draw = jax.random.uniform(patch_key, (FRAMES, patch_rows, 1, patch_cols, 1), jnp.float32)
    pixel_draw = jax.random.uniform(pixel_key, (FRAMES, patch_rows, 8, patch_cols, 8), jnp.float32)
    level = 3.0 + 2.0 * level_draw
    patch = jnp.exp(0.69314718 * patch_draw)
    pixel = 0.8 + 0.4 * pixel_draw
    values = level * patch * pixel
    return values.reshape(FRAMES, ROWS, W).astype(jnp.bfloat16)


def place_ends(drawn, stream_key, least, top_value):
    place = [jax.random.randint(jax.random.fold_in(stream_key, axis), (), 0, length) for axis, length in enumerate(drawn.shape)]
    longest = drawn.shape.index(max(drawn.shape))
    next_to = place[:longest] + [(place[longest] + 1) % drawn.shape[longest]] + place[longest + 1:]
    return drawn.at[tuple(place)].set(least).at[tuple(next_to)].set(top_value)


def level_of(stream_key, extent, cuts, smallest, top_value):
    loudness, own = 1.0, jax.random.fold_in(stream_key, 6)
    for dim, parts in cuts:
        draws = jnp.exp(jax.random.uniform(jax.random.fold_in(own, dim), (parts,), jnp.float32, smallest / len(cuts), top_value / len(cuts)))
        loudness = loudness * jnp.repeat(draws, extent[dim] // parts).reshape([-1 if axis == dim else 1 for axis in range(len(extent))])
    return loudness


def setup_inputs(seed: int = 0) -> dict:
    arg_keys = jax.random.split(jax.random.key(seed), 11)
    return {
        "raw_frames": draw_raw_frames(jax.random.fold_in(arg_keys[10], 71), 0),
        "frame_order": jax.vmap(lambda own: jax.random.permutation(own, F_DEV))(jax.random.split(arg_keys[1], BLOCKS)).reshape((BLOCKS, F_DEV)).astype(jnp.int32),
        "dark_frame": jnp.clip(jax.random.uniform(arg_keys[2], (ROWS, W), jnp.float32, 0.0, 0.5), 0.0, 0.5).astype(jnp.bfloat16),
        "flat_gain": jnp.clip(1.0 + 0.05 * jax.random.normal(arg_keys[3], (ROWS, W), jnp.float32), 0.75, 1.25).astype(jnp.bfloat16),
        "stripe_band": jnp.clip(jax.random.uniform(arg_keys[4], (2 * STRIPE_HALF + 1, W), jnp.float32, -0.015, 0.015), -0.015, 0.015),
        "shear_offset": draw_shear_offset(jax.random.fold_in(arg_keys[10], 71), 0),
        "shear_fraction": jnp.clip(1.0 * jax.random.uniform(arg_keys[6], (FRAMES,), jnp.float32) ** level_of(arg_keys[6], (FRAMES,), ((0, 8),), -0.2, 0.2), 0.0, 1.0),
        "band_index": place_ends(jax.random.randint(arg_keys[7], (FRAMES,), 0, BANK), jax.random.fold_in(arg_keys[7], 1), 0, BANK - 1).astype(jnp.int32),
        "psf_bank": jnp.clip(jax.random.uniform(arg_keys[8], (BANK, 2 * PSF_HALF + 1), jnp.float32, 0.2, 1.0), 0.2, 1.0),
        "lateral_psf": jnp.clip(jax.random.uniform(arg_keys[9], (2 * LAT_HALF + 1,), jnp.float32, 0.2, 1.0), 0.2, 1.0),
    }


background = 1.0


def lateral_blur(volume, kernel):
    half_span = (kernel.shape[0] - 1) // 2
    columns = volume.shape[-1]
    padded = jnp.pad(volume, ((0, 0), (0, 0), (half_span, half_span)))
    summed = jnp.zeros_like(volume)
    for tap_index in range(kernel.shape[0]):
        summed = summed + kernel[tap_index] * padded[:, :, tap_index:tap_index + columns]
    return summed


def axial_forward(volume, band_rows):
    half_span = (band_rows.shape[1] - 1) // 2
    planes = volume.shape[0]
    padded = jnp.pad(volume, ((half_span, half_span), (0, 0), (0, 0)))
    summed = jnp.zeros_like(volume)
    for tap_index in range(band_rows.shape[1]):
        summed = summed + band_rows[:, tap_index][:, None, None] * padded[tap_index:tap_index + planes]
    return summed


def axial_adjoint(volume, band_rows):
    half_span = (band_rows.shape[1] - 1) // 2
    planes = volume.shape[0]
    padded = jnp.pad(volume, ((half_span, half_span), (0, 0), (0, 0)))
    padded_rows = jnp.pad(band_rows, ((half_span, half_span), (0, 0)))
    summed = jnp.zeros_like(volume)
    for tap_index in range(band_rows.shape[1]):
        start_at = 2 * half_span - tap_index
        summed = summed + padded_rows[start_at:start_at + planes, tap_index][:, None, None] * padded[start_at:start_at + planes]
    return summed


def deskew(volume, offsets, fractions):
    leading = SHEAR + 1
    columns = volume.shape[-1]
    padded = jnp.pad(volume, ((0, 0), (0, 0), (leading, 0)))

    def slide_plane(single, amount):
        return lax.dynamic_slice_in_dim(single, leading - amount, columns, 1)

    nearer = jax.vmap(slide_plane)(padded, offsets)
    farther = jax.vmap(slide_plane)(padded, offsets + 1)
    weight = fractions[:, None, None]
    return (1.0 - weight) * nearer + weight * farther


def reference(raw_frames, frame_order, dark_frame, flat_gain, stripe_band, shear_offset, shear_fraction, band_index, psf_bank, lateral_psf):
    half_rows = STRIPE_HALF
    dark_level = dark_frame.astype(jnp.float32)
    gain_level = flat_gain.astype(jnp.float32)

    def destripe_block(block):
        flattened = (block.astype(jnp.float32) - dark_level) * gain_level
        padded = jnp.pad(flattened, ((0, 0), (half_rows, half_rows), (0, 0)))
        summed = flattened
        for tap_index in range(2 * half_rows + 1):
            summed = summed + stripe_band[tap_index][None, None, :] * padded[:, tap_index:tap_index + ROWS, :]
        return summed.astype(jnp.bfloat16)

    blocks = raw_frames.reshape(BLOCKS, F_DEV, ROWS, W)
    destriped = lax.map(destripe_block, blocks).reshape(FRAMES, ROWS, W)
    position = (jnp.arange(BLOCKS, dtype=jnp.int32)[:, None] * F_DEV + frame_order).reshape(-1)
    ordered = jnp.zeros_like(destriped).at[position].set(destriped)

    row_group = ROWS // N_BRICK
    lateral = lateral_psf / jnp.sum(lateral_psf)
    flipped = lateral[::-1]
    kernel_table = psf_bank / jnp.sum(psf_bank, axis=1, keepdims=True)
    per_plane = kernel_table[band_index]

    def restore(row_block):
        selected = lax.dynamic_slice_in_dim(ordered, row_block * row_group, row_group, 1).astype(jnp.float32)
        measured = deskew(selected, shear_offset, shear_fraction)
        estimate = measured
        for sweep_index in range(ITERS):
            blurred = axial_forward(lateral_blur(estimate, lateral), per_plane)
            quotient = measured / (blurred + background)
            estimate = estimate * lateral_blur(axial_adjoint(quotient, per_plane), flipped)
        return estimate.astype(jnp.bfloat16)

    pieces = lax.map(restore, jnp.arange(N_BRICK, dtype=jnp.int32))
    return jnp.transpose(pieces, (1, 0, 2, 3)).reshape(FRAMES, ROWS, W)
```

```python
import functools

import jax
import jax.numpy as jnp
from jax import lax
from jax.experimental import pallas as pl
from jax.experimental.pallas import tpu as pltpu
from jax.sharding import PartitionSpec as P

SHEAR = 512
ITERS = 2
BACKGROUND = 1.0

LANES = 128
TILE = 256
BLOCK_ROWS = 64
MARGIN = SHEAR + LANES
R = 4
VMEM = 50 * 1024 * 1024


def frame_kernel(
    order_ref, offset_ref, fraction_ref,
    raw_prev, raw_main, raw_next,
    dark_prev, dark_main, dark_next,
    gain_prev, gain_main, gain_next,
    band_ref, out0_ref, out1_ref, scratch,
):
    step = pl.program_id(0)
    steps = pl.num_programs(0)
    columns = raw_main.shape[-1]
    tiles = columns // LANES
    rows = BLOCK_ROWS + 16
    brick = lax.axis_index("brick")
    f32 = jnp.float32

    @pl.when(step == 0)
    def _():
        scratch[:, :, :MARGIN] = jnp.zeros((2, BLOCK_ROWS, MARGIN), f32)

    has_prev = (step > 0).astype(f32)
    has_next = (step < steps - 1).astype(f32)

    for place in range(2):
        frame = jnp.where(order_ref[0, 0] == place, 0, 1)

        def destripe(tile, _):
            cols = pl.ds(pl.multiple_of(tile * LANES, LANES), LANES)

            def flat(raw, dark, gain):
                return (raw[frame, :, cols].astype(f32) - dark[:, cols].astype(f32)) * gain[
                    :, cols
                ].astype(f32)

            above = flat(raw_prev, dark_prev, gain_prev)[8:16] * has_prev
            below = flat(raw_next, dark_next, gain_next)[0:8] * has_next
            here = flat(raw_main, dark_main, gain_main)
            f = jnp.concatenate([above, here, below], axis=0)
            after = pltpu.roll(f, rows - 1, 0)
            before = pltpu.roll(f, 1, 0)
            band = band_ref[:, cols]

            def three(k):
                return band[k : k + 1] * before + band[k + 1 : k + 2] * f + band[k + 2 : k + 3] * after

            out = (
                f
                + three(3)
                + pltpu.roll(three(6), rows - 3, 0)
                + pltpu.roll(three(0), 3, 0)
            )
            scratch[place, :, pl.ds(pl.multiple_of(MARGIN + tile * LANES, LANES), LANES)] = out[
                8 : 8 + BLOCK_ROWS
            ]
            return 0

        lax.fori_loop(0, tiles, destripe, 0)

    lane = lax.broadcasted_iota(jnp.int32, (BLOCK_ROWS, LANES), 1)
    bricks = BLOCK_ROWS // 8
    upper = lax.broadcasted_iota(jnp.int32, (bricks, 8, LANES), 1) < 4
    amounts = [offset_ref[brick * 2 + place] for place in range(2)]
    weights = [fraction_ref[brick * 2 + place] for place in range(2)]

    def turned(place, tile):
        whole = amounts[place] // LANES
        part = amounts[place] % LANES
        start = MARGIN + (tile - whole) * LANES
        x = scratch[place, :, pl.ds(pl.multiple_of(start, LANES), LANES)]
        return pltpu.roll(x, part, 1), pltpu.roll(x, (part + 1) % LANES, 1)

    def deskew(tile, carry):
        values = []
        following = []
        for place in range(2):
            part = amounts[place] % LANES
            now = turned(place, tile)
            last = carry[place]
            near = jnp.where(lane < part, last[0], now[0])
            far = jnp.where(lane < part + 1, last[1], now[1])
            mixed = (1.0 - weights[place]) * near + weights[place] * far
            values.append(mixed.reshape(bricks, 8, LANES))
            following.append(now)
        cols = pl.ds(pl.multiple_of(tile * LANES, LANES), LANES)
        out0 = jnp.where(upper, values[0], pltpu.roll(values[1], 4, 1))
        out1 = jnp.where(upper, pltpu.roll(values[0], 4, 1), values[1])
        out0_ref[:, :, cols] = out0.astype(jnp.bfloat16)
        out1_ref[:, :, cols] = out1.astype(jnp.bfloat16)
        return tuple(following)

    lax.fori_loop(0, tiles, deskew, tuple(turned(place, -1) for place in range(2)))


def frame_side(raw, order, dark, gain, band, offset, fraction):
    _, frame_rows, columns = raw.shape
    steps = frame_rows // BLOCK_ROWS
    bricks = frame_rows // 8
    per = BLOCK_ROWS // 16
    last = frame_rows // 16 - 1
    smem = pl.BlockSpec(memory_space=pltpu.SMEM)

    def three(lead):
        zeros = (0,) * len(lead)
        return [
            pl.BlockSpec(lead + (16, columns), lambda i: zeros + (jnp.maximum(per * i - 1, 0), 0)),
            pl.BlockSpec(lead + (BLOCK_ROWS, columns), lambda i: zeros + (i, 0)),
            pl.BlockSpec(lead + (16, columns), lambda i: zeros + (jnp.minimum(per * i + per, last), 0)),
        ]

    piece = jax.ShapeDtypeStruct((bricks, 8, columns), jnp.bfloat16)
    piece_spec = pl.BlockSpec((BLOCK_ROWS // 8, 8, columns), lambda i: (i, 0, 0))
    return pl.pallas_call(
        frame_kernel,
        grid=(steps,),
        in_specs=[smem, smem, smem]
        + three((2,)) + three(()) + three(())
        + [pl.BlockSpec(band.shape, lambda i: (0, 0))],
        out_specs=[piece_spec, piece_spec],
        out_shape=[piece, piece],
        scratch_shapes=[pltpu.VMEM((2, BLOCK_ROWS, MARGIN + columns), jnp.float32)],
        compiler_params=pltpu.CompilerParams(vmem_limit_bytes=VMEM),
        cost_estimate=pl.CostEstimate(flops=30_000_000, bytes_accessed=6_500_000, transcendentals=0),
        name="frame_side",
    )(order, offset, fraction, raw, raw, raw, dark, dark, dark, gain, gain, gain, band)


def bands_kernel(taps, lat_taps, psf_ref, lateral_ref, index_ref, g_ref, gt_ref, tl_ref, tm_ref):
    size = g_ref.shape[0]
    f32 = jnp.float32
    index = index_ref[...]
    raw = []
    for tap in range(taps):
        value = jnp.zeros(index.shape, f32)
        for kernel in range(psf_ref.shape[0]):
            value = jnp.where(index == kernel, psf_ref[kernel, tap], value)
        raw.append(value)
    total = functools.reduce(lambda a, b: a + b, raw)
    total = jnp.where(total > 0.0, total, 1.0)
    row = lax.broadcasted_iota(jnp.int32, (size, size), 0)
    col = lax.broadcasted_iota(jnp.int32, (size, size), 1)
    gap = row - col
    adjoint = jnp.zeros((size, size), f32)
    for tap in range(taps):
        adjoint = jnp.where(gap == R * (tap - taps // 2), raw[tap] / total, adjoint)
    gt_ref[...] = adjoint.astype(jnp.bfloat16)
    g_ref[...] = adjoint.T.astype(jnp.bfloat16)

    lateral_total = lateral_ref[0]
    for tap in range(1, lat_taps):
        lateral_total = lateral_total + lateral_ref[tap]
    k = lax.broadcasted_iota(jnp.int32, tl_ref.shape, 0)
    j = lax.broadcasted_iota(jnp.int32, tl_ref.shape, 1)
    place = k - LANES - j + lat_taps // 2
    forward = jnp.zeros(tl_ref.shape, f32)
    backward = jnp.zeros(tl_ref.shape, f32)
    for tap in range(lat_taps):
        forward = jnp.where(place == tap, lateral_ref[tap], forward)
        backward = jnp.where(place == lat_taps - 1 - tap, lateral_ref[tap], backward)
    scale = jnp.full((1, TILE), lateral_total, f32)
    tl_ref[...] = (forward / scale).astype(jnp.bfloat16)
    tm_ref[...] = (backward / scale).astype(jnp.bfloat16)


def bands(psf_bank, lateral_psf, band_index, planes, halo):
    spread = jnp.pad(band_index, (halo, halo), constant_values=-1)
    first = lax.axis_index("cam") * planes
    mine = lax.dynamic_slice_in_dim(spread, first, planes + 2 * halo, 0)
    size = (planes + 2 * halo) * R
    index = jnp.broadcast_to(mine[:, None], (planes + 2 * halo, R)).reshape(1, size)
    smem = pl.BlockSpec(memory_space=pltpu.SMEM)
    vmem = pl.BlockSpec(memory_space=pltpu.VMEM)
    square = jax.ShapeDtypeStruct((size, size), jnp.bfloat16)
    strip = jax.ShapeDtypeStruct((TILE + 2 * LANES, TILE), jnp.bfloat16)
    return pl.pallas_call(
        functools.partial(bands_kernel, psf_bank.shape[1], lateral_psf.shape[0]),
        in_specs=[smem, smem, vmem],
        out_specs=[vmem] * 4,
        out_shape=[square, square, strip, strip],
        compiler_params=pltpu.CompilerParams(vmem_limit_bytes=VMEM),
        cost_estimate=pl.CostEstimate(flops=10_000_000, bytes_accessed=2_000_000, transcendentals=0),
        name="bands",
    )(psf_bank, lateral_psf, index)


def restore_kernel(half, merge, *refs):
    low, centre, high, g, gt, tl, tm = refs[:7]
    earlier = refs[7] if merge else None
    out, mf, ef, mb, qb, pad = refs[7 + merge :]
    f32 = jnp.float32
    bf16 = jnp.bfloat16
    size, columns = mf.shape
    tiles = columns // TILE
    edge = low.shape[0] * low.shape[1]

    pad[:, :LANES] = jnp.zeros((size, LANES), bf16)
    pad[:, LANES + columns :] = jnp.zeros((size, LANES), bf16)

    def at(tile, shift=0, width=TILE):
        return pl.ds(pl.multiple_of(tile * TILE + shift, LANES), width)

    def every(body):
        lax.fori_loop(0, tiles, lambda tile, _: body(tile), None)

    def load(tile):
        cols = at(tile)
        parts = [
            ref[:, :, cols].astype(f32).reshape(-1, TILE) for ref in (low, centre, high)
        ]
        whole = jnp.concatenate(parts, axis=0)
        mf[:, cols] = whole
        mb[:, cols] = whole.astype(bf16)
        qb[:, cols] = jnp.zeros((size, TILE), bf16)

    every(load)

    def span(reach):
        lo = reach * half * R // 16 * 16
        return slice(lo, size - lo)

    for sweep in range(ITERS):
        rows = span(2 * sweep + 1)
        inner = span(2 * sweep + 2)
        final = sweep == ITERS - 1

        def axial(tile):
            r = jnp.dot(g[rows, :], mb[:, at(tile)], preferred_element_type=f32)
            pad[rows, at(tile, LANES)] = r.astype(bf16)

        def ratio(tile):
            cols = at(tile)
            b = jnp.dot(pad[rows, at(tile, 0, TILE + 2 * LANES)], tl[...], preferred_element_type=f32)
            qb[rows, cols] = (mf[rows, cols] / (b + BACKGROUND)).astype(bf16)

        def axial_back(tile):
            r = jnp.dot(gt[inner, :], qb[:, at(tile)], preferred_element_type=f32)
            pad[inner, at(tile, LANES)] = r.astype(bf16)

        def update(tile):
            cols = at(tile)
            d = jnp.dot(pad[inner, at(tile, 0, TILE + 2 * LANES)], tm[...], preferred_element_type=f32)
            source = mf if sweep == 0 else ef
            e = source[inner, cols] * d
            if not final:
                ef[inner, cols] = e
                mb[inner, cols] = e.astype(bf16)
            elif not merge:
                out[:, cols] = e.astype(bf16)
            else:
                v1 = e.reshape(-1, 8, TILE)
                v0 = earlier[:, cols].astype(f32).reshape(-1, 8, TILE)
                upper = lax.broadcasted_iota(jnp.int32, v0.shape, 1) < 4
                even = jnp.where(upper, v0, pltpu.roll(v1, 4, 1))
                odd = jnp.where(upper, pltpu.roll(v0, 4, 1), v1)
                both = jnp.stack([even, odd], axis=1).reshape(-1, 8, TILE)
                out[:, :, cols] = both.astype(bf16)

        every(axial)
        every(ratio)
        every(axial_back)
        every(update)


def restore(low, centre, high, matrices, earlier, half):
    columns = centre.shape[-1]
    planes = centre.shape[0] * 2
    size = (low.shape[0] + centre.shape[0] + high.shape[0]) * centre.shape[1]
    merge = earlier is not None
    vmem = pl.BlockSpec(memory_space=pltpu.VMEM)
    shape = (planes, 8, columns) if merge else (planes * R, columns)
    operands = (low, centre, high, *matrices) + ((earlier,) if merge else ())
    return pl.pallas_call(
        functools.partial(restore_kernel, half, merge),
        in_specs=[vmem] * len(operands),
        out_specs=vmem,
        out_shape=jax.ShapeDtypeStruct(shape, jnp.bfloat16),
        scratch_shapes=[
            pltpu.VMEM((size, columns), jnp.float32),
            pltpu.VMEM((size, columns), jnp.float32),
            pltpu.VMEM((size, columns), jnp.bfloat16),
            pltpu.VMEM((size, columns), jnp.bfloat16),
            pltpu.VMEM((size, columns + 2 * LANES), jnp.bfloat16),
        ],
        compiler_params=pltpu.CompilerParams(vmem_limit_bytes=VMEM),
        cost_estimate=pl.CostEstimate(
            flops=7_000_000_000, bytes_accessed=8_000_000, transcendentals=0
        ),
        name="restore",
    )(*operands)


def local(
    raw_frames,
    frame_order,
    dark_frame,
    flat_gain,
    stripe_band,
    shear_offset,
    shear_fraction,
    band_index,
    psf_bank,
    lateral_psf,
):
    half = psf_bank.shape[1] // 2
    planes = shear_offset.shape[0]
    halo = 2 * ITERS * half
    pieces = frame_side(
        raw_frames, frame_order, dark_frame, flat_gain, stripe_band, shear_offset, shear_fraction
    )
    count = lax.axis_size("cam")
    forward = [(i, i + 1) for i in range(count - 1)]
    backward = [(i + 1, i) for i in range(count - 1)]
    matrices = bands(psf_bank, lateral_psf, band_index, planes, halo)
    depth = halo // 2
    result = None
    for piece in pieces:
        centre = lax.all_to_all(piece, "brick", split_axis=0, concat_axis=0, tiled=True)
        low = lax.ppermute(centre[-depth:], "cam", forward)
        high = lax.ppermute(centre[:depth], "cam", backward)
        result = restore(low, centre, high, matrices, result, half)
    return result


def solution(mesh):
    placed = (
        P(("cam", "brick"), None, None),
        P(("cam", "brick"), None),
        P(),
        P(),
        P(),
        P("cam"),
        P("cam"),
        P(),
        P(),
        P(),
    )
    return jax.shard_map(
        local, mesh=mesh, in_specs=placed, out_specs=P("cam", "brick", None), check_vma=False
    )
```

```python
import functools

import jax
import jax.numpy as jnp
from jax import lax
from jax.experimental import pallas as pl
from jax.experimental.pallas import tpu as pltpu
from jax.sharding import PartitionSpec as P

SHEAR = 512
ITERS = 2
BACKGROUND = 1.0

LANES = 128
TILE = 256
ROWS = 8
BLOCK_ROWS = 64
LEAD = SHEAR // LANES + 1
SPLIT = 1280
VMEM = 60 * 1024 * 1024
GROUP = 20
SPAN = 32


def frame_kernel(
    first, count,
    order_ref, offset_ref, fraction_ref,
    raw_prev, raw_main, raw_next,
    dark_prev, dark_main, dark_next,
    gain_prev, gain_main, gain_next,
    band_ref, out_ref, scratch,
):
    step = pl.program_id(0)
    steps = pl.num_programs(0)
    rows = BLOCK_ROWS + 16
    brick = lax.axis_index("brick")
    f32 = jnp.float32
    bf16 = jnp.bfloat16
    base = first - LEAD

    @pl.when(step == 0)
    def _():
        if base < 0:
            scratch[:, :, : -base * LANES] = jnp.zeros((2, BLOCK_ROWS, -base * LANES), f32)

    has_prev = (step > 0).astype(f32)
    has_next = (step < steps - 1).astype(f32)
    frames = [jnp.where(order_ref[0, 0] == place, 0, 1) for place in range(2)]

    for tile in range(max(base, 0), first + count):
        cols = pl.ds(tile * LANES, LANES)
        band = band_ref[:, cols]
        levels = []
        for part, keep in ((0, slice(8, 16)), (1, slice(None)), (2, slice(0, 8))):
            dark = (dark_prev, dark_main, dark_next)[part][:, cols].astype(f32)[keep]
            gain = (gain_prev, gain_main, gain_next)[part][:, cols].astype(f32)[keep]
            if part != 1:
                gain = gain * (has_prev, None, has_next)[part]
            levels.append((dark, gain, keep))
        for place in range(2):
            f = jnp.concatenate(
                [
                    (raw[frames[place], :, cols].astype(f32)[keep] - dark) * gain
                    for raw, (dark, gain, keep) in zip((raw_prev, raw_main, raw_next), levels)
                ],
                axis=0,
            )
            after = pltpu.roll(f, rows - 1, 0)
            before = pltpu.roll(f, 1, 0)

            def three(k):
                return band[k : k + 1] * before + band[k + 1 : k + 2] * f + band[k + 2 : k + 3] * after

            out = (
                f
                + three(3)
                + pltpu.roll(three(6), rows - 3, 0)
                + pltpu.roll(three(0), 3, 0)
            )[8 : 8 + BLOCK_ROWS]
            scratch[place, :, pl.ds((tile - base) * LANES, LANES)] = out.astype(bf16).astype(f32)

    lane = lax.broadcasted_iota(jnp.int32, (BLOCK_ROWS, LANES), 1)
    bricks = BLOCK_ROWS // ROWS
    for place in range(2):
        amount = offset_ref[brick * 2 + place]
        weight = fraction_ref[brick * 2 + place]
        whole = amount // LANES
        part = amount % LANES
        near_mask = lane < part
        far_mask = lane < part + 1

        def turned(tile):
            start = (tile - base - whole) * LANES
            x = scratch[place, :, pl.ds(pl.multiple_of(start, LANES), LANES)]
            return (1.0 - weight) * pltpu.roll(x, part, 1), weight * pltpu.roll(x, (part + 1) % LANES, 1)

        last = turned(first - 1)
        for tile in range(first, first + count):
            now = turned(tile)
            mixed = jnp.where(near_mask, last[0], now[0]) + jnp.where(far_mask, last[1], now[1])
            last = now
            out_ref[:, place * ROWS : (place + 1) * ROWS, pl.ds((tile - first) * LANES, LANES)] = (
                mixed.reshape(bricks, ROWS, LANES).astype(bf16)
            )


def frame_side(raw, order, dark, gain, band, offset, fraction, lo, hi):
    _, frame_rows, columns = raw.shape
    steps = frame_rows // BLOCK_ROWS
    bricks = frame_rows // ROWS
    per = BLOCK_ROWS // 16
    last = frame_rows // 16 - 1
    smem = pl.BlockSpec(memory_space=pltpu.SMEM)
    first, count = lo // LANES, (hi - lo) // LANES

    def three(lead):
        zeros = (0,) * len(lead)
        return [
            pl.BlockSpec(lead + (16, columns), lambda i: zeros + (jnp.maximum(per * i - 1, 0), 0)),
            pl.BlockSpec(lead + (BLOCK_ROWS, columns), lambda i: zeros + (i, 0)),
            pl.BlockSpec(lead + (16, columns), lambda i: zeros + (jnp.minimum(per * i + per, last), 0)),
        ]

    return pl.pallas_call(
        functools.partial(frame_kernel, first, count),
        grid=(steps,),
        in_specs=[smem, smem, smem]
        + three((2,)) + three(()) + three(())
        + [pl.BlockSpec(band.shape, lambda i: (0, 0))],
        out_specs=pl.BlockSpec((BLOCK_ROWS // ROWS, 2 * ROWS, hi - lo), lambda i: (i, 0, 0)),
        out_shape=jax.ShapeDtypeStruct((bricks, 2 * ROWS, hi - lo), jnp.bfloat16),
        scratch_shapes=[pltpu.VMEM((2, BLOCK_ROWS, (LEAD + count) * LANES), jnp.float32)],
        compiler_params=pltpu.CompilerParams(vmem_limit_bytes=VMEM),
        cost_estimate=pl.CostEstimate(
            flops=8_000_000_000, bytes_accessed=6_500_000, transcendentals=0
        ),
        name="frame_side",
    )(order, offset, fraction, raw, raw, raw, dark, dark, dark, gain, gain, gain, band)


def stages(planes, half):
    total = planes + 4 * ITERS * half
    plan = []
    for reach in range(1, 2 * ITERS + 1):
        lo, hi = reach * half, total - reach * half
        plan.append([(at, min(GROUP, hi - at)) for at in range(lo, hi, GROUP)])
    return plan


def bands_kernel(taps, lat_taps, plan, psf_ref, lateral_ref, index_ref, g_ref, gt_ref, tl_ref, tm_ref):
    f32 = jnp.float32
    bf16 = jnp.bfloat16
    half = taps // 2
    width = SPAN * ROWS
    index = index_ref[...]
    raw = []
    for tap in range(taps):
        value = jnp.zeros(index.shape, f32)
        for kernel in range(psf_ref.shape[0]):
            value = jnp.where(index == kernel, psf_ref[kernel, tap], value)
        raw.append(value)
    total = functools.reduce(lambda a, b: a + b, raw)
    total = jnp.where(total > 0.0, total, 1.0)
    unit = [value / total for value in raw]
    row = lax.broadcasted_iota(jnp.int32, (width, width), 0)
    col = lax.broadcasted_iota(jnp.int32, (width, width), 1)

    def banded(start, gap, order):
        m = jnp.zeros((width, width), f32)
        for tap in range(taps):
            values = unit[tap][:, start * ROWS : start * ROWS + width]
            m = jnp.where(gap == ROWS * order(tap), values, m)
        return m

    slot = [0, 0]
    for number, groups in enumerate(plan):
        for at, _ in groups:
            if number % 2 == 0:
                m = banded(at, row - col, lambda tap: tap).T
                g_ref[slot[0]] = m[: GROUP * ROWS].astype(bf16)
            else:
                m = banded(at - half, col - row, lambda tap: 2 * half - tap)
                gt_ref[slot[1]] = m[: GROUP * ROWS].astype(bf16)
            slot[number % 2] += 1

    lateral_total = lateral_ref[0]
    for tap in range(1, lat_taps):
        lateral_total = lateral_total + lateral_ref[tap]
    k = lax.broadcasted_iota(jnp.int32, tl_ref.shape, 0)
    j = lax.broadcasted_iota(jnp.int32, tl_ref.shape, 1)
    place = k - LANES - j + lat_taps // 2
    forward = jnp.zeros(tl_ref.shape, f32)
    backward = jnp.zeros(tl_ref.shape, f32)
    for tap in range(lat_taps):
        forward = jnp.where(place == tap, lateral_ref[tap], forward)
        backward = jnp.where(place == lat_taps - 1 - tap, lateral_ref[tap], backward)
    scale = jnp.full((1, TILE), lateral_total, f32)
    tl_ref[...] = (forward / scale).astype(bf16)
    tm_ref[...] = (backward / scale).astype(bf16)


def bands(psf_bank, lateral_psf, band_index, planes, halo):
    half = psf_bank.shape[1] // 2
    plan = stages(planes, half)
    spread = jnp.pad(band_index, (halo, halo + SPAN), constant_values=-1)
    first = lax.axis_index("cam") * planes
    length = planes + 2 * halo + SPAN
    mine = lax.dynamic_slice_in_dim(spread, first, length, 0)
    index = jnp.broadcast_to(mine[:, None], (length, ROWS)).reshape(1, length * ROWS)
    smem = pl.BlockSpec(memory_space=pltpu.SMEM)
    vmem = pl.BlockSpec(memory_space=pltpu.VMEM)
    counts = [sum(len(groups) for groups in plan[kind::2]) for kind in range(2)]
    strip = jax.ShapeDtypeStruct((TILE + 2 * LANES, TILE), jnp.bfloat16)
    return pl.pallas_call(
        functools.partial(bands_kernel, psf_bank.shape[1], lateral_psf.shape[0], plan),
        in_specs=[smem, smem, vmem],
        out_specs=[vmem] * 4,
        out_shape=[
            jax.ShapeDtypeStruct((n, GROUP * ROWS, SPAN * ROWS), jnp.bfloat16) for n in counts
        ]
        + [strip, strip],
        compiler_params=pltpu.CompilerParams(vmem_limit_bytes=VMEM),
        cost_estimate=pl.CostEstimate(
            flops=2_000_000_000, bytes_accessed=2_000_000, transcendentals=0
        ),
        name="bands",
    )(psf_bank, lateral_psf, index)


def restore_kernel(plan, kept, *refs):
    later = kept is not None
    sources = [refs[3 * i : 3 * i + 3] for i in range(2 if later else 1)]
    refs = refs[3 * len(sources) :]
    g, gt, tl, tm = refs[:4]
    earlier = refs[4] if later else None
    out, mf, ef, mb, qb, pad, pad_back = refs[4 + later :]
    f32 = jnp.float32
    bf16 = jnp.bfloat16
    size, columns = mf.shape
    tiles = columns // TILE

    for buffer in (pad, pad_back):
        buffer[:, :LANES] = jnp.zeros((size, LANES), bf16)
        buffer[:, LANES + columns :] = jnp.zeros((size, LANES), bf16)

    at_column = 0
    for source in sources:
        width = source[1].shape[-1]
        at_row = 0
        for ref in source:
            height = ref.shape[0] * ref.shape[1]
            for col in range(0, width, TILE):
                whole = ref[:, :, col : col + TILE].reshape(height, TILE)
                there = slice(at_column + col, at_column + col + TILE)
                mb[at_row : at_row + height, there] = whole
                mf[at_row : at_row + height, there] = whole.astype(f32)
            at_row += height
        at_column += width

    def columns_of(tile):
        return slice(tile * TILE, (tile + 1) * TILE)

    def within(tile):
        return slice(LANES + tile * TILE, LANES + (tile + 1) * TILE)

    def around(tile):
        return slice(tile * TILE, (tile + 1) * TILE + 2 * LANES)

    half = plan[0][0][0]

    def rows_of(groups):
        return slice(groups[0][0] * ROWS, (groups[-1][0] + groups[-1][1]) * ROWS)

    def axial(matrices, skip, groups, source, target, tile):
        for number, (first, count) in enumerate(groups):
            low = (first - half) * ROWS
            high = (first + count + half) * ROWS
            r = jnp.dot(
                matrices[skip + number, : count * ROWS, : high - low],
                source[low:high, columns_of(tile)],
                preferred_element_type=f32,
            )
            target[first * ROWS : (first + count) * ROWS, within(tile)] = r.astype(bf16)

    for sweep in range(ITERS):
        ahead, back = plan[2 * sweep], plan[2 * sweep + 1]
        outer, inner = rows_of(ahead), rows_of(back)
        skip_ahead = sum(len(groups) for groups in plan[0 : 2 * sweep : 2])
        skip_back = sum(len(groups) for groups in plan[1 : 2 * sweep : 2])
        final = sweep == ITERS - 1

        def ratio(tile):
            cols = columns_of(tile)
            b = jnp.dot(pad[outer, around(tile)], tl[...], preferred_element_type=f32) + BACKGROUND
            guess = pl.reciprocal(b, approx=True)
            guess = guess * (2.0 - b * guess)
            qb[outer, cols] = (mf[outer, cols] * guess).astype(bf16)

        def update(tile):
            cols = columns_of(tile)
            d = jnp.dot(pad_back[inner, around(tile)], tm[...], preferred_element_type=f32)
            e = (mf if sweep == 0 else ef)[inner, cols] * d
            if not final:
                ef[inner, cols] = e
                mb[inner, cols] = e.astype(bf16)
                return
            e = e.reshape(-1, ROWS, TILE).astype(bf16)
            if not later:
                lo, hi = tile * TILE, min((tile + 1) * TILE, out.shape[-1])
                if hi > lo:
                    out[:, :, lo:hi] = e[:, :, : hi - lo]
            else:
                cut = kept if tile == 0 else 0
                start = out.shape[-1] - columns + tile * TILE
                out[:, :, start + cut : start + TILE] = e[:, :, cut:]

        for step in range(tiles + 5):
            if step < tiles:
                axial(g, skip_ahead, ahead, mb, pad, step)
            if 0 <= step - 2 < tiles:
                ratio(step - 2)
            if 0 <= step - 3 < tiles:
                axial(gt, skip_back, back, qb, pad_back, step - 3)
            if 0 <= step - 5 < tiles:
                update(step - 5)

    if later:
        out[:, :, : earlier.shape[-1]] = earlier[...]


def restore(parts, matrices, earlier, plan, columns):
    later = earlier is not None
    planes = plan[-1][-1][0] + plan[-1][-1][1] - plan[-1][0][0]
    height = sum(part.shape[0] * part.shape[1] for part in parts[0])
    operands, specs, width = [], [], 0
    for number, part in enumerate(parts):
        kept = 2 * LANES if number < len(parts) - 1 else part[0].shape[-1]
        for array in part:
            block = array.shape[:2] + (kept,)
            index = (0, 0, array.shape[-1] // kept - 1)
            operands.append(array)
            specs.append(pl.BlockSpec(block, lambda i, index=index: index))
        width += kept

    def whole(array):
        return pl.BlockSpec(array.shape, lambda i: (0,) * len(array.shape))

    for array in (*matrices, *([earlier] if later else [])):
        operands.append(array)
        specs.append(whole(array))
    result = jax.ShapeDtypeStruct((planes, ROWS, columns if later else width - LANES), jnp.bfloat16)
    return pl.pallas_call(
        functools.partial(restore_kernel, plan, LANES if later else None),
        grid=(1,),
        in_specs=specs,
        out_specs=whole(result),
        out_shape=result,
        scratch_shapes=[
            pltpu.VMEM((height, width), jnp.float32),
            pltpu.VMEM((height, width), jnp.float32),
            pltpu.VMEM((height, width), jnp.bfloat16),
            pltpu.VMEM((height, width), jnp.bfloat16),
            pltpu.VMEM((height, width + 2 * LANES), jnp.bfloat16),
            pltpu.VMEM((height, width + 2 * LANES), jnp.bfloat16),
        ],
        compiler_params=pltpu.CompilerParams(vmem_limit_bytes=VMEM),
        cost_estimate=pl.CostEstimate(
            flops=7_000_000_000, bytes_accessed=8_000_000, transcendentals=0
        ),
        name="restore",
    )(*operands)


def local(
    raw_frames,
    frame_order,
    dark_frame,
    flat_gain,
    stripe_band,
    shear_offset,
    shear_fraction,
    band_index,
    psf_bank,
    lateral_psf,
):
    half = psf_bank.shape[1] // 2
    planes = shear_offset.shape[0]
    columns = raw_frames.shape[-1]
    halo = 2 * ITERS * half
    plan = stages(planes, half)
    count = lax.axis_size("cam")
    forward = [(i, i + 1) for i in range(count - 1)]
    backward = [(i + 1, i) for i in range(count - 1)]
    matrices = bands(psf_bank, lateral_psf, band_index, planes, halo)
    depth = halo // 2
    result = None
    parts = []
    for lo, hi in ((0, SPLIT), (SPLIT, columns)):
        piece = frame_side(
            raw_frames, frame_order, dark_frame, flat_gain, stripe_band, shear_offset,
            shear_fraction, lo, hi,
        )
        centre = lax.all_to_all(piece, "brick", split_axis=0, concat_axis=0, tiled=True)
        if result is not None:
            centre, result = lax.optimization_barrier((centre, result))
        low = lax.ppermute(centre[-depth:], "cam", forward)
        high = lax.ppermute(centre[:depth], "cam", backward)
        parts.append((low, centre, high))
        result = restore(parts, matrices, result, plan, columns)
    return result


def solution(mesh):
    placed = (
        P(("cam", "brick"), None, None),
        P(("cam", "brick"), None),
        P(),
        P(),
        P(),
        P("cam"),
        P("cam"),
        P(),
        P(),
        P(),
    )
    return jax.shard_map(
        local, mesh=mesh, in_specs=placed, out_specs=P("cam", "brick", None), check_vma=False
    )
```

```python
import functools

import jax
import jax.numpy as jnp
from jax import lax
from jax.experimental import pallas as pl
from jax.experimental.pallas import tpu as pltpu
from jax.sharding import PartitionSpec as P

SHEAR = 512
ITERS = 2
BACKGROUND = 1.0

LANES = 128
TILE = 256
ROWS = 8
BLOCK_ROWS = 64
LEAD = SHEAR // LANES + 1
SPLIT = 1280
VMEM = 60 * 1024 * 1024
GROUP = 20
SPAN = 32


def frame_kernel(
    first, count,
    order_ref, offset_ref, fraction_ref,
    raw_prev, raw_main, raw_next,
    dark_prev, dark_main, dark_next,
    gain_prev, gain_main, gain_next,
    band_ref, out_ref, scratch,
):
    step = pl.program_id(0)
    steps = pl.num_programs(0)
    rows = BLOCK_ROWS + 16
    brick = lax.axis_index("brick")
    f32 = jnp.float32
    bf16 = jnp.bfloat16
    base = first - LEAD

    @pl.when(step == 0)
    def _():
        if base < 0:
            scratch[:, :, : -base * LANES] = jnp.zeros((2, BLOCK_ROWS, -base * LANES), f32)

    has_prev = (step > 0).astype(f32)
    has_next = (step < steps - 1).astype(f32)
    frames = [jnp.where(order_ref[0, 0] == place, 0, 1) for place in range(2)]

    for tile in range(max(base, 0), first + count):
        cols = pl.ds(tile * LANES, LANES)
        band = band_ref[:, cols]
        levels = []
        for part, keep in ((0, slice(8, 16)), (1, slice(None)), (2, slice(0, 8))):
            dark = (dark_prev, dark_main, dark_next)[part][:, cols].astype(f32)[keep]
            gain = (gain_prev, gain_main, gain_next)[part][:, cols].astype(f32)[keep]
            if part != 1:
                gain = gain * (has_prev, None, has_next)[part]
            levels.append((dark, gain, keep))
        for place in range(2):
            f = jnp.concatenate(
                [
                    (raw[frames[place], :, cols].astype(f32)[keep] - dark) * gain
                    for raw, (dark, gain, keep) in zip((raw_prev, raw_main, raw_next), levels)
                ],
                axis=0,
            )
            after = pltpu.roll(f, rows - 1, 0)
            before = pltpu.roll(f, 1, 0)

            def three(k):
                return band[k : k + 1] * before + band[k + 1 : k + 2] * f + band[k + 2 : k + 3] * after

            out = (
                f
                + three(3)
                + pltpu.roll(three(6), rows - 3, 0)
                + pltpu.roll(three(0), 3, 0)
            )[8 : 8 + BLOCK_ROWS]
            scratch[place, :, pl.ds((tile - base) * LANES, LANES)] = out.astype(bf16).astype(f32)

    lane = lax.broadcasted_iota(jnp.int32, (BLOCK_ROWS, LANES), 1)
    bricks = BLOCK_ROWS // ROWS
    for place in range(2):
        amount = offset_ref[brick * 2 + place]
        weight = fraction_ref[brick * 2 + place]
        whole = amount // LANES
        part = amount % LANES
        near_mask = lane < part
        far_mask = lane < part + 1

        def turned(tile):
            start = (tile - base - whole) * LANES
            x = scratch[place, :, pl.ds(pl.multiple_of(start, LANES), LANES)]
            return (1.0 - weight) * pltpu.roll(x, part, 1), weight * pltpu.roll(x, (part + 1) % LANES, 1)

        last = turned(first - 1)
        for tile in range(first, first + count):
            now = turned(tile)
            mixed = jnp.where(near_mask, last[0], now[0]) + jnp.where(far_mask, last[1], now[1])
            last = now
            out_ref[:, place * ROWS : (place + 1) * ROWS, pl.ds((tile - first) * LANES, LANES)] = (
                mixed.reshape(bricks, ROWS, LANES).astype(bf16)
            )


def frame_side(raw, order, dark, gain, band, offset, fraction, lo, hi):
    _, frame_rows, columns = raw.shape
    steps = frame_rows // BLOCK_ROWS
    bricks = frame_rows // ROWS
    per = BLOCK_ROWS // 16
    last = frame_rows // 16 - 1
    smem = pl.BlockSpec(memory_space=pltpu.SMEM)
    first, count = lo // LANES, (hi - lo) // LANES

    def three(lead):
        zeros = (0,) * len(lead)
        return [
            pl.BlockSpec(lead + (16, columns), lambda i: zeros + (jnp.maximum(per * i - 1, 0), 0)),
            pl.BlockSpec(lead + (BLOCK_ROWS, columns), lambda i: zeros + (i, 0)),
            pl.BlockSpec(lead + (16, columns), lambda i: zeros + (jnp.minimum(per * i + per, last), 0)),
        ]

    return pl.pallas_call(
        functools.partial(frame_kernel, first, count),
        grid=(steps,),
        in_specs=[smem, smem, smem]
        + three((2,)) + three(()) + three(())
        + [pl.BlockSpec(band.shape, lambda i: (0, 0))],
        out_specs=pl.BlockSpec((BLOCK_ROWS // ROWS, 2 * ROWS, hi - lo), lambda i: (i, 0, 0)),
        out_shape=jax.ShapeDtypeStruct((bricks, 2 * ROWS, hi - lo), jnp.bfloat16),
        scratch_shapes=[pltpu.VMEM((2, BLOCK_ROWS, (LEAD + count) * LANES), jnp.float32)],
        compiler_params=pltpu.CompilerParams(vmem_limit_bytes=VMEM),
        cost_estimate=pl.CostEstimate(
            flops=8_000_000_000, bytes_accessed=6_500_000, transcendentals=0
        ),
        name="frame_side",
    )(order, offset, fraction, raw, raw, raw, dark, dark, dark, gain, gain, gain, band)


def stages(planes, half):
    total = planes + 4 * ITERS * half
    plan = []
    for reach in range(1, 2 * ITERS + 1):
        lo, hi = reach * half, total - reach * half
        plan.append([(at, min(GROUP, hi - at)) for at in range(lo, hi, GROUP)])
    return plan


def bands_kernel(taps, lat_taps, plan, psf_ref, lateral_ref, index_ref, g_ref, gt_ref, tl_ref, tm_ref):
    f32 = jnp.float32
    bf16 = jnp.bfloat16
    half = taps // 2
    width = SPAN * ROWS
    index = index_ref[...]
    raw = []
    for tap in range(taps):
        value = jnp.zeros(index.shape, f32)
        for kernel in range(psf_ref.shape[0]):
            value = jnp.where(index == kernel, psf_ref[kernel, tap], value)
        raw.append(value)
    total = functools.reduce(lambda a, b: a + b, raw)
    total = jnp.where(total > 0.0, total, 1.0)
    unit = [value / total for value in raw]
    row = lax.broadcasted_iota(jnp.int32, (width, width), 0)
    col = lax.broadcasted_iota(jnp.int32, (width, width), 1)

    def banded(start, gap, order):
        m = jnp.zeros((width, width), f32)
        for tap in range(taps):
            values = unit[tap][:, start * ROWS : start * ROWS + width]
            m = jnp.where(gap == ROWS * order(tap), values, m)
        return m

    slot = [0, 0]
    for number, groups in enumerate(plan):
        for at, _ in groups:
            if number % 2 == 0:
                m = banded(at, row - col, lambda tap: tap).T
                g_ref[slot[0]] = m[: GROUP * ROWS].astype(bf16)
            else:
                m = banded(at - half, col - row, lambda tap: 2 * half - tap)
                gt_ref[slot[1]] = m[: GROUP * ROWS].astype(bf16)
            slot[number % 2] += 1

    lateral_total = lateral_ref[0]
    for tap in range(1, lat_taps):
        lateral_total = lateral_total + lateral_ref[tap]
    k = lax.broadcasted_iota(jnp.int32, tl_ref.shape, 0)
    j = lax.broadcasted_iota(jnp.int32, tl_ref.shape, 1)
    place = k - LANES - j + lat_taps // 2
    forward = jnp.zeros(tl_ref.shape, f32)
    backward = jnp.zeros(tl_ref.shape, f32)
    for tap in range(lat_taps):
        forward = jnp.where(place == tap, lateral_ref[tap], forward)
        backward = jnp.where(place == lat_taps - 1 - tap, lateral_ref[tap], backward)
    scale = jnp.full((1, TILE), lateral_total, f32)
    tl_ref[...] = (forward / scale).astype(bf16)
    tm_ref[...] = (backward / scale).astype(bf16)


def bands(psf_bank, lateral_psf, band_index, planes, halo):
    half = psf_bank.shape[1] // 2
    plan = stages(planes, half)
    spread = jnp.pad(band_index, (halo, halo + SPAN), constant_values=-1)
    first = lax.axis_index("cam") * planes
    length = planes + 2 * halo + SPAN
    mine = lax.dynamic_slice_in_dim(spread, first, length, 0)
    index = jnp.broadcast_to(mine[:, None], (length, ROWS)).reshape(1, length * ROWS)
    smem = pl.BlockSpec(memory_space=pltpu.SMEM)
    vmem = pl.BlockSpec(memory_space=pltpu.VMEM)
    counts = [sum(len(groups) for groups in plan[kind::2]) for kind in range(2)]
    strip = jax.ShapeDtypeStruct((TILE + 2 * LANES, TILE), jnp.bfloat16)
    return pl.pallas_call(
        functools.partial(bands_kernel, psf_bank.shape[1], lateral_psf.shape[0], plan),
        in_specs=[smem, smem, vmem],
        out_specs=[vmem] * 4,
        out_shape=[
            jax.ShapeDtypeStruct((n, GROUP * ROWS, SPAN * ROWS), jnp.bfloat16) for n in counts
        ]
        + [strip, strip],
        compiler_params=pltpu.CompilerParams(vmem_limit_bytes=VMEM),
        cost_estimate=pl.CostEstimate(
            flops=2_000_000_000, bytes_accessed=2_000_000, transcendentals=0
        ),
        name="bands",
    )(psf_bank, lateral_psf, index)


def restore_kernel(plan, kept, *refs):
    later = kept is not None
    sources = [refs[3 * i : 3 * i + 3] for i in range(2 if later else 1)]
    refs = refs[3 * len(sources) :]
    g, gt, tl, tm = refs[:4]
    earlier = refs[4] if later else None
    out, mf, ef, mb, qb, pad, pad_back = refs[4 + later :]
    f32 = jnp.float32
    bf16 = jnp.bfloat16
    size, columns = mf.shape
    tiles = columns // TILE

    for buffer in (pad, pad_back):
        buffer[:, :LANES] = jnp.zeros((size, LANES), bf16)
        buffer[:, LANES + columns :] = jnp.zeros((size, LANES), bf16)

    at_column = 0
    for source in sources:
        width = source[1].shape[-1]
        at_row = 0
        for ref in source:
            height = ref.shape[0] * ref.shape[1]
            for col in range(0, width, TILE):
                whole = ref[:, :, col : col + TILE].reshape(height, TILE)
                there = slice(at_column + col, at_column + col + TILE)
                mb[at_row : at_row + height, there] = whole
                mf[at_row : at_row + height, there] = whole.astype(f32)
            at_row += height
        at_column += width

    def columns_of(tile):
        return slice(tile * TILE, (tile + 1) * TILE)

    def within(tile):
        return slice(LANES + tile * TILE, LANES + (tile + 1) * TILE)

    def around(tile):
        return slice(tile * TILE, (tile + 1) * TILE + 2 * LANES)

    half = plan[0][0][0]

    def rows_of(groups):
        return slice(groups[0][0] * ROWS, (groups[-1][0] + groups[-1][1]) * ROWS)

    def axial(matrices, skip, groups, source, target, tile):
        for number, (first, count) in enumerate(groups):
            low = (first - half) * ROWS
            high = (first + count + half) * ROWS
            r = jnp.dot(
                matrices[skip + number, : count * ROWS, : high - low],
                source[low:high, columns_of(tile)],
                preferred_element_type=f32,
            )
            target[first * ROWS : (first + count) * ROWS, within(tile)] = r.astype(bf16)

    for sweep in range(ITERS):
        ahead, back = plan[2 * sweep], plan[2 * sweep + 1]
        outer, inner = rows_of(ahead), rows_of(back)
        skip_ahead = sum(len(groups) for groups in plan[0 : 2 * sweep : 2])
        skip_back = sum(len(groups) for groups in plan[1 : 2 * sweep : 2])
        final = sweep == ITERS - 1

        def ratio(tile):
            cols = columns_of(tile)
            b = jnp.dot(pad[outer, around(tile)], tl[...], preferred_element_type=f32) + BACKGROUND
            guess = pl.reciprocal(b, approx=True)
            guess = guess * (2.0 - b * guess)
            qb[outer, cols] = (mf[outer, cols] * guess).astype(bf16)

        def update(tile):
            cols = columns_of(tile)
            d = jnp.dot(pad_back[inner, around(tile)], tm[...], preferred_element_type=f32)
            e = (mf if sweep == 0 else ef)[inner, cols] * d
            if not final:
                ef[inner, cols] = e
                mb[inner, cols] = e.astype(bf16)
                return
            e = e.reshape(-1, ROWS, TILE).astype(bf16)
            if not later:
                lo, hi = tile * TILE, min((tile + 1) * TILE, out.shape[-1])
                if hi > lo:
                    out[:, :, lo:hi] = e[:, :, : hi - lo]
            else:
                cut = kept if tile == 0 else 0
                start = out.shape[-1] - columns + tile * TILE
                out[:, :, start + cut : start + TILE] = e[:, :, cut:]

        for step in range(tiles + 5):
            if step < tiles:
                axial(g, skip_ahead, ahead, mb, pad, step)
            if 0 <= step - 2 < tiles:
                ratio(step - 2)
            if 0 <= step - 3 < tiles:
                axial(gt, skip_back, back, qb, pad_back, step - 3)
            if 0 <= step - 5 < tiles:
                update(step - 5)

    if later:
        out[:, :, : earlier.shape[-1]] = earlier[...]


def restore(parts, matrices, earlier, plan, columns):
    later = earlier is not None
    planes = plan[-1][-1][0] + plan[-1][-1][1] - plan[-1][0][0]
    height = sum(part.shape[0] * part.shape[1] for part in parts[0])
    operands, specs, width = [], [], 0
    for number, part in enumerate(parts):
        kept = 2 * LANES if number < len(parts) - 1 else part[0].shape[-1]
        for array in part:
            block = array.shape[:2] + (kept,)
            index = (0, 0, array.shape[-1] // kept - 1)
            operands.append(array)
            specs.append(pl.BlockSpec(block, lambda i, index=index: index))
        width += kept

    def whole(array):
        return pl.BlockSpec(array.shape, lambda i: (0,) * len(array.shape))

    for array in (*matrices, *([earlier] if later else [])):
        operands.append(array)
        specs.append(whole(array))
    result = jax.ShapeDtypeStruct((planes, ROWS, columns if later else width - LANES), jnp.bfloat16)
    return pl.pallas_call(
        functools.partial(restore_kernel, plan, LANES if later else None),
        grid=(1,),
        in_specs=specs,
        out_specs=whole(result),
        out_shape=result,
        scratch_shapes=[
            pltpu.VMEM((height, width), jnp.float32),
            pltpu.VMEM((height, width), jnp.float32),
            pltpu.VMEM((height, width), jnp.bfloat16),
            pltpu.VMEM((height, width), jnp.bfloat16),
            pltpu.VMEM((height, width + 2 * LANES), jnp.bfloat16),
            pltpu.VMEM((height, width + 2 * LANES), jnp.bfloat16),
        ],
        compiler_params=pltpu.CompilerParams(vmem_limit_bytes=VMEM),
        cost_estimate=pl.CostEstimate(
            flops=7_000_000_000, bytes_accessed=8_000_000, transcendentals=0
        ),
        name="restore",
    )(*operands)


def local(
    raw_frames,
    frame_order,
    dark_frame,
    flat_gain,
    stripe_band,
    shear_offset,
    shear_fraction,
    band_index,
    psf_bank,
    lateral_psf,
):
    half = psf_bank.shape[1] // 2
    planes = shear_offset.shape[0]
    columns = raw_frames.shape[-1]
    halo = 2 * ITERS * half
    plan = stages(planes, half)
    count = lax.axis_size("cam")
    forward = [(i, i + 1) for i in range(count - 1)]
    backward = [(i + 1, i) for i in range(count - 1)]
    matrices = bands(psf_bank, lateral_psf, band_index, planes, halo)
    depth = halo // 2
    result = None
    parts = []
    for lo, hi in ((0, SPLIT), (SPLIT, columns)):
        piece = frame_side(
            raw_frames, frame_order, dark_frame, flat_gain, stripe_band, shear_offset,
            shear_fraction, lo, hi,
        )
        centre = lax.all_to_all(piece, "brick", split_axis=0, concat_axis=0, tiled=True)
        low = lax.ppermute(centre[-depth:], "cam", forward)
        high = lax.ppermute(centre[:depth], "cam", backward)
        parts.append((low, centre, high))
        result = restore(parts, matrices, result, plan, columns)
    return result


def solution(mesh):
    placed = (
        P(("cam", "brick"), None, None),
        P(("cam", "brick"), None),
        P(),
        P(),
        P(),
        P("cam"),
        P("cam"),
        P(),
        P(),
        P(),
    )
    return jax.shard_map(
        local, mesh=mesh, in_specs=placed, out_specs=P("cam", "brick", None), check_vma=False
    )
```

```python
import functools

import jax
import jax.numpy as jnp
from jax import lax
from jax.experimental import pallas as pl
from jax.experimental.pallas import tpu as pltpu
from jax.sharding import PartitionSpec as P

SHEAR = 512
ITERS = 2
BACKGROUND = 1.0

LANES = 128
TILE = 256
ROWS = 8
BLOCK_ROWS = 64
LEAD = SHEAR // LANES + 1
SPLIT = 1280
VMEM = 60 * 1024 * 1024
BANDS_VMEM = 20 * 1024 * 1024
RESTORE_VMEM = 42 * 1024 * 1024
GROUP = 20
SPAN = 32


def frame_kernel(
    first, count,
    order_ref, offset_ref, fraction_ref,
    raw_prev, raw_main, raw_next,
    dark_prev, dark_main, dark_next,
    gain_prev, gain_main, gain_next,
    band_ref, out_ref, scratch,
):
    step = pl.program_id(0)
    steps = pl.num_programs(0)
    rows = BLOCK_ROWS + 16
    brick = lax.axis_index("brick")
    f32 = jnp.float32
    bf16 = jnp.bfloat16
    base = first - LEAD

    @pl.when(step == 0)
    def _():
        if base < 0:
            scratch[:, :, : -base * LANES] = jnp.zeros((2, BLOCK_ROWS, -base * LANES), f32)

    has_prev = (step > 0).astype(f32)
    has_next = (step < steps - 1).astype(f32)
    frames = [jnp.where(order_ref[0, 0] == place, 0, 1) for place in range(2)]

    for tile in range(max(base, 0), first + count):
        cols = pl.ds(tile * LANES, LANES)
        band = band_ref[:, cols]
        levels = []
        for part, keep in ((0, slice(8, 16)), (1, slice(None)), (2, slice(0, 8))):
            dark = (dark_prev, dark_main, dark_next)[part][:, cols].astype(f32)[keep]
            gain = (gain_prev, gain_main, gain_next)[part][:, cols].astype(f32)[keep]
            if part != 1:
                gain = gain * (has_prev, None, has_next)[part]
            levels.append((dark, gain, keep))
        for place in range(2):
            f = jnp.concatenate(
                [
                    (raw[frames[place], :, cols].astype(f32)[keep] - dark) * gain
                    for raw, (dark, gain, keep) in zip((raw_prev, raw_main, raw_next), levels)
                ],
                axis=0,
            )
            after = pltpu.roll(f, rows - 1, 0)
            before = pltpu.roll(f, 1, 0)

            def three(k):
                return band[k : k + 1] * before + band[k + 1 : k + 2] * f + band[k + 2 : k + 3] * after

            out = (
                f
                + three(3)
                + pltpu.roll(three(6), rows - 3, 0)
                + pltpu.roll(three(0), 3, 0)
            )[8 : 8 + BLOCK_ROWS]
            scratch[place, :, pl.ds((tile - base) * LANES, LANES)] = out.astype(bf16).astype(f32)

    lane = lax.broadcasted_iota(jnp.int32, (BLOCK_ROWS, LANES), 1)
    bricks = BLOCK_ROWS // ROWS
    for place in range(2):
        amount = offset_ref[brick * 2 + place]
        weight = fraction_ref[brick * 2 + place]
        whole = amount // LANES
        part = amount % LANES
        near_mask = lane < part
        far_mask = lane < part + 1

        def turned(tile):
            start = (tile - base - whole) * LANES
            x = scratch[place, :, pl.ds(pl.multiple_of(start, LANES), LANES)]
            return (1.0 - weight) * pltpu.roll(x, part, 1), weight * pltpu.roll(x, (part + 1) % LANES, 1)

        last = turned(first - 1)
        for tile in range(first, first + count):
            now = turned(tile)
            mixed = jnp.where(near_mask, last[0], now[0]) + jnp.where(far_mask, last[1], now[1])
            last = now
            out_ref[:, place * ROWS : (place + 1) * ROWS, pl.ds((tile - first) * LANES, LANES)] = (
                mixed.reshape(bricks, ROWS, LANES).astype(bf16)
            )


def frame_side(raw, order, dark, gain, band, offset, fraction, lo, hi):
    _, frame_rows, columns = raw.shape
    steps = frame_rows // BLOCK_ROWS
    bricks = frame_rows // ROWS
    per = BLOCK_ROWS // 16
    last = frame_rows // 16 - 1
    smem = pl.BlockSpec(memory_space=pltpu.SMEM)
    first, count = lo // LANES, (hi - lo) // LANES

    def three(lead):
        zeros = (0,) * len(lead)
        return [
            pl.BlockSpec(lead + (16, columns), lambda i: zeros + (jnp.maximum(per * i - 1, 0), 0)),
            pl.BlockSpec(lead + (BLOCK_ROWS, columns), lambda i: zeros + (i, 0)),
            pl.BlockSpec(lead + (16, columns), lambda i: zeros + (jnp.minimum(per * i + per, last), 0)),
        ]

    return pl.pallas_call(
        functools.partial(frame_kernel, first, count),
        grid=(steps,),
        in_specs=[smem, smem, smem]
        + three((2,)) + three(()) + three(())
        + [pl.BlockSpec(band.shape, lambda i: (0, 0))],
        out_specs=pl.BlockSpec((BLOCK_ROWS // ROWS, 2 * ROWS, hi - lo), lambda i: (i, 0, 0)),
        out_shape=jax.ShapeDtypeStruct((bricks, 2 * ROWS, hi - lo), jnp.bfloat16),
        scratch_shapes=[pltpu.VMEM((2, BLOCK_ROWS, (LEAD + count) * LANES), jnp.float32)],
        compiler_params=pltpu.CompilerParams(vmem_limit_bytes=VMEM),
        cost_estimate=pl.CostEstimate(
            flops=8_000_000_000, bytes_accessed=6_500_000, transcendentals=0
        ),
        name="frame_side",
    )(order, offset, fraction, raw, raw, raw, dark, dark, dark, gain, gain, gain, band)


def stages(planes, half):
    halo = 2 * ITERS * half
    total = planes + 2 * halo

    def cut(lo, hi, most):
        parts = -(-(hi - lo) // most)
        size = -(-(hi - lo) // (2 * parts)) * 2
        return [(at, min(size, hi - at)) for at in range(lo, hi, size)]

    inner, outer = [], []
    for stage in range(1, 2 * ITERS + 1):
        reach = stage * half
        lo, hi = halo + reach, total - halo - reach
        inner.append([cut(lo, hi, GROUP)])
        outer.append([cut(reach, lo, GROUP), cut(hi, total - reach, GROUP)])
    return inner, outer


def flat(stage):
    return [group for groups in stage for group in groups]


def bands_kernel(taps, lat_taps, plans, psf_ref, lateral_ref, index_ref, *outs):
    matrices, (tl_ref, tm_ref) = outs[:-2], outs[-2:]
    f32 = jnp.float32
    bf16 = jnp.bfloat16
    half = taps // 2
    width = SPAN * ROWS
    index = index_ref[...]
    raw = []
    for tap in range(taps):
        value = jnp.zeros(index.shape, f32)
        for kernel in range(psf_ref.shape[0]):
            value = jnp.where(index == kernel, psf_ref[kernel, tap], value)
        raw.append(value)
    total = functools.reduce(lambda a, b: a + b, raw)
    total = jnp.where(total > 0.0, total, 1.0)
    unit = [value / total for value in raw]
    row = lax.broadcasted_iota(jnp.int32, (width, width), 0)
    col = lax.broadcasted_iota(jnp.int32, (width, width), 1)

    def banded(start, gap, order):
        m = jnp.zeros((width, width), f32)
        for tap in range(taps):
            values = unit[tap][:, start * ROWS : start * ROWS + width]
            m = jnp.where(gap == ROWS * order(tap), values, m)
        return m

    for which, plan in enumerate(plans):
        slot = [0, 0]
        for number, stage in enumerate(plan):
            kind = number % 2
            target = matrices[2 * which + kind]
            for at, _ in flat(stage):
                if kind == 0:
                    m = banded(at, row - col, lambda tap: tap).T
                else:
                    m = banded(at - half, col - row, lambda tap: 2 * half - tap)
                target[slot[kind]] = m[: GROUP * ROWS].astype(bf16)
                slot[kind] += 1

    lateral_total = lateral_ref[0]
    for tap in range(1, lat_taps):
        lateral_total = lateral_total + lateral_ref[tap]
    k = lax.broadcasted_iota(jnp.int32, tl_ref.shape, 0)
    j = lax.broadcasted_iota(jnp.int32, tl_ref.shape, 1)
    place = k - LANES - j + lat_taps // 2
    forward = jnp.zeros(tl_ref.shape, f32)
    backward = jnp.zeros(tl_ref.shape, f32)
    for tap in range(lat_taps):
        forward = jnp.where(place == tap, lateral_ref[tap], forward)
        backward = jnp.where(place == lat_taps - 1 - tap, lateral_ref[tap], backward)
    scale = jnp.full((1, TILE), lateral_total, f32)
    tl_ref[...] = (forward / scale).astype(bf16)
    tm_ref[...] = (backward / scale).astype(bf16)


def bands(psf_bank, lateral_psf, band_index, planes, halo):
    plans = stages(planes, psf_bank.shape[1] // 2)
    spread = jnp.pad(band_index, (halo, halo + SPAN), constant_values=-1)
    first = lax.axis_index("cam") * planes
    length = planes + 2 * halo + SPAN
    mine = lax.dynamic_slice_in_dim(spread, first, length, 0)
    index = jnp.broadcast_to(mine[:, None], (length, ROWS)).reshape(1, length * ROWS)
    smem = pl.BlockSpec(memory_space=pltpu.SMEM)
    vmem = pl.BlockSpec(memory_space=pltpu.VMEM)
    counts = [
        sum(len(flat(stage)) for stage in plan[kind::2]) for plan in plans for kind in range(2)
    ]
    strip = jax.ShapeDtypeStruct((TILE + 2 * LANES, TILE), jnp.bfloat16)
    return pl.pallas_call(
        functools.partial(bands_kernel, psf_bank.shape[1], lateral_psf.shape[0], plans),
        in_specs=[smem, smem, vmem],
        out_specs=[vmem] * 6,
        out_shape=[
            jax.ShapeDtypeStruct((n, GROUP * ROWS, SPAN * ROWS), jnp.bfloat16) for n in counts
        ]
        + [strip, strip],
        compiler_params=pltpu.CompilerParams(vmem_limit_bytes=BANDS_VMEM),
        cost_estimate=pl.CostEstimate(
            flops=2_000_000_000, bytes_accessed=2_000_000, transcendentals=0
        ),
        name="bands",
    )(psf_bank, lateral_psf, index)


def restore_kernel(plan, inside, counts, merge, cut, *refs):
    parts = []
    for count in counts:
        parts.append(refs[:count])
        refs = refs[count:]
    g, gt, tl, tm = refs[:4]
    refs = refs[4:]
    f32 = jnp.float32
    bf16 = jnp.bfloat16
    half = plan[0][0][0][0] if not inside else plan[1][0][0][0] - plan[0][0][0][0]
    halo = 2 * ITERS * half
    if inside:
        out, q_out, e_out, mf, ef, mb, qb, pad, pad_back = refs
    else:
        q_in, e_in, middle = refs[:3]
        earlier = refs[3] if merge else None
        out, mf, ef, mb, qb, pad, pad_back = refs[3 + merge :]
    size, columns = mf.shape
    total = size // ROWS
    tiles = columns // TILE

    for buffer in (pad, pad_back):
        buffer[:, :LANES] = jnp.zeros((size, LANES), bf16)
        buffer[:, LANES + columns :] = jnp.zeros((size, LANES), bf16)

    at_column = 0
    for part in parts:
        width = part[0].shape[-1]
        at_row = halo * ROWS if inside else 0
        for ref in part:
            height = ref.shape[0] * ref.shape[1]
            for col in range(0, width, TILE):
                whole = ref[:, :, col : col + TILE].reshape(height, TILE)
                there = slice(at_column + col, at_column + col + TILE)
                mb[at_row : at_row + height, there] = whole
                mf[at_row : at_row + height, there] = whole.astype(f32)
            at_row += height
        at_column += width

    q_rows = slice((halo + half) * ROWS, (total - halo - half) * ROWS)
    e_width = half * (2 * ITERS - 2) * ROWS
    e_low = (halo + 2 * half) * ROWS
    e_high = (total - halo - 2 * half) * ROWS - e_width
    if not inside:
        qb[q_rows, :] = q_in[...]
        for number, start in enumerate((e_low, e_high)):
            e = e_in[number * e_width : (number + 1) * e_width, :]
            ef[start : start + e_width, :] = e
            mb[start : start + e_width, :] = e.astype(bf16)
        for lo in range(0, out.shape[-1] if not merge else 0, LANES):
            out[half * 4 : out.shape[0] - half * 4, :, lo : lo + LANES] = middle[:, :, lo : lo + LANES]

    def columns_of(tile):
        return slice(tile * TILE, (tile + 1) * TILE)

    def within(tile):
        return slice(LANES + tile * TILE, LANES + (tile + 1) * TILE)

    def around(tile):
        return slice(tile * TILE, (tile + 1) * TILE + 2 * LANES)

    def rows_of(groups):
        return slice(groups[0][0] * ROWS, (groups[-1][0] + groups[-1][1]) * ROWS)

    def axial(matrices, skip, stage, source, target, tile):
        for number, (first, count) in enumerate(flat(stage)):
            low = (first - half) * ROWS
            high = (first + count + half) * ROWS
            r = jnp.dot(
                matrices[skip + number, : count * ROWS, : high - low],
                source[low:high, columns_of(tile)],
                preferred_element_type=f32,
            )
            target[first * ROWS : (first + count) * ROWS, within(tile)] = r.astype(bf16)

    for sweep in range(ITERS):
        ahead, back = plan[2 * sweep], plan[2 * sweep + 1]
        skip_ahead = sum(len(flat(stage)) for stage in plan[0 : 2 * sweep : 2])
        skip_back = sum(len(flat(stage)) for stage in plan[1 : 2 * sweep : 2])
        final = sweep == ITERS - 1

        def ratio(tile):
            cols = columns_of(tile)
            for groups in ahead:
                rows = rows_of(groups)
                b = jnp.dot(pad[rows, around(tile)], tl[...], preferred_element_type=f32) + BACKGROUND
                guess = pl.reciprocal(b, approx=True)
                guess = guess * (2.0 - b * guess)
                qb[rows, cols] = (mf[rows, cols] * guess).astype(bf16)

        def update(tile):
            cols = columns_of(tile)
            for groups in back:
                rows = rows_of(groups)
                d = jnp.dot(pad_back[rows, around(tile)], tm[...], preferred_element_type=f32)
                e = (mf if sweep == 0 else ef)[rows, cols] * d
                if not final:
                    ef[rows, cols] = e
                    mb[rows, cols] = e.astype(bf16)
                    continue
                e = e.reshape(-1, ROWS, TILE).astype(bf16)
                first = groups[0][0] - plan[-1][0][0][0]
                start = (out.shape[-1] - columns if cut else 0) + tile * TILE
                drop = cut if tile == 0 else 0
                keep = min(TILE, out.shape[-1] - start)
                if keep > drop:
                    out[first : first + e.shape[0], :, start + drop : start + keep] = e[:, :, drop:keep]

        for step in range(tiles + 5):
            if step < tiles:
                axial(g, skip_ahead, ahead, mb, pad, step)
            if 0 <= step - 2 < tiles:
                ratio(step - 2)
            if 0 <= step - 3 < tiles:
                axial(gt, skip_back, back, qb, pad_back, step - 3)
            if 0 <= step - 5 < tiles:
                update(step - 5)

    if inside:
        q_out[...] = qb[q_rows, :]
        e_out[:e_width, :] = ef[e_low : e_low + e_width, :]
        e_out[e_width:, :] = ef[e_high : e_high + e_width, :]
    elif merge:
        kept = earlier.shape[-1]
        out[:, :, :kept] = earlier[...]
        out[half * 4 : out.shape[0] - half * 4, :, kept:] = middle[:, :, columns - (out.shape[-1] - kept) :]


def restore(parts, matrices, state, earlier, plan, inside, planes, half, columns):
    merge = earlier is not None
    operands, specs, width = [], [], 0
    for number, part in enumerate(parts):
        kept = 2 * LANES if number < len(parts) - 1 else part[0].shape[-1]
        for array in part:
            block = array.shape[:2] + (kept,)
            index = (0, 0, array.shape[-1] // kept - 1)
            operands.append(array)
            specs.append(pl.BlockSpec(block, lambda i, index=index: index))
        width += kept

    def whole(array):
        return pl.BlockSpec(array.shape, lambda i: (0,) * len(array.shape))

    for array in (*matrices, *state, *([earlier] if merge else [])):
        operands.append(array)
        specs.append(whole(array))
    halo = 2 * ITERS * half
    height = (planes + 2 * halo) * ROWS
    bf16 = jnp.bfloat16
    if inside:
        cut = 0
        results = [
            jax.ShapeDtypeStruct((planes - 2 * halo, ROWS, width), bf16),
            jax.ShapeDtypeStruct(((planes - 2 * half) * ROWS, width), bf16),
            jax.ShapeDtypeStruct((2 * half * (2 * ITERS - 2) * ROWS, width), jnp.float32),
        ]
    else:
        cut = LANES if merge else 0
        results = [jax.ShapeDtypeStruct((planes, ROWS, columns if merge else width - LANES), bf16)]
    return pl.pallas_call(
        functools.partial(restore_kernel, plan, inside, [len(part) for part in parts], merge, cut),
        grid=(1,),
        in_specs=specs,
        out_specs=[whole(result) for result in results],
        out_shape=results,
        scratch_shapes=[
            pltpu.VMEM((height, width), jnp.float32),
            pltpu.VMEM((height, width), jnp.float32),
            pltpu.VMEM((height, width), bf16),
            pltpu.VMEM((height, width), bf16),
            pltpu.VMEM((height, width + 2 * LANES), bf16),
            pltpu.VMEM((height, width + 2 * LANES), bf16),
        ],
        compiler_params=pltpu.CompilerParams(vmem_limit_bytes=RESTORE_VMEM),
        cost_estimate=pl.CostEstimate(
            flops=5_000_000_000, bytes_accessed=8_000_000, transcendentals=0
        ),
        name="inside" if inside else "ends",
    )(*operands)


def local(
    raw_frames,
    frame_order,
    dark_frame,
    flat_gain,
    stripe_band,
    shear_offset,
    shear_fraction,
    band_index,
    psf_bank,
    lateral_psf,
):
    half = psf_bank.shape[1] // 2
    planes = shear_offset.shape[0]
    columns = raw_frames.shape[-1]
    halo = 2 * ITERS * half
    inner, outer = stages(planes, half)
    count = lax.axis_size("cam")
    forward = [(i, i + 1) for i in range(count - 1)]
    backward = [(i + 1, i) for i in range(count - 1)]
    *axial, forward_lateral, backward_lateral = bands(psf_bank, lateral_psf, band_index, planes, halo)
    inner_matrices = (*axial[:2], forward_lateral, backward_lateral)
    outer_matrices = (*axial[2:], forward_lateral, backward_lateral)
    depth = halo // 2
    result = None
    parts = []
    centres = []
    for lo, hi in ((0, SPLIT), (SPLIT, columns)):
        piece = frame_side(
            raw_frames, frame_order, dark_frame, flat_gain, stripe_band, shear_offset,
            shear_fraction, lo, hi,
        )
        centre = lax.all_to_all(piece, "brick", split_axis=0, concat_axis=0, tiled=True)
        low = lax.ppermute(centre[-depth:], "cam", forward)
        high = lax.ppermute(centre[:depth], "cam", backward)
        centres.append((centre,))
        parts.append((low, centre, high))
        middle, quotients, estimates = restore(
            centres, inner_matrices, (), None, inner, True, planes, half, columns
        )
        (result,) = restore(
            parts, outer_matrices, (quotients, estimates, middle), result, outer, False, planes, half,
            columns,
        )
    return result


def solution(mesh):
    placed = (
        P(("cam", "brick"), None, None),
        P(("cam", "brick"), None),
        P(),
        P(),
        P(),
        P("cam"),
        P("cam"),
        P(),
        P(),
        P(),
    )
    return jax.shard_map(
        local, mesh=mesh, in_specs=placed, out_specs=P("cam", "brick", None), check_vma=False
    )
```

```python
import functools

import jax
import jax.numpy as jnp
from jax import lax
from jax.experimental import pallas as pl
from jax.experimental.pallas import tpu as pltpu
from jax.sharding import PartitionSpec as P

SHEAR = 512
ITERS = 2
BACKGROUND = 1.0

LANES = 128
TILE = 256
ROWS = 8
BLOCK_ROWS = 64
LEAD = SHEAR // LANES + 1
SPLIT = 1280
VMEM = 60 * 1024 * 1024
BANDS_VMEM = 20 * 1024 * 1024
RESTORE_VMEM = 42 * 1024 * 1024
GROUP = 20
SPAN = 32


def frame_kernel(
    first, count,
    order_ref, offset_ref, fraction_ref,
    raw_prev, raw_main, raw_next,
    dark_prev, dark_main, dark_next,
    gain_prev, gain_main, gain_next,
    band_ref, out_ref, scratch,
):
    step = pl.program_id(0)
    steps = pl.num_programs(0)
    rows = BLOCK_ROWS + 16
    brick = lax.axis_index("brick")
    f32 = jnp.float32
    bf16 = jnp.bfloat16
    base = first - LEAD

    @pl.when(step == 0)
    def _():
        if base < 0:
            scratch[:, :, : -base * LANES] = jnp.zeros((2, BLOCK_ROWS, -base * LANES), f32)

    has_prev = (step > 0).astype(f32)
    has_next = (step < steps - 1).astype(f32)
    frames = [jnp.where(order_ref[0, 0] == place, 0, 1) for place in range(2)]

    for tile in range(max(base, 0), first + count):
        cols = pl.ds(tile * LANES, LANES)
        band = band_ref[:, cols]
        levels = []
        for part, keep in ((0, slice(8, 16)), (1, slice(None)), (2, slice(0, 8))):
            dark = (dark_prev, dark_main, dark_next)[part][:, cols].astype(f32)[keep]
            gain = (gain_prev, gain_main, gain_next)[part][:, cols].astype(f32)[keep]
            if part != 1:
                gain = gain * (has_prev, None, has_next)[part]
            levels.append((dark, gain, keep))
        for place in range(2):
            f = jnp.concatenate(
                [
                    (raw[frames[place], :, cols].astype(f32)[keep] - dark) * gain
                    for raw, (dark, gain, keep) in zip((raw_prev, raw_main, raw_next), levels)
                ],
                axis=0,
            )
            after = pltpu.roll(f, rows - 1, 0)
            before = pltpu.roll(f, 1, 0)

            def three(k):
                return band[k : k + 1] * before + band[k + 1 : k + 2] * f + band[k + 2 : k + 3] * after

            out = (
                f
                + three(3)
                + pltpu.roll(three(6), rows - 3, 0)
                + pltpu.roll(three(0), 3, 0)
            )[8 : 8 + BLOCK_ROWS]
            scratch[place, :, pl.ds((tile - base) * LANES, LANES)] = out.astype(bf16).astype(f32)

    lane = lax.broadcasted_iota(jnp.int32, (BLOCK_ROWS, LANES), 1)
    bricks = BLOCK_ROWS // ROWS
    for place in range(2):
        amount = offset_ref[brick * 2 + place]
        weight = fraction_ref[brick * 2 + place]
        whole = amount // LANES
        part = amount % LANES
        near_mask = lane < part
        far_mask = lane < part + 1

        def turned(tile):
            start = (tile - base - whole) * LANES
            x = scratch[place, :, pl.ds(pl.multiple_of(start, LANES), LANES)]
            return (1.0 - weight) * pltpu.roll(x, part, 1), weight * pltpu.roll(x, (part + 1) % LANES, 1)

        last = turned(first - 1)
        for tile in range(first, first + count):
            now = turned(tile)
            mixed = jnp.where(near_mask, last[0], now[0]) + jnp.where(far_mask, last[1], now[1])
            last = now
            out_ref[:, place * ROWS : (place + 1) * ROWS, pl.ds((tile - first) * LANES, LANES)] = (
                mixed.reshape(bricks, ROWS, LANES).astype(bf16)
            )


def frame_side(raw, order, dark, gain, band, offset, fraction, lo, hi):
    _, frame_rows, columns = raw.shape
    steps = frame_rows // BLOCK_ROWS
    bricks = frame_rows // ROWS
    per = BLOCK_ROWS // 16
    last = frame_rows // 16 - 1
    smem = pl.BlockSpec(memory_space=pltpu.SMEM)
    first, count = lo // LANES, (hi - lo) // LANES

    def three(lead):
        zeros = (0,) * len(lead)
        return [
            pl.BlockSpec(lead + (16, columns), lambda i: zeros + (jnp.maximum(per * i - 1, 0), 0)),
            pl.BlockSpec(lead + (BLOCK_ROWS, columns), lambda i: zeros + (i, 0)),
            pl.BlockSpec(lead + (16, columns), lambda i: zeros + (jnp.minimum(per * i + per, last), 0)),
        ]

    return pl.pallas_call(
        functools.partial(frame_kernel, first, count),
        grid=(steps,),
        in_specs=[smem, smem, smem]
        + three((2,)) + three(()) + three(())
        + [pl.BlockSpec(band.shape, lambda i: (0, 0))],
        out_specs=pl.BlockSpec((BLOCK_ROWS // ROWS, 2 * ROWS, hi - lo), lambda i: (i, 0, 0)),
        out_shape=jax.ShapeDtypeStruct((bricks, 2 * ROWS, hi - lo), jnp.bfloat16),
        scratch_shapes=[pltpu.VMEM((2, BLOCK_ROWS, (LEAD + count) * LANES), jnp.float32)],
        compiler_params=pltpu.CompilerParams(vmem_limit_bytes=VMEM),
        cost_estimate=pl.CostEstimate(
            flops=8_000_000_000, bytes_accessed=6_500_000, transcendentals=0
        ),
        name="frame_side",
    )(order, offset, fraction, raw, raw, raw, dark, dark, dark, gain, gain, gain, band)


def stages(planes, half):
    halo = 2 * ITERS * half
    total = planes + 2 * halo

    def cut(lo, hi, most):
        parts = -(-(hi - lo) // most)
        size = -(-(hi - lo) // (2 * parts)) * 2
        return [(at, min(size, hi - at)) for at in range(lo, hi, size)]

    inner, outer = [], []
    for stage in range(1, 2 * ITERS + 1):
        reach = stage * half
        lo, hi = halo + reach, total - halo - reach
        inner.append([cut(lo, hi, GROUP)])
        outer.append([cut(reach, lo, GROUP), cut(hi, total - reach, GROUP)])
    return inner, outer


def flat(stage):
    return [group for groups in stage for group in groups]


def bands_kernel(taps, lat_taps, plans, psf_ref, lateral_ref, index_ref, *outs):
    matrices, (tl_ref, tm_ref) = outs[:-2], outs[-2:]
    f32 = jnp.float32
    bf16 = jnp.bfloat16
    half = taps // 2
    width = SPAN * ROWS
    index = index_ref[...]
    raw = []
    for tap in range(taps):
        value = jnp.zeros(index.shape, f32)
        for kernel in range(psf_ref.shape[0]):
            value = jnp.where(index == kernel, psf_ref[kernel, tap], value)
        raw.append(value)
    total = functools.reduce(lambda a, b: a + b, raw)
    total = jnp.where(total > 0.0, total, 1.0)
    unit = [value / total for value in raw]
    row = lax.broadcasted_iota(jnp.int32, (width, width), 0)
    col = lax.broadcasted_iota(jnp.int32, (width, width), 1)

    def banded(start, gap, order):
        m = jnp.zeros((width, width), f32)
        for tap in range(taps):
            values = unit[tap][:, start * ROWS : start * ROWS + width]
            m = jnp.where(gap == ROWS * order(tap), values, m)
        return m

    for which, plan in enumerate(plans):
        slot = [0, 0]
        for number, stage in enumerate(plan):
            kind = number % 2
            target = matrices[2 * which + kind]
            for at, _ in flat(stage):
                if kind == 0:
                    m = banded(at, row - col, lambda tap: tap).T
                else:
                    m = banded(at - half, col - row, lambda tap: 2 * half - tap)
                target[slot[kind]] = m[: GROUP * ROWS].astype(bf16)
                slot[kind] += 1

    lateral_total = lateral_ref[0]
    for tap in range(1, lat_taps):
        lateral_total = lateral_total + lateral_ref[tap]
    k = lax.broadcasted_iota(jnp.int32, tl_ref.shape, 0)
    j = lax.broadcasted_iota(jnp.int32, tl_ref.shape, 1)
    place = k - LANES - j + lat_taps // 2
    forward = jnp.zeros(tl_ref.shape, f32)
    backward = jnp.zeros(tl_ref.shape, f32)
    for tap in range(lat_taps):
        forward = jnp.where(place == tap, lateral_ref[tap], forward)
        backward = jnp.where(place == lat_taps - 1 - tap, lateral_ref[tap], backward)
    scale = jnp.full((1, TILE), lateral_total, f32)
    tl_ref[...] = (forward / scale).astype(bf16)
    tm_ref[...] = (backward / scale).astype(bf16)


def bands(psf_bank, lateral_psf, band_index, planes, halo):
    plans = stages(planes, psf_bank.shape[1] // 2)
    spread = jnp.pad(band_index, (halo, halo + SPAN), constant_values=-1)
    first = lax.axis_index("cam") * planes
    length = planes + 2 * halo + SPAN
    mine = lax.dynamic_slice_in_dim(spread, first, length, 0)
    index = jnp.broadcast_to(mine[:, None], (length, ROWS)).reshape(1, length * ROWS)
    smem = pl.BlockSpec(memory_space=pltpu.SMEM)
    vmem = pl.BlockSpec(memory_space=pltpu.VMEM)
    counts = [
        sum(len(flat(stage)) for stage in plan[kind::2]) for plan in plans for kind in range(2)
    ]
    strip = jax.ShapeDtypeStruct((TILE + 2 * LANES, TILE), jnp.bfloat16)
    return pl.pallas_call(
        functools.partial(bands_kernel, psf_bank.shape[1], lateral_psf.shape[0], plans),
        in_specs=[smem, smem, vmem],
        out_specs=[vmem] * 6,
        out_shape=[
            jax.ShapeDtypeStruct((n, GROUP * ROWS, SPAN * ROWS), jnp.bfloat16) for n in counts
        ]
        + [strip, strip],
        compiler_params=pltpu.CompilerParams(vmem_limit_bytes=BANDS_VMEM),
        cost_estimate=pl.CostEstimate(
            flops=2_000_000_000, bytes_accessed=2_000_000, transcendentals=0
        ),
        name="bands",
    )(psf_bank, lateral_psf, index)


def restore_kernel(plan, inside, counts, merge, cut, *refs):
    parts = []
    for count in counts:
        parts.append(refs[:count])
        refs = refs[count:]
    g, gt, tl, tm = refs[:4]
    refs = refs[4:]
    f32 = jnp.float32
    bf16 = jnp.bfloat16
    half = plan[0][0][0][0] if not inside else plan[1][0][0][0] - plan[0][0][0][0]
    halo = 2 * ITERS * half
    if inside:
        out, q_out, e_out, mf, ef, mb, qb, pad, pad_back = refs
    else:
        q_in, e_in, middle = refs[:3]
        earlier = refs[3] if merge else None
        out, mf, ef, mb, qb, pad, pad_back = refs[3 + merge :]
    size, columns = mf.shape
    total = size // ROWS
    tiles = columns // TILE

    for buffer in (pad, pad_back):
        buffer[:, :LANES] = jnp.zeros((size, LANES), bf16)
        buffer[:, LANES + columns :] = jnp.zeros((size, LANES), bf16)

    at_column = 0
    for part in parts:
        width = part[0].shape[-1]
        at_row = halo * ROWS if inside else 0
        for ref in part:
            height = ref.shape[0] * ref.shape[1]
            for col in range(0, width, TILE):
                whole = ref[:, :, col : col + TILE].reshape(height, TILE)
                there = slice(at_column + col, at_column + col + TILE)
                mb[at_row : at_row + height, there] = whole
                mf[at_row : at_row + height, there] = whole.astype(f32)
            at_row += height
        at_column += width

    q_rows = slice((halo + half) * ROWS, (total - halo - half) * ROWS)
    e_width = half * (2 * ITERS - 2) * ROWS
    e_low = (halo + 2 * half) * ROWS
    e_high = (total - halo - 2 * half) * ROWS - e_width
    if not inside:
        qb[q_rows, :] = q_in[...]
        for number, start in enumerate((e_low, e_high)):
            e = e_in[number * e_width : (number + 1) * e_width, :]
            ef[start : start + e_width, :] = e
            mb[start : start + e_width, :] = e.astype(bf16)
        for lo in range(0, out.shape[-1] if not merge else 0, LANES):
            out[half * 4 : out.shape[0] - half * 4, :, lo : lo + LANES] = middle[:, :, lo : lo + LANES]

    def columns_of(tile):
        return slice(tile * TILE, (tile + 1) * TILE)

    def within(tile):
        return slice(LANES + tile * TILE, LANES + (tile + 1) * TILE)

    def around(tile):
        return slice(tile * TILE, (tile + 1) * TILE + 2 * LANES)

    def rows_of(groups):
        return slice(groups[0][0] * ROWS, (groups[-1][0] + groups[-1][1]) * ROWS)

    def axial(matrices, skip, stage, source, target, tile):
        for number, (first, count) in enumerate(flat(stage)):
            low = (first - half) * ROWS
            high = (first + count + half) * ROWS
            r = jnp.dot(
                matrices[skip + number, : count * ROWS, : high - low],
                source[low:high, columns_of(tile)],
                preferred_element_type=f32,
            )
            target[first * ROWS : (first + count) * ROWS, within(tile)] = r.astype(bf16)

    for sweep in range(ITERS):
        ahead, back = plan[2 * sweep], plan[2 * sweep + 1]
        skip_ahead = sum(len(flat(stage)) for stage in plan[0 : 2 * sweep : 2])
        skip_back = sum(len(flat(stage)) for stage in plan[1 : 2 * sweep : 2])
        final = sweep == ITERS - 1

        def ratio(tile):
            cols = columns_of(tile)
            for groups in ahead:
                rows = rows_of(groups)
                b = jnp.dot(pad[rows, around(tile)], tl[...], preferred_element_type=f32) + BACKGROUND
                guess = pl.reciprocal(b, approx=True)
                guess = guess * (2.0 - b * guess)
                qb[rows, cols] = (mf[rows, cols] * guess).astype(bf16)

        def update(tile):
            cols = columns_of(tile)
            for groups in back:
                rows = rows_of(groups)
                d = jnp.dot(pad_back[rows, around(tile)], tm[...], preferred_element_type=f32)
                e = (mf if sweep == 0 else ef)[rows, cols] * d
                if not final:
                    ef[rows, cols] = e
                    mb[rows, cols] = e.astype(bf16)
                    continue
                e = e.reshape(-1, ROWS, TILE).astype(bf16)
                first = groups[0][0] - plan[-1][0][0][0]
                start = (out.shape[-1] - columns if cut else 0) + tile * TILE
                drop = cut if tile == 0 else 0
                keep = min(TILE, out.shape[-1] - start)
                if keep > drop:
                    out[first : first + e.shape[0], :, start + drop : start + keep] = e[:, :, drop:keep]

        for step in range(tiles + 5):
            if step < tiles:
                axial(g, skip_ahead, ahead, mb, pad, step)
            if 0 <= step - 2 < tiles:
                ratio(step - 2)
            if 0 <= step - 3 < tiles:
                axial(gt, skip_back, back, qb, pad_back, step - 3)
            if 0 <= step - 5 < tiles:
                update(step - 5)

    if inside:
        q_out[...] = qb[q_rows, :]
        e_out[:e_width, :] = ef[e_low : e_low + e_width, :]
        e_out[e_width:, :] = ef[e_high : e_high + e_width, :]
    elif merge:
        kept = earlier.shape[-1]
        out[:, :, :kept] = earlier[...]
        out[half * 4 : out.shape[0] - half * 4, :, kept:] = middle[:, :, columns - (out.shape[-1] - kept) :]


def restore(parts, matrices, state, earlier, plan, inside, planes, half, columns):
    merge = earlier is not None
    operands, specs, width = [], [], 0
    for number, part in enumerate(parts):
        kept = 2 * LANES if number < len(parts) - 1 else part[0].shape[-1]
        for array in part:
            block = array.shape[:2] + (kept,)
            index = (0, 0, array.shape[-1] // kept - 1)
            operands.append(array)
            specs.append(pl.BlockSpec(block, lambda i, index=index: index))
        width += kept

    def whole(array):
        return pl.BlockSpec(array.shape, lambda i: (0,) * len(array.shape))

    for array in (*matrices, *state, *([earlier] if merge else [])):
        operands.append(array)
        specs.append(whole(array))
    halo = 2 * ITERS * half
    height = (planes + 2 * halo) * ROWS
    bf16 = jnp.bfloat16
    if inside:
        cut = 0
        results = [
            jax.ShapeDtypeStruct((planes - 2 * halo, ROWS, width), bf16),
            jax.ShapeDtypeStruct(((planes - 2 * half) * ROWS, width), bf16),
            jax.ShapeDtypeStruct((2 * half * (2 * ITERS - 2) * ROWS, width), jnp.float32),
        ]
    else:
        cut = LANES if merge else 0
        results = [jax.ShapeDtypeStruct((planes, ROWS, columns if merge else width - LANES), bf16)]
    return pl.pallas_call(
        functools.partial(restore_kernel, plan, inside, [len(part) for part in parts], merge, cut),
        grid=(1,),
        in_specs=specs,
        out_specs=[whole(result) for result in results],
        out_shape=results,
        scratch_shapes=[
            pltpu.VMEM((height, width), jnp.float32),
            pltpu.VMEM((height, width), jnp.float32),
            pltpu.VMEM((height, width), bf16),
            pltpu.VMEM((height, width), bf16),
            pltpu.VMEM((height, width + 2 * LANES), bf16),
            pltpu.VMEM((height, width + 2 * LANES), bf16),
        ],
        compiler_params=pltpu.CompilerParams(vmem_limit_bytes=RESTORE_VMEM),
        cost_estimate=pl.CostEstimate(
            flops=5_000_000_000, bytes_accessed=8_000_000, transcendentals=0
        ),
        name="inside" if inside else "ends",
    )(*operands)


def local(
    raw_frames,
    frame_order,
    dark_frame,
    flat_gain,
    stripe_band,
    shear_offset,
    shear_fraction,
    band_index,
    psf_bank,
    lateral_psf,
):
    half = psf_bank.shape[1] // 2
    planes = shear_offset.shape[0]
    columns = raw_frames.shape[-1]
    halo = 2 * ITERS * half
    inner, outer = stages(planes, half)
    count = lax.axis_size("cam")
    forward = [(i, i + 1) for i in range(count - 1)]
    backward = [(i + 1, i) for i in range(count - 1)]
    *axial, forward_lateral, backward_lateral = bands(psf_bank, lateral_psf, band_index, planes, halo)
    inner_matrices = (*axial[:2], forward_lateral, backward_lateral)
    outer_matrices = (*axial[2:], forward_lateral, backward_lateral)
    depth = halo // 2
    first_piece = frame_side(
        raw_frames, frame_order, dark_frame, flat_gain, stripe_band, shear_offset, shear_fraction, 0, SPLIT
    )
    first_piece, later_order = lax.optimization_barrier((first_piece, frame_order))
    second_piece = frame_side(
        raw_frames, later_order, dark_frame, flat_gain, stripe_band, shear_offset, shear_fraction,
        SPLIT, columns,
    )
    second_piece, inner_matrices, outer_matrices = lax.optimization_barrier(
        (second_piece, inner_matrices, outer_matrices)
    )
    result = None
    parts = []
    centres = []
    for piece in (first_piece, second_piece):
        centre = lax.all_to_all(piece, "brick", split_axis=0, concat_axis=0, tiled=True)
        low = lax.ppermute(centre[-depth:], "cam", forward)
        high = lax.ppermute(centre[:depth], "cam", backward)
        centres.append((centre,))
        parts.append((low, centre, high))
        middle, quotients, estimates = restore(
            centres, inner_matrices, (), None, inner, True, planes, half, columns
        )
        (result,) = restore(
            parts, outer_matrices, (quotients, estimates, middle), result, outer, False, planes, half,
            columns,
        )
    return result


def solution(mesh):
    placed = (
        P(("cam", "brick"), None, None),
        P(("cam", "brick"), None),
        P(),
        P(),
        P(),
        P("cam"),
        P("cam"),
        P(),
        P(),
        P(),
    )
    return jax.shard_map(
        local, mesh=mesh, in_specs=placed, out_specs=P("cam", "brick", None), check_vma=False
    )
```

```python
import functools

import jax
import jax.numpy as jnp
from jax import lax
from jax.experimental import pallas as pl
from jax.experimental.pallas import tpu as pltpu
from jax.sharding import PartitionSpec as P

SHEAR = 512
ITERS = 2
BACKGROUND = 1.0

LANES = 128
TILE = 256
ROWS = 8
BLOCK_ROWS = 64
LEAD = SHEAR // LANES + 1
SPLIT = 1280
VMEM = 60 * 1024 * 1024
BANDS_VMEM = 20 * 1024 * 1024
RESTORE_VMEM = 42 * 1024 * 1024
GROUP = 20
SPAN = 32


def frame_kernel(
    first, count,
    order_ref, offset_ref, fraction_ref,
    raw_prev, raw_main, raw_next,
    dark_prev, dark_main, dark_next,
    gain_prev, gain_main, gain_next,
    band_ref, out_ref, scratch,
):
    step = pl.program_id(0)
    steps = pl.num_programs(0)
    rows = BLOCK_ROWS + 16
    brick = lax.axis_index("brick")
    f32 = jnp.float32
    bf16 = jnp.bfloat16
    base = first - LEAD

    @pl.when(step == 0)
    def _():
        if base < 0:
            scratch[:, :, : -base * LANES] = jnp.zeros((2, BLOCK_ROWS, -base * LANES), f32)

    has_prev = (step > 0).astype(f32)
    has_next = (step < steps - 1).astype(f32)
    frames = [jnp.where(order_ref[0, 0] == place, 0, 1) for place in range(2)]

    for tile in range(max(base, 0), first + count):
        cols = pl.ds(tile * LANES, LANES)
        band = band_ref[:, cols]
        levels = []
        for part, keep in ((0, slice(8, 16)), (1, slice(None)), (2, slice(0, 8))):
            dark = (dark_prev, dark_main, dark_next)[part][:, cols].astype(f32)[keep]
            gain = (gain_prev, gain_main, gain_next)[part][:, cols].astype(f32)[keep]
            if part != 1:
                gain = gain * (has_prev, None, has_next)[part]
            levels.append((dark, gain, keep))
        for place in range(2):
            f = jnp.concatenate(
                [
                    (raw[frames[place], :, cols].astype(f32)[keep] - dark) * gain
                    for raw, (dark, gain, keep) in zip((raw_prev, raw_main, raw_next), levels)
                ],
                axis=0,
            )
            after = pltpu.roll(f, rows - 1, 0)
            before = pltpu.roll(f, 1, 0)

            def three(k):
                return band[k : k + 1] * before + band[k + 1 : k + 2] * f + band[k + 2 : k + 3] * after

            out = (
                f
                + three(3)
                + pltpu.roll(three(6), rows - 3, 0)
                + pltpu.roll(three(0), 3, 0)
            )[8 : 8 + BLOCK_ROWS]
            scratch[place, :, pl.ds((tile - base) * LANES, LANES)] = out.astype(bf16).astype(f32)

    lane = lax.broadcasted_iota(jnp.int32, (BLOCK_ROWS, LANES), 1)
    bricks = BLOCK_ROWS // ROWS
    for place in range(2):
        amount = offset_ref[brick * 2 + place]
        weight = fraction_ref[brick * 2 + place]
        whole = amount // LANES
        part = amount % LANES
        near_mask = lane < part
        far_mask = lane < part + 1

        def turned(tile):
            start = (tile - base - whole) * LANES
            x = scratch[place, :, pl.ds(pl.multiple_of(start, LANES), LANES)]
            return (1.0 - weight) * pltpu.roll(x, part, 1), weight * pltpu.roll(x, (part + 1) % LANES, 1)

        last = turned(first - 1)
        for tile in range(first, first + count):
            now = turned(tile)
            mixed = jnp.where(near_mask, last[0], now[0]) + jnp.where(far_mask, last[1], now[1])
            last = now
            out_ref[:, place * ROWS : (place + 1) * ROWS, pl.ds((tile - first) * LANES, LANES)] = (
                mixed.reshape(bricks, ROWS, LANES).astype(bf16)
            )


def frame_side(raw, order, dark, gain, band, offset, fraction, lo, hi):
    _, frame_rows, columns = raw.shape
    steps = frame_rows // BLOCK_ROWS
    bricks = frame_rows // ROWS
    per = BLOCK_ROWS // 16
    last = frame_rows // 16 - 1
    smem = pl.BlockSpec(memory_space=pltpu.SMEM)
    first, count = lo // LANES, (hi - lo) // LANES

    def three(lead):
        zeros = (0,) * len(lead)
        return [
            pl.BlockSpec(lead + (16, columns), lambda i: zeros + (jnp.maximum(per * i - 1, 0), 0)),
            pl.BlockSpec(lead + (BLOCK_ROWS, columns), lambda i: zeros + (i, 0)),
            pl.BlockSpec(lead + (16, columns), lambda i: zeros + (jnp.minimum(per * i + per, last), 0)),
        ]

    return pl.pallas_call(
        functools.partial(frame_kernel, first, count),
        grid=(steps,),
        in_specs=[smem, smem, smem]
        + three((2,)) + three(()) + three(())
        + [pl.BlockSpec(band.shape, lambda i: (0, 0))],
        out_specs=pl.BlockSpec((BLOCK_ROWS // ROWS, 2 * ROWS, hi - lo), lambda i: (i, 0, 0)),
        out_shape=jax.ShapeDtypeStruct((bricks, 2 * ROWS, hi - lo), jnp.bfloat16),
        scratch_shapes=[pltpu.VMEM((2, BLOCK_ROWS, (LEAD + count) * LANES), jnp.float32)],
        compiler_params=pltpu.CompilerParams(vmem_limit_bytes=VMEM),
        cost_estimate=pl.CostEstimate(
            flops=8_000_000_000, bytes_accessed=6_500_000, transcendentals=0
        ),
        name="frame_side",
    )(order, offset, fraction, raw, raw, raw, dark, dark, dark, gain, gain, gain, band)


def stages(planes, half):
    halo = 2 * ITERS * half
    total = planes + 2 * halo

    def cut(lo, hi, most):
        parts = -(-(hi - lo) // most)
        size = -(-(hi - lo) // (2 * parts)) * 2
        return [(at, min(size, hi - at)) for at in range(lo, hi, size)]

    inner, outer = [], []
    for stage in range(1, 2 * ITERS + 1):
        reach = stage * half
        lo, hi = halo + reach, total - halo - reach
        inner.append([cut(lo, hi, GROUP)])
        outer.append([cut(reach, lo, GROUP), cut(hi, total - reach, GROUP)])
    return inner, outer


def flat(stage):
    return [group for groups in stage for group in groups]


def bands_kernel(taps, lat_taps, plans, psf_ref, lateral_ref, index_ref, *outs):
    matrices, (tl_ref, tm_ref) = outs[:-2], outs[-2:]
    f32 = jnp.float32
    bf16 = jnp.bfloat16
    half = taps // 2
    width = SPAN * ROWS
    index = index_ref[...]
    raw = []
    for tap in range(taps):
        value = jnp.zeros(index.shape, f32)
        for kernel in range(psf_ref.shape[0]):
            value = jnp.where(index == kernel, psf_ref[kernel, tap], value)
        raw.append(value)
    total = functools.reduce(lambda a, b: a + b, raw)
    total = jnp.where(total > 0.0, total, 1.0)
    unit = [value / total for value in raw]
    row = lax.broadcasted_iota(jnp.int32, (width, width), 0)
    col = lax.broadcasted_iota(jnp.int32, (width, width), 1)

    def banded(start, gap, order):
        m = jnp.zeros((width, width), f32)
        for tap in range(taps):
            values = unit[tap][:, start * ROWS : start * ROWS + width]
            m = jnp.where(gap == ROWS * order(tap), values, m)
        return m

    for which, plan in enumerate(plans):
        slot = [0, 0]
        for number, stage in enumerate(plan):
            kind = number % 2
            target = matrices[2 * which + kind]
            for at, _ in flat(stage):
                if kind == 0:
                    m = banded(at, row - col, lambda tap: tap).T
                else:
                    m = banded(at - half, col - row, lambda tap: 2 * half - tap)
                target[slot[kind]] = m[: GROUP * ROWS].astype(bf16)
                slot[kind] += 1

    lateral_total = lateral_ref[0]
    for tap in range(1, lat_taps):
        lateral_total = lateral_total + lateral_ref[tap]
    k = lax.broadcasted_iota(jnp.int32, tl_ref.shape, 0)
    j = lax.broadcasted_iota(jnp.int32, tl_ref.shape, 1)
    place = k - LANES - j + lat_taps // 2
    forward = jnp.zeros(tl_ref.shape, f32)
    backward = jnp.zeros(tl_ref.shape, f32)
    for tap in range(lat_taps):
        forward = jnp.where(place == tap, lateral_ref[tap], forward)
        backward = jnp.where(place == lat_taps - 1 - tap, lateral_ref[tap], backward)
    scale = jnp.full((1, TILE), lateral_total, f32)
    tl_ref[...] = (forward / scale).astype(bf16)
    tm_ref[...] = (backward / scale).astype(bf16)


def bands(psf_bank, lateral_psf, band_index, planes, halo):
    plans = stages(planes, psf_bank.shape[1] // 2)
    spread = jnp.pad(band_index, (halo, halo + SPAN), constant_values=-1)
    first = lax.axis_index("cam") * planes
    length = planes + 2 * halo + SPAN
    mine = lax.dynamic_slice_in_dim(spread, first, length, 0)
    index = jnp.broadcast_to(mine[:, None], (length, ROWS)).reshape(1, length * ROWS)
    smem = pl.BlockSpec(memory_space=pltpu.SMEM)
    vmem = pl.BlockSpec(memory_space=pltpu.VMEM)
    counts = [
        sum(len(flat(stage)) for stage in plan[kind::2]) for plan in plans for kind in range(2)
    ]
    strip = jax.ShapeDtypeStruct((TILE + 2 * LANES, TILE), jnp.bfloat16)
    return pl.pallas_call(
        functools.partial(bands_kernel, psf_bank.shape[1], lateral_psf.shape[0], plans),
        in_specs=[smem, smem, vmem],
        out_specs=[vmem] * 6,
        out_shape=[
            jax.ShapeDtypeStruct((n, GROUP * ROWS, SPAN * ROWS), jnp.bfloat16) for n in counts
        ]
        + [strip, strip],
        compiler_params=pltpu.CompilerParams(vmem_limit_bytes=BANDS_VMEM),
        cost_estimate=pl.CostEstimate(
            flops=2_000_000_000, bytes_accessed=2_000_000, transcendentals=0
        ),
        name="bands",
    )(psf_bank, lateral_psf, index)


def restore_kernel(plan, inside, counts, merge, cut, *refs):
    parts = []
    for count in counts:
        parts.append(refs[:count])
        refs = refs[count:]
    g, gt, tl, tm = refs[:4]
    refs = refs[4:]
    f32 = jnp.float32
    bf16 = jnp.bfloat16
    half = plan[0][0][0][0] if not inside else plan[1][0][0][0] - plan[0][0][0][0]
    halo = 2 * ITERS * half
    if inside:
        out, q_out, e_out, mf, ef, mb, qb, pad, pad_back = refs
    else:
        q_in, e_in, middle = refs[:3]
        earlier = refs[3] if merge else None
        out, mf, ef, mb, qb, pad, pad_back = refs[3 + merge :]
    size, columns = mf.shape
    total = size // ROWS
    tiles = columns // TILE

    for buffer in (pad, pad_back):
        buffer[:, :LANES] = jnp.zeros((size, LANES), bf16)
        buffer[:, LANES + columns :] = jnp.zeros((size, LANES), bf16)

    at_column = 0
    for part in parts:
        width = part[0].shape[-1]
        at_row = halo * ROWS if inside else 0
        for ref in part:
            height = ref.shape[0] * ref.shape[1]
            for col in range(0, width, TILE):
                whole = ref[:, :, col : col + TILE].reshape(height, TILE)
                there = slice(at_column + col, at_column + col + TILE)
                mb[at_row : at_row + height, there] = whole
                mf[at_row : at_row + height, there] = whole.astype(f32)
            at_row += height
        at_column += width

    q_rows = slice((halo + half) * ROWS, (total - halo - half) * ROWS)
    e_width = half * (2 * ITERS - 2) * ROWS
    e_low = (halo + 2 * half) * ROWS
    e_high = (total - halo - 2 * half) * ROWS - e_width
    if not inside:
        qb[q_rows, :] = q_in[...]
        for number, start in enumerate((e_low, e_high)):
            e = e_in[number * e_width : (number + 1) * e_width, :]
            ef[start : start + e_width, :] = e
            mb[start : start + e_width, :] = e.astype(bf16)
        for lo in range(0, out.shape[-1] if not merge else 0, LANES):
            out[half * 4 : out.shape[0] - half * 4, :, lo : lo + LANES] = middle[:, :, lo : lo + LANES]

    def columns_of(tile):
        return slice(tile * TILE, (tile + 1) * TILE)

    def within(tile):
        return slice(LANES + tile * TILE, LANES + (tile + 1) * TILE)

    def around(tile):
        return slice(tile * TILE, (tile + 1) * TILE + 2 * LANES)

    def rows_of(groups):
        return slice(groups[0][0] * ROWS, (groups[-1][0] + groups[-1][1]) * ROWS)

    def axial(matrices, skip, stage, source, target, tile):
        for number, (first, count) in enumerate(flat(stage)):
            low = (first - half) * ROWS
            high = (first + count + half) * ROWS
            r = jnp.dot(
                matrices[skip + number, : count * ROWS, : high - low],
                source[low:high, columns_of(tile)],
                preferred_element_type=f32,
            )
            target[first * ROWS : (first + count) * ROWS, within(tile)] = r.astype(bf16)

    for sweep in range(ITERS):
        ahead, back = plan[2 * sweep], plan[2 * sweep + 1]
        skip_ahead = sum(len(flat(stage)) for stage in plan[0 : 2 * sweep : 2])
        skip_back = sum(len(flat(stage)) for stage in plan[1 : 2 * sweep : 2])
        final = sweep == ITERS - 1

        def ratio(tile):
            cols = columns_of(tile)
            for groups in ahead:
                rows = rows_of(groups)
                b = jnp.dot(pad[rows, around(tile)], tl[...], preferred_element_type=f32) + BACKGROUND
                guess = pl.reciprocal(b, approx=True)
                guess = guess * (2.0 - b * guess)
                qb[rows, cols] = (mf[rows, cols] * guess).astype(bf16)

        def update(tile):
            cols = columns_of(tile)
            for groups in back:
                rows = rows_of(groups)
                d = jnp.dot(pad_back[rows, around(tile)], tm[...], preferred_element_type=f32)
                e = (mf if sweep == 0 else ef)[rows, cols] * d
                if not final:
                    ef[rows, cols] = e
                    mb[rows, cols] = e.astype(bf16)
                    continue
                e = e.reshape(-1, ROWS, TILE).astype(bf16)
                first = groups[0][0] - plan[-1][0][0][0]
                start = (out.shape[-1] - columns if cut else 0) + tile * TILE
                drop = cut if tile == 0 else 0
                keep = min(TILE, out.shape[-1] - start)
                if keep > drop:
                    out[first : first + e.shape[0], :, start + drop : start + keep] = e[:, :, drop:keep]

        for step in range(tiles + 5):
            if step < tiles:
                axial(g, skip_ahead, ahead, mb, pad, step)
            if 0 <= step - 2 < tiles:
                ratio(step - 2)
            if 0 <= step - 3 < tiles:
                axial(gt, skip_back, back, qb, pad_back, step - 3)
            if 0 <= step - 5 < tiles:
                update(step - 5)

    if inside:
        q_out[...] = qb[q_rows, :]
        e_out[:e_width, :] = ef[e_low : e_low + e_width, :]
        e_out[e_width:, :] = ef[e_high : e_high + e_width, :]
    elif merge:
        kept = earlier.shape[-1]
        out[:, :, :kept] = earlier[...]
        out[half * 4 : out.shape[0] - half * 4, :, kept:] = middle[:, :, columns - (out.shape[-1] - kept) :]


def restore(parts, matrices, state, earlier, plan, inside, planes, half, columns):
    merge = earlier is not None
    operands, specs, width = [], [], 0
    for number, part in enumerate(parts):
        kept = 2 * LANES if number < len(parts) - 1 else part[0].shape[-1]
        for array in part:
            block = array.shape[:2] + (kept,)
            index = (0, 0, array.shape[-1] // kept - 1)
            operands.append(array)
            specs.append(pl.BlockSpec(block, lambda i, index=index: index))
        width += kept

    def whole(array):
        return pl.BlockSpec(array.shape, lambda i: (0,) * len(array.shape))

    for array in (*matrices, *state, *([earlier] if merge else [])):
        operands.append(array)
        specs.append(whole(array))
    halo = 2 * ITERS * half
    height = (planes + 2 * halo) * ROWS
    bf16 = jnp.bfloat16
    if inside:
        cut = 0
        results = [
            jax.ShapeDtypeStruct((planes - 2 * halo, ROWS, width), bf16),
            jax.ShapeDtypeStruct(((planes - 2 * half) * ROWS, width), bf16),
            jax.ShapeDtypeStruct((2 * half * (2 * ITERS - 2) * ROWS, width), jnp.float32),
        ]
    else:
        cut = LANES if merge else 0
        results = [jax.ShapeDtypeStruct((planes, ROWS, columns if merge else width - LANES), bf16)]
    return pl.pallas_call(
        functools.partial(restore_kernel, plan, inside, [len(part) for part in parts], merge, cut),
        grid=(1,),
        in_specs=specs,
        out_specs=[whole(result) for result in results],
        out_shape=results,
        scratch_shapes=[
            pltpu.VMEM((height, width), jnp.float32),
            pltpu.VMEM((height, width), jnp.float32),
            pltpu.VMEM((height, width), bf16),
            pltpu.VMEM((height, width), bf16),
            pltpu.VMEM((height, width + 2 * LANES), bf16),
            pltpu.VMEM((height, width + 2 * LANES), bf16),
        ],
        compiler_params=pltpu.CompilerParams(vmem_limit_bytes=RESTORE_VMEM),
        cost_estimate=pl.CostEstimate(
            flops=5_000_000_000, bytes_accessed=8_000_000, transcendentals=0
        ),
        name="inside" if inside else "ends",
    )(*operands)


def local(
    raw_frames,
    frame_order,
    dark_frame,
    flat_gain,
    stripe_band,
    shear_offset,
    shear_fraction,
    band_index,
    psf_bank,
    lateral_psf,
):
    half = psf_bank.shape[1] // 2
    planes = shear_offset.shape[0]
    columns = raw_frames.shape[-1]
    halo = 2 * ITERS * half
    inner, outer = stages(planes, half)
    count = lax.axis_size("cam")
    forward = [(i, i + 1) for i in range(count - 1)]
    backward = [(i + 1, i) for i in range(count - 1)]
    *axial, forward_lateral, backward_lateral = bands(psf_bank, lateral_psf, band_index, planes, halo)
    inner_matrices = (*axial[:2], forward_lateral, backward_lateral)
    outer_matrices = (*axial[2:], forward_lateral, backward_lateral)
    depth = halo // 2
    first_piece = frame_side(
        raw_frames, frame_order, dark_frame, flat_gain, stripe_band, shear_offset, shear_fraction, 0, SPLIT
    )
    first_piece, later_order = lax.optimization_barrier((first_piece, frame_order))
    second_piece = frame_side(
        raw_frames, later_order, dark_frame, flat_gain, stripe_band, shear_offset, shear_fraction,
        SPLIT, columns,
    )
    result = None
    parts = []
    centres = []
    for number in range(2):
        piece = second_piece if number else first_piece
        centre = lax.all_to_all(piece, "brick", split_axis=0, concat_axis=0, tiled=True)
        if number == 0:
            centre, second_piece, inner_matrices, outer_matrices = lax.optimization_barrier(
                (centre, second_piece, inner_matrices, outer_matrices)
            )
        low = lax.ppermute(centre[-depth:], "cam", forward)
        high = lax.ppermute(centre[:depth], "cam", backward)
        centres.append((centre,))
        parts.append((low, centre, high))
        middle, quotients, estimates = restore(
            centres, inner_matrices, (), None, inner, True, planes, half, columns
        )
        (result,) = restore(
            parts, outer_matrices, (quotients, estimates, middle), result, outer, False, planes, half,
            columns,
        )
    return result


def solution(mesh):
    placed = (
        P(("cam", "brick"), None, None),
        P(("cam", "brick"), None),
        P(),
        P(),
        P(),
        P("cam"),
        P("cam"),
        P(),
        P(),
        P(),
    )
    return jax.shard_map(
        local, mesh=mesh, in_specs=placed, out_specs=P("cam", "brick", None), check_vma=False
    )
```

```python
import functools

import jax
import jax.numpy as jnp
from jax import lax
from jax.experimental import pallas as pl
from jax.experimental.pallas import tpu as pltpu
from jax.sharding import PartitionSpec as P

SHEAR = 512
ITERS = 2
BACKGROUND = 1.0

LANES = 128
TILE = 256
ROWS = 8
BLOCK_ROWS = 64
LEAD = SHEAR // LANES + 1
SPLIT = 1280
VMEM = 60 * 1024 * 1024
BANDS_VMEM = 20 * 1024 * 1024
RESTORE_VMEM = 42 * 1024 * 1024
GROUP = 20
SPAN = 32


def frame_kernel(
    first, count,
    order_ref, offset_ref, fraction_ref,
    raw_prev, raw_main, raw_next,
    dark_prev, dark_main, dark_next,
    gain_prev, gain_main, gain_next,
    band_ref, out_ref, scratch,
):
    step = pl.program_id(0)
    steps = pl.num_programs(0)
    rows = BLOCK_ROWS + 16
    brick = lax.axis_index("brick")
    f32 = jnp.float32
    bf16 = jnp.bfloat16
    base = first - LEAD

    @pl.when(step == 0)
    def _():
        if base < 0:
            scratch[:, :, : -base * LANES] = jnp.zeros((2, BLOCK_ROWS, -base * LANES), f32)

    has_prev = (step > 0).astype(f32)
    has_next = (step < steps - 1).astype(f32)
    frames = [jnp.where(order_ref[0, 0] == place, 0, 1) for place in range(2)]

    for tile in range(max(base, 0), first + count):
        cols = pl.ds(tile * LANES, LANES)
        band = band_ref[:, cols]
        levels = []
        for part, keep in ((0, slice(8, 16)), (1, slice(None)), (2, slice(0, 8))):
            dark = (dark_prev, dark_main, dark_next)[part][:, cols].astype(f32)[keep]
            gain = (gain_prev, gain_main, gain_next)[part][:, cols].astype(f32)[keep]
            if part != 1:
                gain = gain * (has_prev, None, has_next)[part]
            levels.append((dark, gain, keep))
        for place in range(2):
            f = jnp.concatenate(
                [
                    (raw[frames[place], :, cols].astype(f32)[keep] - dark) * gain
                    for raw, (dark, gain, keep) in zip((raw_prev, raw_main, raw_next), levels)
                ],
                axis=0,
            )
            after = pltpu.roll(f, rows - 1, 0)
            before = pltpu.roll(f, 1, 0)

            def three(k):
                return band[k : k + 1] * before + band[k + 1 : k + 2] * f + band[k + 2 : k + 3] * after

            out = (
                f
                + three(3)
                + pltpu.roll(three(6), rows - 3, 0)
                + pltpu.roll(three(0), 3, 0)
            )[8 : 8 + BLOCK_ROWS]
            scratch[place, :, pl.ds((tile - base) * LANES, LANES)] = out.astype(bf16).astype(f32)

    lane = lax.broadcasted_iota(jnp.int32, (BLOCK_ROWS, LANES), 1)
    bricks = BLOCK_ROWS // ROWS
    for place in range(2):
        amount = offset_ref[brick * 2 + place]
        weight = fraction_ref[brick * 2 + place]
        whole = amount // LANES
        part = amount % LANES
        near_mask = lane < part
        far_mask = lane < part + 1

        def turned(tile):
            start = (tile - base - whole) * LANES
            x = scratch[place, :, pl.ds(pl.multiple_of(start, LANES), LANES)]
            return (1.0 - weight) * pltpu.roll(x, part, 1), weight * pltpu.roll(x, (part + 1) % LANES, 1)

        last = turned(first - 1)
        for tile in range(first, first + count):
            now = turned(tile)
            mixed = jnp.where(near_mask, last[0], now[0]) + jnp.where(far_mask, last[1], now[1])
            last = now
            out_ref[:, place * ROWS : (place + 1) * ROWS, pl.ds((tile - first) * LANES, LANES)] = (
                mixed.reshape(bricks, ROWS, LANES).astype(bf16)
            )


def frame_side(raw, order, dark, gain, band, offset, fraction, lo, hi):
    _, frame_rows, columns = raw.shape
    steps = frame_rows // BLOCK_ROWS
    bricks = frame_rows // ROWS
    per = BLOCK_ROWS // 16
    last = frame_rows // 16 - 1
    smem = pl.BlockSpec(memory_space=pltpu.SMEM)
    first, count = lo // LANES, (hi - lo) // LANES

    def three(lead):
        zeros = (0,) * len(lead)
        return [
            pl.BlockSpec(lead + (16, columns), lambda i: zeros + (jnp.maximum(per * i - 1, 0), 0)),
            pl.BlockSpec(lead + (BLOCK_ROWS, columns), lambda i: zeros + (i, 0)),
            pl.BlockSpec(lead + (16, columns), lambda i: zeros + (jnp.minimum(per * i + per, last), 0)),
        ]

    return pl.pallas_call(
        functools.partial(frame_kernel, first, count),
        grid=(steps,),
        in_specs=[smem, smem, smem]
        + three((2,)) + three(()) + three(())
        + [pl.BlockSpec(band.shape, lambda i: (0, 0))],
        out_specs=pl.BlockSpec((BLOCK_ROWS // ROWS, 2 * ROWS, hi - lo), lambda i: (i, 0, 0)),
        out_shape=jax.ShapeDtypeStruct((bricks, 2 * ROWS, hi - lo), jnp.bfloat16),
        scratch_shapes=[pltpu.VMEM((2, BLOCK_ROWS, (LEAD + count) * LANES), jnp.float32)],
        compiler_params=pltpu.CompilerParams(vmem_limit_bytes=VMEM),
        cost_estimate=pl.CostEstimate(
            flops=8_000_000_000, bytes_accessed=6_500_000, transcendentals=0
        ),
        name="frame_side",
    )(order, offset, fraction, raw, raw, raw, dark, dark, dark, gain, gain, gain, band)


def stages(planes, half):
    halo = 2 * ITERS * half
    total = planes + 2 * halo

    def cut(lo, hi, most):
        parts = -(-(hi - lo) // most)
        size = -(-(hi - lo) // (2 * parts)) * 2
        return [(at, min(size, hi - at)) for at in range(lo, hi, size)]

    inner, outer = [], []
    for stage in range(1, 2 * ITERS + 1):
        reach = stage * half
        lo, hi = halo + reach, total - halo - reach
        inner.append([cut(lo, hi, GROUP)])
        outer.append([cut(reach, lo, GROUP), cut(hi, total - reach, GROUP)])
    return inner, outer


def flat(stage):
    return [group for groups in stage for group in groups]


def bands_kernel(taps, lat_taps, plans, psf_ref, lateral_ref, index_ref, *outs):
    matrices, (tl_ref, tm_ref) = outs[:-2], outs[-2:]
    f32 = jnp.float32
    bf16 = jnp.bfloat16
    half = taps // 2
    width = SPAN * ROWS
    index = index_ref[...]
    raw = []
    for tap in range(taps):
        value = jnp.zeros(index.shape, f32)
        for kernel in range(psf_ref.shape[0]):
            value = jnp.where(index == kernel, psf_ref[kernel, tap], value)
        raw.append(value)
    total = functools.reduce(lambda a, b: a + b, raw)
    total = jnp.where(total > 0.0, total, 1.0)
    unit = [value / total for value in raw]
    row = lax.broadcasted_iota(jnp.int32, (width, width), 0)
    col = lax.broadcasted_iota(jnp.int32, (width, width), 1)

    def banded(start, gap, order):
        m = jnp.zeros((width, width), f32)
        for tap in range(taps):
            values = unit[tap][:, start * ROWS : start * ROWS + width]
            m = jnp.where(gap == ROWS * order(tap), values, m)
        return m

    for which, plan in enumerate(plans):
        slot = [0, 0]
        for number, stage in enumerate(plan):
            kind = number % 2
            target = matrices[2 * which + kind]
            for at, _ in flat(stage):
                if kind == 0:
                    m = banded(at, row - col, lambda tap: tap).T
                else:
                    m = banded(at - half, col - row, lambda tap: 2 * half - tap)
                target[slot[kind]] = m[: GROUP * ROWS].astype(bf16)
                slot[kind] += 1

    lateral_total = lateral_ref[0]
    for tap in range(1, lat_taps):
        lateral_total = lateral_total + lateral_ref[tap]
    k = lax.broadcasted_iota(jnp.int32, tl_ref.shape, 0)
    j = lax.broadcasted_iota(jnp.int32, tl_ref.shape, 1)
    place = k - LANES - j + lat_taps // 2
    forward = jnp.zeros(tl_ref.shape, f32)
    backward = jnp.zeros(tl_ref.shape, f32)
    for tap in range(lat_taps):
        forward = jnp.where(place == tap, lateral_ref[tap], forward)
        backward = jnp.where(place == lat_taps - 1 - tap, lateral_ref[tap], backward)
    scale = jnp.full((1, TILE), lateral_total, f32)
    tl_ref[...] = (forward / scale).astype(bf16)
    tm_ref[...] = (backward / scale).astype(bf16)


def bands(psf_bank, lateral_psf, band_index, planes, halo):
    plans = stages(planes, psf_bank.shape[1] // 2)
    spread = jnp.pad(band_index, (halo, halo + SPAN), constant_values=-1)
    first = lax.axis_index("cam") * planes
    length = planes + 2 * halo + SPAN
    mine = lax.dynamic_slice_in_dim(spread, first, length, 0)
    index = jnp.broadcast_to(mine[:, None], (length, ROWS)).reshape(1, length * ROWS)
    smem = pl.BlockSpec(memory_space=pltpu.SMEM)
    vmem = pl.BlockSpec(memory_space=pltpu.VMEM)
    counts = [
        sum(len(flat(stage)) for stage in plan[kind::2]) for plan in plans for kind in range(2)
    ]
    strip = jax.ShapeDtypeStruct((TILE + 2 * LANES, TILE), jnp.bfloat16)
    return pl.pallas_call(
        functools.partial(bands_kernel, psf_bank.shape[1], lateral_psf.shape[0], plans),
        in_specs=[smem, smem, vmem],
        out_specs=[vmem] * 6,
        out_shape=[
            jax.ShapeDtypeStruct((n, GROUP * ROWS, SPAN * ROWS), jnp.bfloat16) for n in counts
        ]
        + [strip, strip],
        compiler_params=pltpu.CompilerParams(vmem_limit_bytes=BANDS_VMEM),
        cost_estimate=pl.CostEstimate(
            flops=2_000_000_000, bytes_accessed=2_000_000, transcendentals=0
        ),
        name="bands",
    )(psf_bank, lateral_psf, index)


def restore_kernel(plan, inside, counts, merge, cut, *refs):
    parts = []
    for count in counts:
        parts.append(refs[:count])
        refs = refs[count:]
    g, gt, tl, tm = refs[:4]
    refs = refs[4:]
    f32 = jnp.float32
    bf16 = jnp.bfloat16
    half = plan[0][0][0][0] if not inside else plan[1][0][0][0] - plan[0][0][0][0]
    halo = 2 * ITERS * half
    if inside:
        out, q_out, e_out, mf, ef, mb, qb, pad, pad_back = refs
    else:
        q_in, e_in, middle = refs[:3]
        earlier = refs[3] if merge else None
        out, mf, ef, mb, qb, pad, pad_back = refs[3 + merge :]
    size, columns = mf.shape
    total = size // ROWS
    tiles = columns // TILE

    for buffer in (pad, pad_back):
        buffer[:, :LANES] = jnp.zeros((size, LANES), bf16)
        buffer[:, LANES + columns :] = jnp.zeros((size, LANES), bf16)

    at_column = 0
    for part in parts:
        width = part[0].shape[-1]
        at_row = halo * ROWS if inside else 0
        for ref in part:
            height = ref.shape[0] * ref.shape[1]
            for col in range(0, width, TILE):
                whole = ref[:, :, col : col + TILE].reshape(height, TILE)
                there = slice(at_column + col, at_column + col + TILE)
                mb[at_row : at_row + height, there] = whole
                mf[at_row : at_row + height, there] = whole.astype(f32)
            at_row += height
        at_column += width

    q_rows = slice((halo + half) * ROWS, (total - halo - half) * ROWS)
    e_width = half * (2 * ITERS - 2) * ROWS
    e_low = (halo + 2 * half) * ROWS
    e_high = (total - halo - 2 * half) * ROWS - e_width
    if not inside:
        qb[q_rows, :] = q_in[...]
        for number, start in enumerate((e_low, e_high)):
            e = e_in[number * e_width : (number + 1) * e_width, :]
            ef[start : start + e_width, :] = e
            mb[start : start + e_width, :] = e.astype(bf16)
        for lo in range(0, out.shape[-1] if not merge else 0, LANES):
            out[half * 4 : out.shape[0] - half * 4, :, lo : lo + LANES] = middle[:, :, lo : lo + LANES]

    def columns_of(tile):
        return slice(tile * TILE, (tile + 1) * TILE)

    def within(tile):
        return slice(LANES + tile * TILE, LANES + (tile + 1) * TILE)

    def around(tile):
        return slice(tile * TILE, (tile + 1) * TILE + 2 * LANES)

    def rows_of(groups):
        return slice(groups[0][0] * ROWS, (groups[-1][0] + groups[-1][1]) * ROWS)

    def axial(matrices, skip, stage, source, target, tile):
        for number, (first, count) in enumerate(flat(stage)):
            low = (first - half) * ROWS
            high = (first + count + half) * ROWS
            r = jnp.dot(
                matrices[skip + number, : count * ROWS, : high - low],
                source[low:high, columns_of(tile)],
                preferred_element_type=f32,
            )
            target[first * ROWS : (first + count) * ROWS, within(tile)] = r.astype(bf16)

    for sweep in range(ITERS):
        ahead, back = plan[2 * sweep], plan[2 * sweep + 1]
        skip_ahead = sum(len(flat(stage)) for stage in plan[0 : 2 * sweep : 2])
        skip_back = sum(len(flat(stage)) for stage in plan[1 : 2 * sweep : 2])
        final = sweep == ITERS - 1

        def ratio(tile):
            cols = columns_of(tile)
            for groups in ahead:
                rows = rows_of(groups)
                b = jnp.dot(pad[rows, around(tile)], tl[...], preferred_element_type=f32) + BACKGROUND
                guess = pl.reciprocal(b, approx=True)
                guess = guess * (2.0 - b * guess)
                qb[rows, cols] = (mf[rows, cols] * guess).astype(bf16)

        def update(tile):
            cols = columns_of(tile)
            for groups in back:
                rows = rows_of(groups)
                d = jnp.dot(pad_back[rows, around(tile)], tm[...], preferred_element_type=f32)
                e = (mf if sweep == 0 else ef)[rows, cols] * d
                if not final:
                    ef[rows, cols] = e
                    mb[rows, cols] = e.astype(bf16)
                    continue
                e = e.reshape(-1, ROWS, TILE).astype(bf16)
                first = groups[0][0] - plan[-1][0][0][0]
                start = (out.shape[-1] - columns if cut else 0) + tile * TILE
                drop = cut if tile == 0 else 0
                keep = min(TILE, out.shape[-1] - start)
                if keep > drop:
                    out[first : first + e.shape[0], :, start + drop : start + keep] = e[:, :, drop:keep]

        for step in range(tiles + 5):
            if step < tiles:
                axial(g, skip_ahead, ahead, mb, pad, step)
            if 0 <= step - 2 < tiles:
                ratio(step - 2)
            if 0 <= step - 3 < tiles:
                axial(gt, skip_back, back, qb, pad_back, step - 3)
            if 0 <= step - 5 < tiles:
                update(step - 5)

    if inside:
        q_out[...] = qb[q_rows, :]
        e_out[:e_width, :] = ef[e_low : e_low + e_width, :]
        e_out[e_width:, :] = ef[e_high : e_high + e_width, :]
    elif merge:
        kept = earlier.shape[-1]
        out[:, :, :kept] = earlier[...]
        out[half * 4 : out.shape[0] - half * 4, :, kept:] = middle[:, :, columns - (out.shape[-1] - kept) :]


def restore(parts, matrices, state, earlier, plan, inside, planes, half, columns):
    merge = earlier is not None
    operands, specs, width = [], [], 0
    for number, part in enumerate(parts):
        kept = 2 * LANES if number < len(parts) - 1 else part[0].shape[-1]
        for array in part:
            block = array.shape[:2] + (kept,)
            index = (0, 0, array.shape[-1] // kept - 1)
            operands.append(array)
            specs.append(pl.BlockSpec(block, lambda i, index=index: index))
        width += kept

    def whole(array):
        return pl.BlockSpec(array.shape, lambda i: (0,) * len(array.shape))

    for array in (*matrices, *state, *([earlier] if merge else [])):
        operands.append(array)
        specs.append(whole(array))
    halo = 2 * ITERS * half
    height = (planes + 2 * halo) * ROWS
    bf16 = jnp.bfloat16
    if inside:
        cut = 0
        results = [
            jax.ShapeDtypeStruct((planes - 2 * halo, ROWS, width), bf16),
            jax.ShapeDtypeStruct(((planes - 2 * half) * ROWS, width), bf16),
            jax.ShapeDtypeStruct((2 * half * (2 * ITERS - 2) * ROWS, width), jnp.float32),
        ]
    else:
        cut = LANES if merge else 0
        results = [jax.ShapeDtypeStruct((planes, ROWS, columns if merge else width - LANES), bf16)]
    return pl.pallas_call(
        functools.partial(restore_kernel, plan, inside, [len(part) for part in parts], merge, cut),
        grid=(1,),
        in_specs=specs,
        out_specs=[whole(result) for result in results],
        out_shape=results,
        scratch_shapes=[
            pltpu.VMEM((height, width), jnp.float32),
            pltpu.VMEM((height, width), jnp.float32),
            pltpu.VMEM((height, width), bf16),
            pltpu.VMEM((height, width), bf16),
            pltpu.VMEM((height, width + 2 * LANES), bf16),
            pltpu.VMEM((height, width + 2 * LANES), bf16),
        ],
        compiler_params=pltpu.CompilerParams(vmem_limit_bytes=RESTORE_VMEM),
        cost_estimate=pl.CostEstimate(
            flops=5_000_000_000, bytes_accessed=8_000_000, transcendentals=0
        ),
        name="inside" if inside else "ends",
    )(*operands)


def local(
    raw_frames,
    frame_order,
    dark_frame,
    flat_gain,
    stripe_band,
    shear_offset,
    shear_fraction,
    band_index,
    psf_bank,
    lateral_psf,
):
    half = psf_bank.shape[1] // 2
    planes = shear_offset.shape[0]
    columns = raw_frames.shape[-1]
    halo = 2 * ITERS * half
    inner, outer = stages(planes, half)
    count = lax.axis_size("cam")
    forward = [(i, i + 1) for i in range(count - 1)]
    backward = [(i + 1, i) for i in range(count - 1)]
    *axial, forward_lateral, backward_lateral = bands(psf_bank, lateral_psf, band_index, planes, halo)
    inner_matrices = (*axial[:2], forward_lateral, backward_lateral)
    outer_matrices = (*axial[2:], forward_lateral, backward_lateral)
    depth = halo // 2
    first_piece = frame_side(
        raw_frames, frame_order, dark_frame, flat_gain, stripe_band, shear_offset, shear_fraction, 0, SPLIT
    )
    first_piece, later_order = lax.optimization_barrier((first_piece, frame_order))
    second_piece = frame_side(
        raw_frames, later_order, dark_frame, flat_gain, stripe_band, shear_offset, shear_fraction,
        SPLIT, columns,
    )
    def exchange(piece):
        return lax.all_to_all(piece, "brick", split_axis=0, concat_axis=0, tiled=True)

    def with_halo(centre):
        low = lax.ppermute(centre[-depth:], "cam", forward)
        high = lax.ppermute(centre[:depth], "cam", backward)
        return low, centre, high

    def inside(centres):
        middle, quotients, estimates = restore(
            centres, inner_matrices, (), None, inner, True, planes, half, columns
        )
        return quotients, estimates, middle

    def ends(parts, state, earlier):
        return restore(
            parts, outer_matrices, state, earlier, outer, False, planes, half, columns
        )[0]

    first, second_piece, inner_matrices, outer_matrices = lax.optimization_barrier(
        (exchange(first_piece), second_piece, inner_matrices, outer_matrices)
    )
    first_part = with_halo(first)
    first_state = inside([(first,)])
    second, first_state = lax.optimization_barrier((exchange(second_piece), first_state))
    second_part = with_halo(second)
    second_state = inside([(first,), (second,)])
    result = ends([first_part], first_state, None)
    return ends([first_part, second_part], second_state, result)


def solution(mesh):
    placed = (
        P(("cam", "brick"), None, None),
        P(("cam", "brick"), None),
        P(),
        P(),
        P(),
        P("cam"),
        P("cam"),
        P(),
        P(),
        P(),
    )
    return jax.shard_map(
        local, mesh=mesh, in_specs=placed, out_specs=P("cam", "brick", None), check_vma=False
    )
```

```python
import functools

import jax
import jax.numpy as jnp
from jax import lax
from jax.experimental import pallas as pl
from jax.experimental.pallas import tpu as pltpu
from jax.sharding import PartitionSpec as P

SHEAR = 512
ITERS = 2
BACKGROUND = 1.0

LANES = 128
TILE = 256
ROWS = 8
BLOCK_ROWS = 64
LEAD = SHEAR // LANES + 1
SPLIT = 1024
VMEM = 60 * 1024 * 1024
BANDS_VMEM = 20 * 1024 * 1024
RESTORE_VMEM = 42 * 1024 * 1024
GROUP = 20
SPAN = 32


def frame_kernel(
    first, count,
    order_ref, offset_ref, fraction_ref,
    raw_prev, raw_main, raw_next,
    dark_prev, dark_main, dark_next,
    gain_prev, gain_main, gain_next,
    band_ref, out_ref, scratch, level,
):
    step = pl.program_id(0)
    steps = pl.num_programs(0)
    rows = BLOCK_ROWS + 16
    brick = lax.axis_index("brick")
    f32 = jnp.float32
    bf16 = jnp.bfloat16
    base = first - LEAD

    @pl.when(step == 0)
    def _():
        if base < 0:
            scratch[:, :, : -base * LANES] = jnp.zeros((2, BLOCK_ROWS, -base * LANES), f32)

    has_prev = (step > 0).astype(f32)
    has_next = (step < steps - 1).astype(f32)
    frames = [jnp.where(order_ref[0, 0] == place, 0, 1) for place in range(2)]

    used = range(max(base, 0), first + count)
    for tile in used:
        cols = pl.ds(tile * LANES, LANES)
        for part, keep, start in ((0, slice(8, 16), 0), (1, slice(None), 8), (2, slice(0, 8), rows - 8)):
            dark = (dark_prev, dark_main, dark_next)[part][:, cols].astype(f32)[keep]
            gain = (gain_prev, gain_main, gain_next)[part][:, cols].astype(f32)[keep]
            if part != 1:
                gain = gain * (has_prev, None, has_next)[part]
            raw = (raw_prev, raw_main, raw_next)[part]
            for place in range(2):
                f = (raw[frames[place], :, cols].astype(f32)[keep] - dark) * gain
                level[place, tile - used[0], start : start + f.shape[0], :] = f

    zero = jnp.minimum(step, 0)
    taps = band_ref.shape[0]
    for tile in used:
        band = band_ref[:, pl.ds(tile * LANES, LANES)]
        for place in range(2):
            here = tile - used[0]
            out = level[place, here, 8 : 8 + BLOCK_ROWS, :] * (1.0 + band[taps // 2 : taps // 2 + 1])
            for tap in range(taps):
                if tap != taps // 2:
                    shifted = level[place, here, pl.ds(zero + 8 + tap - taps // 2, BLOCK_ROWS), :]
                    out = out + band[tap : tap + 1] * shifted
            scratch[place, :, pl.ds((tile - base) * LANES, LANES)] = out.astype(bf16).astype(f32)

    lane = lax.broadcasted_iota(jnp.int32, (BLOCK_ROWS, LANES), 1)
    bricks = BLOCK_ROWS // ROWS
    for place in range(2):
        amount = offset_ref[brick * 2 + place]
        weight = fraction_ref[brick * 2 + place]
        whole = amount // LANES
        part = amount % LANES
        near_mask = lane < part
        far_mask = lane < part + 1

        def turned(tile):
            start = (tile - base - whole) * LANES
            x = scratch[place, :, pl.ds(pl.multiple_of(start, LANES), LANES)]
            return (1.0 - weight) * pltpu.roll(x, part, 1), weight * pltpu.roll(x, (part + 1) % LANES, 1)

        last = turned(first - 1)
        for tile in range(first, first + count):
            now = turned(tile)
            mixed = jnp.where(near_mask, last[0], now[0]) + jnp.where(far_mask, last[1], now[1])
            last = now
            out_ref[:, place * ROWS : (place + 1) * ROWS, pl.ds((tile - first) * LANES, LANES)] = (
                mixed.reshape(bricks, ROWS, LANES).astype(bf16)
            )


def frame_side(raw, order, dark, gain, band, offset, fraction, lo, hi):
    _, frame_rows, columns = raw.shape
    steps = frame_rows // BLOCK_ROWS
    bricks = frame_rows // ROWS
    per = BLOCK_ROWS // 16
    last = frame_rows // 16 - 1
    smem = pl.BlockSpec(memory_space=pltpu.SMEM)
    first, count = lo // LANES, (hi - lo) // LANES

    def three(lead):
        zeros = (0,) * len(lead)
        return [
            pl.BlockSpec(lead + (16, columns), lambda i: zeros + (jnp.maximum(per * i - 1, 0), 0)),
            pl.BlockSpec(lead + (BLOCK_ROWS, columns), lambda i: zeros + (i, 0)),
            pl.BlockSpec(lead + (16, columns), lambda i: zeros + (jnp.minimum(per * i + per, last), 0)),
        ]

    return pl.pallas_call(
        functools.partial(frame_kernel, first, count),
        grid=(steps,),
        in_specs=[smem, smem, smem]
        + three((2,)) + three(()) + three(())
        + [pl.BlockSpec(band.shape, lambda i: (0, 0))],
        out_specs=pl.BlockSpec((BLOCK_ROWS // ROWS, 2 * ROWS, hi - lo), lambda i: (i, 0, 0)),
        out_shape=jax.ShapeDtypeStruct((bricks, 2 * ROWS, hi - lo), jnp.bfloat16),
        scratch_shapes=[
            pltpu.VMEM((2, BLOCK_ROWS, (LEAD + count) * LANES), jnp.float32),
            pltpu.VMEM((2, min(first, LEAD) + count, BLOCK_ROWS + 16, LANES), jnp.float32),
        ],
        compiler_params=pltpu.CompilerParams(vmem_limit_bytes=VMEM),
        cost_estimate=pl.CostEstimate(
            flops=8_000_000_000, bytes_accessed=6_500_000, transcendentals=0
        ),
        name="frame_side",
    )(order, offset, fraction, raw, raw, raw, dark, dark, dark, gain, gain, gain, band)


def stages(planes, half):
    halo = 2 * ITERS * half
    total = planes + 2 * halo

    def cut(lo, hi, most):
        parts = -(-(hi - lo) // most)
        size = -(-(hi - lo) // (2 * parts)) * 2
        return [(at, min(size, hi - at)) for at in range(lo, hi, size)]

    inner, outer = [], []
    for stage in range(1, 2 * ITERS + 1):
        reach = stage * half
        lo, hi = halo + reach, total - halo - reach
        inner.append([cut(lo, hi, GROUP)])
        outer.append([cut(reach, lo, GROUP), cut(hi, total - reach, GROUP)])
    return inner, outer


def flat(stage):
    return [group for groups in stage for group in groups]


def bands_kernel(taps, lat_taps, plans, psf_ref, lateral_ref, index_ref, *outs):
    matrices, (tl_ref, tm_ref) = outs[:-2], outs[-2:]
    f32 = jnp.float32
    bf16 = jnp.bfloat16
    half = taps // 2
    width = SPAN * ROWS
    index = index_ref[...]
    raw = []
    for tap in range(taps):
        value = jnp.zeros(index.shape, f32)
        for kernel in range(psf_ref.shape[0]):
            value = jnp.where(index == kernel, psf_ref[kernel, tap], value)
        raw.append(value)
    total = functools.reduce(lambda a, b: a + b, raw)
    total = jnp.where(total > 0.0, total, 1.0)
    unit = [value / total for value in raw]
    row = lax.broadcasted_iota(jnp.int32, (width, width), 0)
    col = lax.broadcasted_iota(jnp.int32, (width, width), 1)

    def banded(start, gap, order):
        m = jnp.zeros((width, width), f32)
        for tap in range(taps):
            values = unit[tap][:, start * ROWS : start * ROWS + width]
            m = jnp.where(gap == ROWS * order(tap), values, m)
        return m

    for which, plan in enumerate(plans):
        slot = [0, 0]
        for number, stage in enumerate(plan):
            kind = number % 2
            target = matrices[2 * which + kind]
            for at, _ in flat(stage):
                if kind == 0:
                    m = banded(at, row - col, lambda tap: tap).T
                else:
                    m = banded(at - half, col - row, lambda tap: 2 * half - tap)
                target[slot[kind]] = m[: GROUP * ROWS].astype(bf16)
                slot[kind] += 1

    lateral_total = lateral_ref[0]
    for tap in range(1, lat_taps):
        lateral_total = lateral_total + lateral_ref[tap]
    k = lax.broadcasted_iota(jnp.int32, tl_ref.shape, 0)
    j = lax.broadcasted_iota(jnp.int32, tl_ref.shape, 1)
    place = k - LANES - j + lat_taps // 2
    forward = jnp.zeros(tl_ref.shape, f32)
    backward = jnp.zeros(tl_ref.shape, f32)
    for tap in range(lat_taps):
        forward = jnp.where(place == tap, lateral_ref[tap], forward)
        backward = jnp.where(place == lat_taps - 1 - tap, lateral_ref[tap], backward)
    scale = jnp.full((1, TILE), lateral_total, f32)
    tl_ref[...] = (forward / scale).astype(bf16)
    tm_ref[...] = (backward / scale).astype(bf16)


def bands(psf_bank, lateral_psf, band_index, planes, halo):
    plans = stages(planes, psf_bank.shape[1] // 2)
    spread = jnp.pad(band_index, (halo, halo + SPAN), constant_values=-1)
    first = lax.axis_index("cam") * planes
    length = planes + 2 * halo + SPAN
    mine = lax.dynamic_slice_in_dim(spread, first, length, 0)
    index = jnp.broadcast_to(mine[:, None], (length, ROWS)).reshape(1, length * ROWS)
    smem = pl.BlockSpec(memory_space=pltpu.SMEM)
    vmem = pl.BlockSpec(memory_space=pltpu.VMEM)
    counts = [
        sum(len(flat(stage)) for stage in plan[kind::2]) for plan in plans for kind in range(2)
    ]
    strip = jax.ShapeDtypeStruct((TILE + 2 * LANES, TILE), jnp.bfloat16)
    return pl.pallas_call(
        functools.partial(bands_kernel, psf_bank.shape[1], lateral_psf.shape[0], plans),
        in_specs=[smem, smem, vmem],
        out_specs=[vmem] * 6,
        out_shape=[
            jax.ShapeDtypeStruct((n, GROUP * ROWS, SPAN * ROWS), jnp.bfloat16) for n in counts
        ]
        + [strip, strip],
        compiler_params=pltpu.CompilerParams(vmem_limit_bytes=BANDS_VMEM),
        cost_estimate=pl.CostEstimate(
            flops=2_000_000_000, bytes_accessed=2_000_000, transcendentals=0
        ),
        name="bands",
    )(psf_bank, lateral_psf, index)


def restore_kernel(plan, inside, counts, merge, cut, *refs):
    parts = []
    for count in counts:
        parts.append(refs[:count])
        refs = refs[count:]
    g, gt, tl, tm = refs[:4]
    refs = refs[4:]
    f32 = jnp.float32
    bf16 = jnp.bfloat16
    half = plan[0][0][0][0] if not inside else plan[1][0][0][0] - plan[0][0][0][0]
    halo = 2 * ITERS * half
    if inside:
        out, q_out, e_out, mf, ef, mb, qb, pad, pad_back = refs
    else:
        q_in, e_in, middle = refs[:3]
        earlier = refs[3] if merge else None
        out, mf, ef, mb, qb, pad, pad_back = refs[3 + merge :]
    size, columns = mf.shape
    total = size // ROWS
    tiles = columns // TILE

    for buffer in (pad, pad_back):
        buffer[:, :LANES] = jnp.zeros((size, LANES), bf16)
        buffer[:, LANES + columns :] = jnp.zeros((size, LANES), bf16)

    at_column = 0
    for part in parts:
        width = part[0].shape[-1]
        at_row = halo * ROWS if inside else 0
        for ref in part:
            height = ref.shape[0] * ref.shape[1]
            for col in range(0, width, TILE):
                whole = ref[:, :, col : col + TILE].reshape(height, TILE)
                there = slice(at_column + col, at_column + col + TILE)
                mb[at_row : at_row + height, there] = whole
                mf[at_row : at_row + height, there] = whole.astype(f32)
            at_row += height
        at_column += width

    q_rows = slice((halo + half) * ROWS, (total - halo - half) * ROWS)
    e_width = half * (2 * ITERS - 2) * ROWS
    e_low = (halo + 2 * half) * ROWS
    e_high = (total - halo - 2 * half) * ROWS - e_width
    if not inside:
        qb[q_rows, :] = q_in[...]
        for number, start in enumerate((e_low, e_high)):
            e = e_in[number * e_width : (number + 1) * e_width, :]
            ef[start : start + e_width, :] = e
            mb[start : start + e_width, :] = e.astype(bf16)
        for lo in range(0, out.shape[-1] if not merge else 0, LANES):
            out[half * 4 : out.shape[0] - half * 4, :, lo : lo + LANES] = middle[:, :, lo : lo + LANES]

    def columns_of(tile):
        return slice(tile * TILE, (tile + 1) * TILE)

    def within(tile):
        return slice(LANES + tile * TILE, LANES + (tile + 1) * TILE)

    def around(tile):
        return slice(tile * TILE, (tile + 1) * TILE + 2 * LANES)

    def rows_of(groups):
        return slice(groups[0][0] * ROWS, (groups[-1][0] + groups[-1][1]) * ROWS)

    def axial(matrices, skip, stage, source, target, tile):
        for number, (first, count) in enumerate(flat(stage)):
            low = (first - half) * ROWS
            high = (first + count + half) * ROWS
            r = jnp.dot(
                matrices[skip + number, : count * ROWS, : high - low],
                source[low:high, columns_of(tile)],
                preferred_element_type=f32,
            )
            target[first * ROWS : (first + count) * ROWS, within(tile)] = r.astype(bf16)

    for sweep in range(ITERS):
        ahead, back = plan[2 * sweep], plan[2 * sweep + 1]
        skip_ahead = sum(len(flat(stage)) for stage in plan[0 : 2 * sweep : 2])
        skip_back = sum(len(flat(stage)) for stage in plan[1 : 2 * sweep : 2])
        final = sweep == ITERS - 1

        def ratio(tile):
            cols = columns_of(tile)
            for groups in ahead:
                rows = rows_of(groups)
                b = jnp.dot(pad[rows, around(tile)], tl[...], preferred_element_type=f32) + BACKGROUND
                guess = pl.reciprocal(b, approx=True)
                guess = guess * (2.0 - b * guess)
                qb[rows, cols] = (mf[rows, cols] * guess).astype(bf16)

        def update(tile):
            cols = columns_of(tile)
            for groups in back:
                rows = rows_of(groups)
                d = jnp.dot(pad_back[rows, around(tile)], tm[...], preferred_element_type=f32)
                e = (mf if sweep == 0 else ef)[rows, cols] * d
                if not final:
                    ef[rows, cols] = e
                    mb[rows, cols] = e.astype(bf16)
                    continue
                e = e.reshape(-1, ROWS, TILE).astype(bf16)
                first = groups[0][0] - plan[-1][0][0][0]
                start = (out.shape[-1] - columns if cut else 0) + tile * TILE
                drop = cut if tile == 0 else 0
                keep = min(TILE, out.shape[-1] - start)
                if keep > drop:
                    out[first : first + e.shape[0], :, start + drop : start + keep] = e[:, :, drop:keep]

        for step in range(tiles + 5):
            if step < tiles:
                axial(g, skip_ahead, ahead, mb, pad, step)
            if 0 <= step - 2 < tiles:
                ratio(step - 2)
            if 0 <= step - 3 < tiles:
                axial(gt, skip_back, back, qb, pad_back, step - 3)
            if 0 <= step - 5 < tiles:
                update(step - 5)

    if inside:
        q_out[...] = qb[q_rows, :]
        e_out[:e_width, :] = ef[e_low : e_low + e_width, :]
        e_out[e_width:, :] = ef[e_high : e_high + e_width, :]
    elif merge:
        kept = earlier.shape[-1]
        out[:, :, :kept] = earlier[...]
        out[half * 4 : out.shape[0] - half * 4, :, kept:] = middle[:, :, columns - (out.shape[-1] - kept) :]


def restore(parts, matrices, state, earlier, plan, inside, planes, half, columns):
    merge = earlier is not None
    operands, specs, width = [], [], 0
    for number, part in enumerate(parts):
        kept = 2 * LANES if number < len(parts) - 1 else part[0].shape[-1]
        for array in part:
            block = array.shape[:2] + (kept,)
            index = (0, 0, array.shape[-1] // kept - 1)
            operands.append(array)
            specs.append(pl.BlockSpec(block, lambda i, index=index: index))
        width += kept

    def whole(array):
        return pl.BlockSpec(array.shape, lambda i: (0,) * len(array.shape))

    for array in (*matrices, *state, *([earlier] if merge else [])):
        operands.append(array)
        specs.append(whole(array))
    halo = 2 * ITERS * half
    height = (planes + 2 * halo) * ROWS
    bf16 = jnp.bfloat16
    if inside:
        cut = 0
        results = [
            jax.ShapeDtypeStruct((planes - 2 * halo, ROWS, width), bf16),
            jax.ShapeDtypeStruct(((planes - 2 * half) * ROWS, width), bf16),
            jax.ShapeDtypeStruct((2 * half * (2 * ITERS - 2) * ROWS, width), jnp.float32),
        ]
    else:
        cut = LANES if merge else 0
        results = [jax.ShapeDtypeStruct((planes, ROWS, columns if merge else width - LANES), bf16)]
    return pl.pallas_call(
        functools.partial(restore_kernel, plan, inside, [len(part) for part in parts], merge, cut),
        grid=(1,),
        in_specs=specs,
        out_specs=[whole(result) for result in results],
        out_shape=results,
        scratch_shapes=[
            pltpu.VMEM((height, width), jnp.float32),
            pltpu.VMEM((height, width), jnp.float32),
            pltpu.VMEM((height, width), bf16),
            pltpu.VMEM((height, width), bf16),
            pltpu.VMEM((height, width + 2 * LANES), bf16),
            pltpu.VMEM((height, width + 2 * LANES), bf16),
        ],
        compiler_params=pltpu.CompilerParams(vmem_limit_bytes=RESTORE_VMEM),
        cost_estimate=pl.CostEstimate(
            flops=5_000_000_000, bytes_accessed=8_000_000, transcendentals=0
        ),
        name="inside" if inside else "ends",
    )(*operands)


def local(
    raw_frames,
    frame_order,
    dark_frame,
    flat_gain,
    stripe_band,
    shear_offset,
    shear_fraction,
    band_index,
    psf_bank,
    lateral_psf,
):
    half = psf_bank.shape[1] // 2
    planes = shear_offset.shape[0]
    columns = raw_frames.shape[-1]
    halo = 2 * ITERS * half
    inner, outer = stages(planes, half)
    count = lax.axis_size("cam")
    forward = [(i, i + 1) for i in range(count - 1)]
    backward = [(i + 1, i) for i in range(count - 1)]
    *axial, forward_lateral, backward_lateral = bands(psf_bank, lateral_psf, band_index, planes, halo)
    inner_matrices = (*axial[:2], forward_lateral, backward_lateral)
    outer_matrices = (*axial[2:], forward_lateral, backward_lateral)
    depth = halo // 2
    first_piece = frame_side(
        raw_frames, frame_order, dark_frame, flat_gain, stripe_band, shear_offset, shear_fraction, 0, SPLIT
    )
    first_piece, later_order = lax.optimization_barrier((first_piece, frame_order))
    second_piece = frame_side(
        raw_frames, later_order, dark_frame, flat_gain, stripe_band, shear_offset, shear_fraction,
        SPLIT, columns,
    )
    def exchange(piece):
        return lax.all_to_all(piece, "brick", split_axis=0, concat_axis=0, tiled=True)

    def with_halo(centre):
        low = lax.ppermute(centre[-depth:], "cam", forward)
        high = lax.ppermute(centre[:depth], "cam", backward)
        return low, centre, high

    def inside(centres):
        middle, quotients, estimates = restore(
            centres, inner_matrices, (), None, inner, True, planes, half, columns
        )
        return quotients, estimates, middle

    def ends(parts, state, earlier):
        return restore(
            parts, outer_matrices, state, earlier, outer, False, planes, half, columns
        )[0]

    first, second_piece, inner_matrices, outer_matrices = lax.optimization_barrier(
        (exchange(first_piece), second_piece, inner_matrices, outer_matrices)
    )
    first_part = with_halo(first)
    first_state = inside([(first,)])
    second, first_state = lax.optimization_barrier((exchange(second_piece), first_state))
    second_part = with_halo(second)
    second_state = inside([(first,), (second,)])
    result = ends([first_part], first_state, None)
    return ends([first_part, second_part], second_state, result)


def solution(mesh):
    placed = (
        P(("cam", "brick"), None, None),
        P(("cam", "brick"), None),
        P(),
        P(),
        P(),
        P("cam"),
        P("cam"),
        P(),
        P(),
        P(),
    )
    return jax.shard_map(
        local, mesh=mesh, in_specs=placed, out_specs=P("cam", "brick", None), check_vma=False
    )
```

```python
import functools

import jax
import jax.numpy as jnp
from jax import lax
from jax.experimental import pallas as pl
from jax.experimental.pallas import tpu as pltpu
from jax.sharding import PartitionSpec as P

SHEAR = 512
ITERS = 2
BACKGROUND = 1.0

LANES = 128
TILE = 256
ROWS = 8
BLOCK_ROWS = 64
LEAD = SHEAR // LANES + 1
SPLIT = 1024
VMEM = 60 * 1024 * 1024
BANDS_VMEM = 20 * 1024 * 1024
RESTORE_VMEM = 30 * 1024 * 1024
LATER_VMEM = 20 * 1024 * 1024
GROUP = 20
SPAN = 32


def frame_kernel(
    first, count,
    order_ref, offset_ref, fraction_ref,
    raw_prev, raw_main, raw_next,
    dark_prev, dark_main, dark_next,
    gain_prev, gain_main, gain_next,
    band_ref, out_ref, scratch, level,
):
    step = pl.program_id(0)
    steps = pl.num_programs(0)
    rows = BLOCK_ROWS + 16
    brick = lax.axis_index("brick")
    f32 = jnp.float32
    bf16 = jnp.bfloat16
    base = first - LEAD

    @pl.when(step == 0)
    def _():
        if base < 0:
            scratch[:, :, : -base * LANES] = jnp.zeros((2, BLOCK_ROWS, -base * LANES), f32)

    has_prev = (step > 0).astype(f32)
    has_next = (step < steps - 1).astype(f32)
    frames = [jnp.where(order_ref[0, 0] == place, 0, 1) for place in range(2)]

    used = range(max(base, 0), first + count)
    for tile in used:
        cols = pl.ds(tile * LANES, LANES)
        for part, keep, start in ((0, slice(8, 16), 0), (1, slice(None), 8), (2, slice(0, 8), rows - 8)):
            dark = (dark_prev, dark_main, dark_next)[part][:, cols].astype(f32)[keep]
            gain = (gain_prev, gain_main, gain_next)[part][:, cols].astype(f32)[keep]
            if part != 1:
                gain = gain * (has_prev, None, has_next)[part]
            raw = (raw_prev, raw_main, raw_next)[part]
            for place in range(2):
                f = (raw[frames[place], :, cols].astype(f32)[keep] - dark) * gain
                level[place, tile - used[0], start : start + f.shape[0], :] = f

    zero = jnp.minimum(step, 0)
    taps = band_ref.shape[0]
    for tile in used:
        band = band_ref[:, pl.ds(tile * LANES, LANES)]
        for place in range(2):
            here = tile - used[0]
            out = level[place, here, 8 : 8 + BLOCK_ROWS, :] * (1.0 + band[taps // 2 : taps // 2 + 1])
            for tap in range(taps):
                if tap != taps // 2:
                    shifted = level[place, here, pl.ds(zero + 8 + tap - taps // 2, BLOCK_ROWS), :]
                    out = out + band[tap : tap + 1] * shifted
            scratch[place, :, pl.ds((tile - base) * LANES, LANES)] = out.astype(bf16).astype(f32)

    lane = lax.broadcasted_iota(jnp.int32, (BLOCK_ROWS, LANES), 1)
    bricks = BLOCK_ROWS // ROWS
    for place in range(2):
        amount = offset_ref[brick * 2 + place]
        weight = fraction_ref[brick * 2 + place]
        whole = amount // LANES
        part = amount % LANES
        near_mask = lane < part
        far_mask = lane < part + 1

        def turned(tile):
            start = (tile - base - whole) * LANES
            x = scratch[place, :, pl.ds(pl.multiple_of(start, LANES), LANES)]
            return (1.0 - weight) * pltpu.roll(x, part, 1), weight * pltpu.roll(x, (part + 1) % LANES, 1)

        last = turned(first - 1)
        for tile in range(first, first + count):
            now = turned(tile)
            mixed = jnp.where(near_mask, last[0], now[0]) + jnp.where(far_mask, last[1], now[1])
            last = now
            out_ref[:, place * ROWS : (place + 1) * ROWS, pl.ds((tile - first) * LANES, LANES)] = (
                mixed.reshape(bricks, ROWS, LANES).astype(bf16)
            )


def frame_side(raw, order, dark, gain, band, offset, fraction, lo, hi):
    _, frame_rows, columns = raw.shape
    steps = frame_rows // BLOCK_ROWS
    bricks = frame_rows // ROWS
    per = BLOCK_ROWS // 16
    last = frame_rows // 16 - 1
    smem = pl.BlockSpec(memory_space=pltpu.SMEM)
    first, count = lo // LANES, (hi - lo) // LANES
    if lo == 0:
        columns = hi

    def three(lead):
        zeros = (0,) * len(lead)
        return [
            pl.BlockSpec(lead + (16, columns), lambda i: zeros + (jnp.maximum(per * i - 1, 0), 0)),
            pl.BlockSpec(lead + (BLOCK_ROWS, columns), lambda i: zeros + (i, 0)),
            pl.BlockSpec(lead + (16, columns), lambda i: zeros + (jnp.minimum(per * i + per, last), 0)),
        ]

    return pl.pallas_call(
        functools.partial(frame_kernel, first, count),
        grid=(steps,),
        in_specs=[smem, smem, smem]
        + three((2,)) + three(()) + three(())
        + [pl.BlockSpec((band.shape[0], columns), lambda i: (0, 0))],
        out_specs=pl.BlockSpec((BLOCK_ROWS // ROWS, 2 * ROWS, hi - lo), lambda i: (i, 0, 0)),
        out_shape=jax.ShapeDtypeStruct((bricks, 2 * ROWS, hi - lo), jnp.bfloat16),
        scratch_shapes=[
            pltpu.VMEM((2, BLOCK_ROWS, (LEAD + count) * LANES), jnp.float32),
            pltpu.VMEM((2, min(first, LEAD) + count, BLOCK_ROWS + 16, LANES), jnp.float32),
        ],
        compiler_params=pltpu.CompilerParams(vmem_limit_bytes=VMEM if lo == 0 else LATER_VMEM),
        cost_estimate=pl.CostEstimate(
            flops=8_000_000_000, bytes_accessed=6_500_000, transcendentals=0
        ),
        name="frame_side",
    )(order, offset, fraction, raw, raw, raw, dark, dark, dark, gain, gain, gain, band)


def stages(planes, half):
    halo = 2 * ITERS * half
    total = planes + 2 * halo

    def cut(lo, hi, most):
        parts = -(-(hi - lo) // most)
        size = -(-(hi - lo) // (2 * parts)) * 2
        return [(at, min(size, hi - at)) for at in range(lo, hi, size)]

    inner, outer = [], []
    for stage in range(1, 2 * ITERS + 1):
        reach = stage * half
        lo, hi = halo + reach, total - halo - reach
        inner.append([cut(lo, hi, GROUP)])
        outer.append([cut(reach, lo, GROUP), cut(hi, total - reach, GROUP)])
    return inner, outer


def flat(stage):
    return [group for groups in stage for group in groups]


def bands_kernel(taps, lat_taps, plans, psf_ref, lateral_ref, index_ref, *outs):
    matrices, (tl_ref, tm_ref) = outs[:-2], outs[-2:]
    f32 = jnp.float32
    bf16 = jnp.bfloat16
    half = taps // 2
    width = SPAN * ROWS
    index = index_ref[...]
    raw = []
    for tap in range(taps):
        value = jnp.zeros(index.shape, f32)
        for kernel in range(psf_ref.shape[0]):
            value = jnp.where(index == kernel, psf_ref[kernel, tap], value)
        raw.append(value)
    total = functools.reduce(lambda a, b: a + b, raw)
    total = jnp.where(total > 0.0, total, 1.0)
    unit = [value / total for value in raw]
    row = lax.broadcasted_iota(jnp.int32, (width, width), 0)
    col = lax.broadcasted_iota(jnp.int32, (width, width), 1)

    def banded(start, gap, order):
        m = jnp.zeros((width, width), f32)
        for tap in range(taps):
            values = unit[tap][:, start * ROWS : start * ROWS + width]
            m = jnp.where(gap == ROWS * order(tap), values, m)
        return m

    for which, plan in enumerate(plans):
        slot = [0, 0]
        for number, stage in enumerate(plan):
            kind = number % 2
            target = matrices[2 * which + kind]
            for at, _ in flat(stage):
                if kind == 0:
                    m = banded(at, row - col, lambda tap: tap).T
                else:
                    m = banded(at - half, col - row, lambda tap: 2 * half - tap)
                target[slot[kind]] = m[: GROUP * ROWS].astype(bf16)
                slot[kind] += 1

    lateral_total = lateral_ref[0]
    for tap in range(1, lat_taps):
        lateral_total = lateral_total + lateral_ref[tap]
    k = lax.broadcasted_iota(jnp.int32, tl_ref.shape, 0)
    j = lax.broadcasted_iota(jnp.int32, tl_ref.shape, 1)
    place = k - LANES - j + lat_taps // 2
    forward = jnp.zeros(tl_ref.shape, f32)
    backward = jnp.zeros(tl_ref.shape, f32)
    for tap in range(lat_taps):
        forward = jnp.where(place == tap, lateral_ref[tap], forward)
        backward = jnp.where(place == lat_taps - 1 - tap, lateral_ref[tap], backward)
    scale = jnp.full((1, TILE), lateral_total, f32)
    tl_ref[...] = (forward / scale).astype(bf16)
    tm_ref[...] = (backward / scale).astype(bf16)


def bands(psf_bank, lateral_psf, band_index, planes, halo):
    plans = stages(planes, psf_bank.shape[1] // 2)
    spread = jnp.pad(band_index, (halo, halo + SPAN), constant_values=-1)
    first = lax.axis_index("cam") * planes
    length = planes + 2 * halo + SPAN
    mine = lax.dynamic_slice_in_dim(spread, first, length, 0)
    index = jnp.broadcast_to(mine[:, None], (length, ROWS)).reshape(1, length * ROWS)
    smem = pl.BlockSpec(memory_space=pltpu.SMEM)
    vmem = pl.BlockSpec(memory_space=pltpu.VMEM)
    counts = [
        sum(len(flat(stage)) for stage in plan[kind::2]) for plan in plans for kind in range(2)
    ]
    strip = jax.ShapeDtypeStruct((TILE + 2 * LANES, TILE), jnp.bfloat16)
    return pl.pallas_call(
        functools.partial(bands_kernel, psf_bank.shape[1], lateral_psf.shape[0], plans),
        in_specs=[smem, smem, vmem],
        out_specs=[vmem] * 6,
        out_shape=[
            jax.ShapeDtypeStruct((n, GROUP * ROWS, SPAN * ROWS), jnp.bfloat16) for n in counts
        ]
        + [strip, strip],
        compiler_params=pltpu.CompilerParams(vmem_limit_bytes=BANDS_VMEM),
        cost_estimate=pl.CostEstimate(
            flops=2_000_000_000, bytes_accessed=2_000_000, transcendentals=0
        ),
        name="bands",
    )(psf_bank, lateral_psf, index)


def restore_kernel(plan, inside, counts, cut, *refs):
    parts = []
    for count in counts:
        parts.append(refs[:count])
        refs = refs[count:]
    g, gt, tl, tm = refs[:4]
    refs = refs[4:]
    f32 = jnp.float32
    bf16 = jnp.bfloat16
    half = plan[0][0][0][0] if not inside else plan[1][0][0][0] - plan[0][0][0][0]
    halo = 2 * ITERS * half
    if not inside:
        q_in, e_in = refs[:2]
        refs = refs[2:]
    buffers = refs[-8:]
    mf, ef, mb, qb, pad, pad_back, done, sems = buffers
    if inside:
        canvas, q_out, e_out = refs[-11:-8]
    else:
        canvas = refs[-9]
    size, columns = mf.shape
    total = size // ROWS
    tiles = columns // TILE

    for buffer in (pad, pad_back):
        buffer[:, :LANES] = jnp.zeros((size, LANES), bf16)
        buffer[:, LANES + columns :] = jnp.zeros((size, LANES), bf16)

    at_column = 0
    for part in parts:
        width = part[0].shape[-1] if part is parts[-1] else 2 * LANES
        skip = part[0].shape[-1] - width
        at_row = halo * ROWS if inside else 0
        for ref in part:
            height = ref.shape[0] * ref.shape[1]
            for col in range(0, width, TILE):
                whole = ref[:, :, skip + col : skip + col + TILE].reshape(height, TILE)
                there = slice(at_column + col, at_column + col + TILE)
                mb[at_row : at_row + height, there] = whole
                mf[at_row : at_row + height, there] = whole.astype(f32)
            at_row += height
        at_column += width

    q_rows = slice((halo + half) * ROWS, (total - halo - half) * ROWS)
    e_width = half * (2 * ITERS - 2) * ROWS
    e_low = (halo + 2 * half) * ROWS
    e_high = (total - halo - 2 * half) * ROWS - e_width
    if not inside:
        qb[q_rows, :] = q_in[...]
        for number, start in enumerate((e_low, e_high)):
            e = e_in[number * e_width : (number + 1) * e_width, :]
            ef[start : start + e_width, :] = e
            mb[start : start + e_width, :] = e.astype(bf16)

    copies = []
    base = canvas.shape[-1] - columns if cut else 0
    limit = canvas.shape[-1] if cut else columns - LANES
    top = ITERS * 2 * half

    def columns_of(tile):
        return slice(tile * TILE, (tile + 1) * TILE)

    def within(tile):
        return slice(LANES + tile * TILE, LANES + (tile + 1) * TILE)

    def around(tile):
        return slice(tile * TILE, (tile + 1) * TILE + 2 * LANES)

    def rows_of(groups):
        return slice(groups[0][0] * ROWS, (groups[-1][0] + groups[-1][1]) * ROWS)

    def axial(matrices, skip, stage, source, target, tile):
        for number, (first, count) in enumerate(flat(stage)):
            low = (first - half) * ROWS
            high = (first + count + half) * ROWS
            r = jnp.dot(
                matrices[skip + number, : count * ROWS, : high - low],
                source[low:high, columns_of(tile)],
                preferred_element_type=f32,
            )
            target[first * ROWS : (first + count) * ROWS, within(tile)] = r.astype(bf16)

    for sweep in range(ITERS):
        ahead, back = plan[2 * sweep], plan[2 * sweep + 1]
        skip_ahead = sum(len(flat(stage)) for stage in plan[0 : 2 * sweep : 2])
        skip_back = sum(len(flat(stage)) for stage in plan[1 : 2 * sweep : 2])
        final = sweep == ITERS - 1

        def ratio(tile):
            cols = columns_of(tile)
            for groups in ahead:
                rows = rows_of(groups)
                b = jnp.dot(pad[rows, around(tile)], tl[...], preferred_element_type=f32) + BACKGROUND
                guess = pl.reciprocal(b, approx=True)
                guess = guess * (2.0 - b * guess)
                qb[rows, cols] = (mf[rows, cols] * guess).astype(bf16)

        def update(tile):
            cols = columns_of(tile)
            for groups in back:
                rows = rows_of(groups)
                d = jnp.dot(pad_back[rows, around(tile)], tm[...], preferred_element_type=f32)
                e = (mf if sweep == 0 else ef)[rows, cols] * d
                if not final:
                    ef[rows, cols] = e
                    mb[rows, cols] = e.astype(bf16)
                    continue
                start = base + tile * TILE
                drop = cut if tile == 0 else 0
                keep = min(TILE, limit - start)
                if keep > drop:
                    first, count = groups[0][0] - top, e.shape[0] // ROWS
                    where = (slice(first, first + count), slice(None))
                    here = slice(tile * TILE + drop, tile * TILE + keep)
                    done[where + (here,)] = e.reshape(-1, ROWS, TILE)[:, :, drop:keep].astype(bf16)
                    copy = pltpu.make_async_copy(
                        done.at[where + (here,)],
                        canvas.at[where + (slice(start + drop, start + keep),)],
                        sems.at[len(copies)],
                    )
                    copy.start()
                    copies.append(copy)

        for step in range(tiles + 5):
            if step < tiles:
                axial(g, skip_ahead, ahead, mb, pad, step)
            if 0 <= step - 2 < tiles:
                ratio(step - 2)
            if 0 <= step - 3 < tiles:
                axial(gt, skip_back, back, qb, pad_back, step - 3)
            if 0 <= step - 5 < tiles:
                update(step - 5)

    if inside:
        q_out[...] = qb[q_rows, :]
        e_out[:e_width, :] = ef[e_low : e_low + e_width, :]
        e_out[e_width:, :] = ef[e_high : e_high + e_width, :]
    for copy in copies:
        copy.wait()


def restore(parts, matrices, state, canvas, plan, inside, planes, half, columns):
    later = len(parts) > 1
    width = parts[-1][0].shape[-1] + (2 * LANES if later else 0)
    halo = 2 * ITERS * half
    height = (planes + 2 * halo) * ROWS
    bf16 = jnp.bfloat16
    vmem = pl.BlockSpec(memory_space=pltpu.VMEM)
    hbm = pl.BlockSpec(memory_space=pltpu.HBM)
    operands = [array for part in parts for array in part] + [*matrices, *state]
    specs = [vmem] * len(operands)
    aliases = {}
    if canvas is not None:
        aliases = {len(operands): 0}
        operands.append(canvas)
        specs.append(hbm)
    results = [jax.ShapeDtypeStruct((planes, ROWS, columns), bf16)]
    if inside:
        results += [
            jax.ShapeDtypeStruct(((planes - 2 * half) * ROWS, width), bf16),
            jax.ShapeDtypeStruct((2 * half * (2 * ITERS - 2) * ROWS, width), jnp.float32),
        ]
    return pl.pallas_call(
        functools.partial(
            restore_kernel, plan, inside, [len(part) for part in parts], LANES if later else 0
        ),
        in_specs=specs,
        out_specs=[hbm] + [vmem] * (len(results) - 1),
        out_shape=results,
        input_output_aliases=aliases,
        scratch_shapes=[
            pltpu.VMEM((height, width), jnp.float32),
            pltpu.VMEM((height, width), jnp.float32),
            pltpu.VMEM((height, width), bf16),
            pltpu.VMEM((height, width), bf16),
            pltpu.VMEM((height, width + 2 * LANES), bf16),
            pltpu.VMEM((height, width + 2 * LANES), bf16),
            pltpu.VMEM((planes, ROWS, width), bf16),
            pltpu.SemaphoreType.DMA((2 * (width // TILE),)),
        ],
        compiler_params=pltpu.CompilerParams(vmem_limit_bytes=RESTORE_VMEM),
        cost_estimate=pl.CostEstimate(
            flops=5_000_000_000, bytes_accessed=8_000_000, transcendentals=0
        ),
        name="inside" if inside else "ends",
    )(*operands)


def local(
    raw_frames,
    frame_order,
    dark_frame,
    flat_gain,
    stripe_band,
    shear_offset,
    shear_fraction,
    band_index,
    psf_bank,
    lateral_psf,
):
    half = psf_bank.shape[1] // 2
    planes = shear_offset.shape[0]
    columns = raw_frames.shape[-1]
    halo = 2 * ITERS * half
    inner, outer = stages(planes, half)
    count = lax.axis_size("cam")
    forward = [(i, i + 1) for i in range(count - 1)]
    backward = [(i + 1, i) for i in range(count - 1)]
    *axial, forward_lateral, backward_lateral = bands(psf_bank, lateral_psf, band_index, planes, halo)
    inner_matrices = (*axial[:2], forward_lateral, backward_lateral)
    outer_matrices = (*axial[2:], forward_lateral, backward_lateral)
    depth = halo // 2
    first_piece = frame_side(
        raw_frames, frame_order, dark_frame, flat_gain, stripe_band, shear_offset, shear_fraction, 0, SPLIT
    )
    first_piece, later_order = lax.optimization_barrier((first_piece, frame_order))
    second_piece = frame_side(
        raw_frames, later_order, dark_frame, flat_gain, stripe_band, shear_offset, shear_fraction,
        SPLIT, columns,
    )
    def exchange(piece):
        return lax.all_to_all(piece, "brick", split_axis=0, concat_axis=0, tiled=True)

    def with_halo(centre):
        low = lax.ppermute(centre[-depth:], "cam", forward)
        high = lax.ppermute(centre[:depth], "cam", backward)
        return low, centre, high

    def inside(centres, canvas):
        canvas, *state = restore(
            centres, inner_matrices, (), canvas, inner, True, planes, half, columns
        )
        return canvas, state

    def ends(parts, state, canvas):
        return restore(parts, outer_matrices, state, canvas, outer, False, planes, half, columns)[0]

    first, second_piece, inner_matrices, outer_matrices = lax.optimization_barrier(
        (exchange(first_piece), second_piece, inner_matrices, outer_matrices)
    )
    first_part = with_halo(first)
    canvas, first_state = inside([(first,)], None)
    second, first_state = lax.optimization_barrier((exchange(second_piece), first_state))
    second_part = with_halo(second)
    canvas, second_state = inside([(first,), (second,)], canvas)
    canvas = ends([first_part], first_state, canvas)
    return ends([first_part, second_part], second_state, canvas)


def solution(mesh):
    placed = (
        P(("cam", "brick"), None, None),
        P(("cam", "brick"), None),
        P(),
        P(),
        P(),
        P("cam"),
        P("cam"),
        P(),
        P(),
        P(),
    )
    return jax.shard_map(
        local, mesh=mesh, in_specs=placed, out_specs=P("cam", "brick", None), check_vma=False
    )
```

```python
import functools

import jax
import jax.numpy as jnp
from jax import lax
from jax.experimental import pallas as pl
from jax.experimental.pallas import tpu as pltpu
from jax.sharding import PartitionSpec as P

SHEAR = 512
ITERS = 2
BACKGROUND = 1.0

LANES = 128
TILE = 256
ROWS = 8
BLOCK_ROWS = 64
LEAD = SHEAR // LANES + 1
CUTS = (1024, 1792)
VMEM = 60 * 1024 * 1024
BANDS_VMEM = 20 * 1024 * 1024
RESTORE_VMEM = 30 * 1024 * 1024
LATER_VMEM = 20 * 1024 * 1024
GROUP = 20
SPAN = 32


def frame_kernel(
    first, count,
    order_ref, offset_ref, fraction_ref,
    raw_prev, raw_main, raw_next,
    dark_prev, dark_main, dark_next,
    gain_prev, gain_main, gain_next,
    band_ref, out_ref, scratch, level,
):
    step = pl.program_id(0)
    steps = pl.num_programs(0)
    rows = BLOCK_ROWS + 16
    brick = lax.axis_index("brick")
    f32 = jnp.float32
    bf16 = jnp.bfloat16
    base = first - LEAD

    @pl.when(step == 0)
    def _():
        if base < 0:
            scratch[:, :, : -base * LANES] = jnp.zeros((2, BLOCK_ROWS, -base * LANES), f32)

    has_prev = (step > 0).astype(f32)
    has_next = (step < steps - 1).astype(f32)
    frames = [jnp.where(order_ref[0, 0] == place, 0, 1) for place in range(2)]

    used = range(max(base, 0), first + count)
    for tile in used:
        cols = pl.ds(tile * LANES, LANES)
        for part, keep, start in ((0, slice(8, 16), 0), (1, slice(None), 8), (2, slice(0, 8), rows - 8)):
            dark = (dark_prev, dark_main, dark_next)[part][:, cols].astype(f32)[keep]
            gain = (gain_prev, gain_main, gain_next)[part][:, cols].astype(f32)[keep]
            if part != 1:
                gain = gain * (has_prev, None, has_next)[part]
            raw = (raw_prev, raw_main, raw_next)[part]
            for place in range(2):
                f = (raw[frames[place], :, cols].astype(f32)[keep] - dark) * gain
                level[place, tile - used[0], start : start + f.shape[0], :] = f

    zero = jnp.minimum(step, 0)
    taps = band_ref.shape[0]
    for tile in used:
        band = band_ref[:, pl.ds(tile * LANES, LANES)]
        for place in range(2):
            here = tile - used[0]
            out = level[place, here, 8 : 8 + BLOCK_ROWS, :] * (1.0 + band[taps // 2 : taps // 2 + 1])
            for tap in range(taps):
                if tap != taps // 2:
                    shifted = level[place, here, pl.ds(zero + 8 + tap - taps // 2, BLOCK_ROWS), :]
                    out = out + band[tap : tap + 1] * shifted
            scratch[place, :, pl.ds((tile - base) * LANES, LANES)] = out.astype(bf16).astype(f32)

    lane = lax.broadcasted_iota(jnp.int32, (BLOCK_ROWS, LANES), 1)
    bricks = BLOCK_ROWS // ROWS
    for place in range(2):
        amount = offset_ref[brick * 2 + place]
        weight = fraction_ref[brick * 2 + place]
        whole = amount // LANES
        part = amount % LANES
        near_mask = lane < part
        far_mask = lane < part + 1

        def turned(tile):
            start = (tile - base - whole) * LANES
            x = scratch[place, :, pl.ds(pl.multiple_of(start, LANES), LANES)]
            return (1.0 - weight) * pltpu.roll(x, part, 1), weight * pltpu.roll(x, (part + 1) % LANES, 1)

        last = turned(first - 1)
        for tile in range(first, first + count):
            now = turned(tile)
            mixed = jnp.where(near_mask, last[0], now[0]) + jnp.where(far_mask, last[1], now[1])
            last = now
            out_ref[:, place * ROWS : (place + 1) * ROWS, pl.ds((tile - first) * LANES, LANES)] = (
                mixed.reshape(bricks, ROWS, LANES).astype(bf16)
            )


def frame_side(raw, order, dark, gain, band, offset, fraction, lo, hi):
    _, frame_rows, columns = raw.shape
    steps = frame_rows // BLOCK_ROWS
    bricks = frame_rows // ROWS
    per = BLOCK_ROWS // 16
    last = frame_rows // 16 - 1
    smem = pl.BlockSpec(memory_space=pltpu.SMEM)
    first, count = lo // LANES, (hi - lo) // LANES
    if lo == 0:
        columns = hi

    def three(lead):
        zeros = (0,) * len(lead)
        return [
            pl.BlockSpec(lead + (16, columns), lambda i: zeros + (jnp.maximum(per * i - 1, 0), 0)),
            pl.BlockSpec(lead + (BLOCK_ROWS, columns), lambda i: zeros + (i, 0)),
            pl.BlockSpec(lead + (16, columns), lambda i: zeros + (jnp.minimum(per * i + per, last), 0)),
        ]

    return pl.pallas_call(
        functools.partial(frame_kernel, first, count),
        grid=(steps,),
        in_specs=[smem, smem, smem]
        + three((2,)) + three(()) + three(())
        + [pl.BlockSpec((band.shape[0], columns), lambda i: (0, 0))],
        out_specs=pl.BlockSpec((BLOCK_ROWS // ROWS, 2 * ROWS, hi - lo), lambda i: (i, 0, 0)),
        out_shape=jax.ShapeDtypeStruct((bricks, 2 * ROWS, hi - lo), jnp.bfloat16),
        scratch_shapes=[
            pltpu.VMEM((2, BLOCK_ROWS, (LEAD + count) * LANES), jnp.float32),
            pltpu.VMEM((2, min(first, LEAD) + count, BLOCK_ROWS + 16, LANES), jnp.float32),
        ],
        compiler_params=pltpu.CompilerParams(vmem_limit_bytes=VMEM if lo == 0 else LATER_VMEM),
        cost_estimate=pl.CostEstimate(
            flops=8_000_000_000, bytes_accessed=6_500_000, transcendentals=0
        ),
        name="frame_side",
    )(order, offset, fraction, raw, raw, raw, dark, dark, dark, gain, gain, gain, band)


def stages(planes, half):
    halo = 2 * ITERS * half
    total = planes + 2 * halo

    def cut(lo, hi, most):
        parts = -(-(hi - lo) // most)
        size = -(-(hi - lo) // (2 * parts)) * 2
        return [(at, min(size, hi - at)) for at in range(lo, hi, size)]

    inner, outer = [], []
    for stage in range(1, 2 * ITERS + 1):
        reach = stage * half
        lo, hi = halo + reach, total - halo - reach
        inner.append([cut(lo, hi, GROUP)])
        outer.append([cut(reach, lo, GROUP), cut(hi, total - reach, GROUP)])
    return inner, outer


def flat(stage):
    return [group for groups in stage for group in groups]


def bands_kernel(taps, lat_taps, plans, psf_ref, lateral_ref, index_ref, *outs):
    matrices, (tl_ref, tm_ref) = outs[:-2], outs[-2:]
    f32 = jnp.float32
    bf16 = jnp.bfloat16
    half = taps // 2
    width = SPAN * ROWS
    index = index_ref[...]
    raw = []
    for tap in range(taps):
        value = jnp.zeros(index.shape, f32)
        for kernel in range(psf_ref.shape[0]):
            value = jnp.where(index == kernel, psf_ref[kernel, tap], value)
        raw.append(value)
    total = functools.reduce(lambda a, b: a + b, raw)
    total = jnp.where(total > 0.0, total, 1.0)
    unit = [value / total for value in raw]
    row = lax.broadcasted_iota(jnp.int32, (width, width), 0)
    col = lax.broadcasted_iota(jnp.int32, (width, width), 1)

    def banded(start, gap, order):
        m = jnp.zeros((width, width), f32)
        for tap in range(taps):
            values = unit[tap][:, start * ROWS : start * ROWS + width]
            m = jnp.where(gap == ROWS * order(tap), values, m)
        return m

    for which, plan in enumerate(plans):
        slot = [0, 0]
        for number, stage in enumerate(plan):
            kind = number % 2
            target = matrices[2 * which + kind]
            for at, _ in flat(stage):
                if kind == 0:
                    m = banded(at, row - col, lambda tap: tap).T
                else:
                    m = banded(at - half, col - row, lambda tap: 2 * half - tap)
                target[slot[kind]] = m[: GROUP * ROWS].astype(bf16)
                slot[kind] += 1

    lateral_total = lateral_ref[0]
    for tap in range(1, lat_taps):
        lateral_total = lateral_total + lateral_ref[tap]
    k = lax.broadcasted_iota(jnp.int32, tl_ref.shape, 0)
    j = lax.broadcasted_iota(jnp.int32, tl_ref.shape, 1)
    place = k - LANES - j + lat_taps // 2
    forward = jnp.zeros(tl_ref.shape, f32)
    backward = jnp.zeros(tl_ref.shape, f32)
    for tap in range(lat_taps):
        forward = jnp.where(place == tap, lateral_ref[tap], forward)
        backward = jnp.where(place == lat_taps - 1 - tap, lateral_ref[tap], backward)
    scale = jnp.full((1, TILE), lateral_total, f32)
    tl_ref[...] = (forward / scale).astype(bf16)
    tm_ref[...] = (backward / scale).astype(bf16)


def bands(psf_bank, lateral_psf, band_index, planes, halo):
    plans = stages(planes, psf_bank.shape[1] // 2)
    spread = jnp.pad(band_index, (halo, halo + SPAN), constant_values=-1)
    first = lax.axis_index("cam") * planes
    length = planes + 2 * halo + SPAN
    mine = lax.dynamic_slice_in_dim(spread, first, length, 0)
    index = jnp.broadcast_to(mine[:, None], (length, ROWS)).reshape(1, length * ROWS)
    smem = pl.BlockSpec(memory_space=pltpu.SMEM)
    vmem = pl.BlockSpec(memory_space=pltpu.VMEM)
    counts = [
        sum(len(flat(stage)) for stage in plan[kind::2]) for plan in plans for kind in range(2)
    ]
    strip = jax.ShapeDtypeStruct((TILE + 2 * LANES, TILE), jnp.bfloat16)
    return pl.pallas_call(
        functools.partial(bands_kernel, psf_bank.shape[1], lateral_psf.shape[0], plans),
        in_specs=[smem, smem, vmem],
        out_specs=[vmem] * 6,
        out_shape=[
            jax.ShapeDtypeStruct((n, GROUP * ROWS, SPAN * ROWS), jnp.bfloat16) for n in counts
        ]
        + [strip, strip],
        compiler_params=pltpu.CompilerParams(vmem_limit_bytes=BANDS_VMEM),
        cost_estimate=pl.CostEstimate(
            flops=2_000_000_000, bytes_accessed=2_000_000, transcendentals=0
        ),
        name="bands",
    )(psf_bank, lateral_psf, index)


def restore_kernel(plan, inside, counts, base, cut, limit, *refs):
    parts = []
    for count in counts:
        parts.append(refs[:count])
        refs = refs[count:]
    g, gt, tl, tm = refs[:4]
    refs = refs[4:]
    f32 = jnp.float32
    bf16 = jnp.bfloat16
    half = plan[0][0][0][0] if not inside else plan[1][0][0][0] - plan[0][0][0][0]
    halo = 2 * ITERS * half
    if not inside:
        q_in, e_in = refs[:2]
        refs = refs[2:]
    buffers = refs[-8:]
    mf, ef, mb, qb, pad, pad_back, done, sems = buffers
    if inside:
        canvas, q_out, e_out = refs[-11:-8]
    else:
        canvas = refs[-9]
    size, columns = mf.shape
    total = size // ROWS
    tiles = columns // TILE

    for buffer in (pad, pad_back):
        buffer[:, :LANES] = jnp.zeros((size, LANES), bf16)
        buffer[:, LANES + columns :] = jnp.zeros((size, LANES), bf16)

    at_column = 0
    for part in parts:
        width = part[0].shape[-1] if part is parts[-1] else 2 * LANES
        skip = part[0].shape[-1] - width
        at_row = halo * ROWS if inside else 0
        for ref in part:
            height = ref.shape[0] * ref.shape[1]
            for col in range(0, width, TILE):
                whole = ref[:, :, skip + col : skip + col + TILE].reshape(height, TILE)
                there = slice(at_column + col, at_column + col + TILE)
                mb[at_row : at_row + height, there] = whole
                mf[at_row : at_row + height, there] = whole.astype(f32)
            at_row += height
        at_column += width

    q_rows = slice((halo + half) * ROWS, (total - halo - half) * ROWS)
    e_width = half * (2 * ITERS - 2) * ROWS
    e_low = (halo + 2 * half) * ROWS
    e_high = (total - halo - 2 * half) * ROWS - e_width
    if not inside:
        qb[q_rows, :] = q_in[...]
        for number, start in enumerate((e_low, e_high)):
            e = e_in[number * e_width : (number + 1) * e_width, :]
            ef[start : start + e_width, :] = e
            mb[start : start + e_width, :] = e.astype(bf16)

    copies = []
    top = ITERS * 2 * half

    def columns_of(tile):
        return slice(tile * TILE, (tile + 1) * TILE)

    def within(tile):
        return slice(LANES + tile * TILE, LANES + (tile + 1) * TILE)

    def around(tile):
        return slice(tile * TILE, (tile + 1) * TILE + 2 * LANES)

    def rows_of(groups):
        return slice(groups[0][0] * ROWS, (groups[-1][0] + groups[-1][1]) * ROWS)

    def axial(matrices, skip, stage, source, target, tile):
        for number, (first, count) in enumerate(flat(stage)):
            low = (first - half) * ROWS
            high = (first + count + half) * ROWS
            r = jnp.dot(
                matrices[skip + number, : count * ROWS, : high - low],
                source[low:high, columns_of(tile)],
                preferred_element_type=f32,
            )
            target[first * ROWS : (first + count) * ROWS, within(tile)] = r.astype(bf16)

    for sweep in range(ITERS):
        ahead, back = plan[2 * sweep], plan[2 * sweep + 1]
        skip_ahead = sum(len(flat(stage)) for stage in plan[0 : 2 * sweep : 2])
        skip_back = sum(len(flat(stage)) for stage in plan[1 : 2 * sweep : 2])
        final = sweep == ITERS - 1

        def ratio(tile):
            cols = columns_of(tile)
            for groups in ahead:
                rows = rows_of(groups)
                b = jnp.dot(pad[rows, around(tile)], tl[...], preferred_element_type=f32) + BACKGROUND
                guess = pl.reciprocal(b, approx=True)
                guess = guess * (2.0 - b * guess)
                qb[rows, cols] = (mf[rows, cols] * guess).astype(bf16)

        def update(tile):
            cols = columns_of(tile)
            for groups in back:
                rows = rows_of(groups)
                d = jnp.dot(pad_back[rows, around(tile)], tm[...], preferred_element_type=f32)
                e = (mf if sweep == 0 else ef)[rows, cols] * d
                if not final:
                    ef[rows, cols] = e
                    mb[rows, cols] = e.astype(bf16)
                    continue
                start = base + tile * TILE
                drop = cut if tile == 0 else 0
                keep = min(TILE, limit - start)
                if keep > drop:
                    first, count = groups[0][0] - top, e.shape[0] // ROWS
                    where = (slice(first, first + count), slice(None))
                    here = slice(tile * TILE + drop, tile * TILE + keep)
                    done[where + (here,)] = e.reshape(-1, ROWS, TILE)[:, :, drop:keep].astype(bf16)
                    copy = pltpu.make_async_copy(
                        done.at[where + (here,)],
                        canvas.at[where + (slice(start + drop, start + keep),)],
                        sems.at[len(copies)],
                    )
                    copy.start()
                    copies.append(copy)

        for step in range(tiles + 5):
            if step < tiles:
                axial(g, skip_ahead, ahead, mb, pad, step)
            if 0 <= step - 2 < tiles:
                ratio(step - 2)
            if 0 <= step - 3 < tiles:
                axial(gt, skip_back, back, qb, pad_back, step - 3)
            if 0 <= step - 5 < tiles:
                update(step - 5)

    if inside:
        q_out[...] = qb[q_rows, :]
        e_out[:e_width, :] = ef[e_low : e_low + e_width, :]
        e_out[e_width:, :] = ef[e_high : e_high + e_width, :]
    for copy in copies:
        copy.wait()


def restore(parts, matrices, state, canvas, plan, inside, planes, half, columns, hi):
    later = len(parts) > 1
    width = parts[-1][0].shape[-1] + (2 * LANES if later else 0)
    halo = 2 * ITERS * half
    height = (planes + 2 * halo) * ROWS
    bf16 = jnp.bfloat16
    vmem = pl.BlockSpec(memory_space=pltpu.VMEM)
    hbm = pl.BlockSpec(memory_space=pltpu.HBM)
    operands = [array for part in parts for array in part] + [*matrices, *state]
    specs = [vmem] * len(operands)
    aliases = {}
    if canvas is not None:
        aliases = {len(operands): 0}
        operands.append(canvas)
        specs.append(hbm)
    results = [jax.ShapeDtypeStruct((planes, ROWS, columns), bf16)]
    if inside:
        results += [
            jax.ShapeDtypeStruct(((planes - 2 * half) * ROWS, width), bf16),
            jax.ShapeDtypeStruct((2 * half * (2 * ITERS - 2) * ROWS, width), jnp.float32),
        ]
    return pl.pallas_call(
        functools.partial(
            restore_kernel, plan, inside, [len(part) for part in parts],
            hi - width, LANES if later else 0, hi if hi == columns else hi - LANES,
        ),
        in_specs=specs,
        out_specs=[hbm] + [vmem] * (len(results) - 1),
        out_shape=results,
        input_output_aliases=aliases,
        scratch_shapes=[
            pltpu.VMEM((height, width), jnp.float32),
            pltpu.VMEM((height, width), jnp.float32),
            pltpu.VMEM((height, width), bf16),
            pltpu.VMEM((height, width), bf16),
            pltpu.VMEM((height, width + 2 * LANES), bf16),
            pltpu.VMEM((height, width + 2 * LANES), bf16),
            pltpu.VMEM((planes, ROWS, width), bf16),
            pltpu.SemaphoreType.DMA((2 * (width // TILE),)),
        ],
        compiler_params=pltpu.CompilerParams(vmem_limit_bytes=RESTORE_VMEM),
        cost_estimate=pl.CostEstimate(
            flops=5_000_000_000, bytes_accessed=8_000_000, transcendentals=0
        ),
        name="inside" if inside else "ends",
    )(*operands)


def local(
    raw_frames,
    frame_order,
    dark_frame,
    flat_gain,
    stripe_band,
    shear_offset,
    shear_fraction,
    band_index,
    psf_bank,
    lateral_psf,
):
    half = psf_bank.shape[1] // 2
    planes = shear_offset.shape[0]
    columns = raw_frames.shape[-1]
    halo = 2 * ITERS * half
    inner, outer = stages(planes, half)
    count = lax.axis_size("cam")
    forward = [(i, i + 1) for i in range(count - 1)]
    backward = [(i + 1, i) for i in range(count - 1)]
    *axial, forward_lateral, backward_lateral = bands(psf_bank, lateral_psf, band_index, planes, halo)
    inner_matrices = (*axial[:2], forward_lateral, backward_lateral)
    outer_matrices = (*axial[2:], forward_lateral, backward_lateral)
    depth = halo // 2
    edges = (0, *CUTS, columns)
    pieces = []
    order = frame_order
    for lo, hi in zip(edges[:-1], edges[1:]):
        piece = frame_side(
            raw_frames, order, dark_frame, flat_gain, stripe_band, shear_offset, shear_fraction, lo, hi
        )
        piece, order = lax.optimization_barrier((piece, order))
        pieces.append(piece)

    def exchange(piece):
        return lax.all_to_all(piece, "brick", split_axis=0, concat_axis=0, tiled=True)

    def with_halo(centre):
        low = lax.ppermute(centre[-depth:], "cam", forward)
        high = lax.ppermute(centre[:depth], "cam", backward)
        return low, centre, high

    def inside(centres, canvas, hi):
        canvas, *state = restore(
            centres, inner_matrices, (), canvas, inner, True, planes, half, columns, hi
        )
        return canvas, state

    def ends(parts, state, canvas, hi):
        return restore(
            parts, outer_matrices, state, canvas, outer, False, planes, half, columns, hi
        )[0]

    parts, states, canvas = [], [], None
    inner_matrices, outer_matrices = tuple(inner_matrices), tuple(outer_matrices)
    for number, hi in enumerate(edges[1:]):
        centre = exchange(pieces[number])
        following = pieces[number + 1 : number + 2]
        if number == 0:
            centre, following, inner_matrices, outer_matrices = lax.optimization_barrier(
                (centre, following, inner_matrices, outer_matrices)
            )
        else:
            centre, following, states[-1] = lax.optimization_barrier((centre, following, states[-1]))
        pieces[number + 1 : number + 2] = following
        parts.append(with_halo(centre))
        centres = [(part[1],) for part in parts[-2:]]
        if number > 1:
            canvas = ends(parts[:-1][-3:-1], states[-2], canvas, edges[number - 1])
        canvas, state = inside(centres, canvas, hi)
        states.append(state)
    last = len(parts) - 1
    canvas = ends(parts[-3:-1], states[-2], canvas, edges[last])
    return ends(parts[-2:], states[-1], canvas, columns)


def solution(mesh):
    placed = (
        P(("cam", "brick"), None, None),
        P(("cam", "brick"), None),
        P(),
        P(),
        P(),
        P("cam"),
        P("cam"),
        P(),
        P(),
        P(),
    )
    return jax.shard_map(
        local, mesh=mesh, in_specs=placed, out_specs=P("cam", "brick", None), check_vma=False
    )
```

```python
import functools

import jax
import jax.numpy as jnp
from jax import lax
from jax.experimental import pallas as pl
from jax.experimental.pallas import tpu as pltpu
from jax.sharding import PartitionSpec as P

SHEAR = 512
ITERS = 2
BACKGROUND = 1.0

LANES = 128
TILE = 256
ROWS = 8
BLOCK_ROWS = 64
LEAD = SHEAR // LANES + 1
SPLIT = 1152
VMEM = 60 * 1024 * 1024
BANDS_VMEM = 20 * 1024 * 1024
RESTORE_VMEM = 30 * 1024 * 1024
LATER_VMEM = 20 * 1024 * 1024
GROUP = 20
SPAN = 32


def frame_kernel(
    first, count,
    order_ref, offset_ref, fraction_ref,
    raw_prev, raw_main, raw_next,
    dark_prev, dark_main, dark_next,
    gain_prev, gain_main, gain_next,
    band_ref, out_ref, scratch, level,
):
    step = pl.program_id(0)
    steps = pl.num_programs(0)
    rows = BLOCK_ROWS + 16
    brick = lax.axis_index("brick")
    f32 = jnp.float32
    bf16 = jnp.bfloat16
    base = first - LEAD

    @pl.when(step == 0)
    def _():
        if base < 0:
            scratch[:, :, : -base * LANES] = jnp.zeros((2, BLOCK_ROWS, -base * LANES), f32)

    has_prev = (step > 0).astype(f32)
    has_next = (step < steps - 1).astype(f32)
    frames = [jnp.where(order_ref[0, 0] == place, 0, 1) for place in range(2)]

    used = range(max(base, 0), first + count)
    for tile in used:
        cols = pl.ds(tile * LANES, LANES)
        for part, keep, start in ((0, slice(8, 16), 0), (1, slice(None), 8), (2, slice(0, 8), rows - 8)):
            dark = (dark_prev, dark_main, dark_next)[part][:, cols].astype(f32)[keep]
            gain = (gain_prev, gain_main, gain_next)[part][:, cols].astype(f32)[keep]
            if part != 1:
                gain = gain * (has_prev, None, has_next)[part]
            raw = (raw_prev, raw_main, raw_next)[part]
            for place in range(2):
                f = (raw[frames[place], :, cols].astype(f32)[keep] - dark) * gain
                level[place, tile - used[0], start : start + f.shape[0], :] = f

    zero = jnp.minimum(step, 0)
    taps = band_ref.shape[0]
    for tile in used:
        band = band_ref[:, pl.ds(tile * LANES, LANES)]
        for place in range(2):
            here = tile - used[0]
            out = level[place, here, 8 : 8 + BLOCK_ROWS, :] * (1.0 + band[taps // 2 : taps // 2 + 1])
            for tap in range(taps):
                if tap != taps // 2:
                    shifted = level[place, here, pl.ds(zero + 8 + tap - taps // 2, BLOCK_ROWS), :]
                    out = out + band[tap : tap + 1] * shifted
            scratch[place, :, pl.ds((tile - base) * LANES, LANES)] = out.astype(bf16).astype(f32)

    lane = lax.broadcasted_iota(jnp.int32, (BLOCK_ROWS, LANES), 1)
    bricks = BLOCK_ROWS // ROWS
    for place in range(2):
        amount = offset_ref[brick * 2 + place]
        weight = fraction_ref[brick * 2 + place]
        whole = amount // LANES
        part = amount % LANES
        near_mask = lane < part
        far_mask = lane < part + 1

        def turned(tile):
            start = (tile - base - whole) * LANES
            x = scratch[place, :, pl.ds(pl.multiple_of(start, LANES), LANES)]
            return (1.0 - weight) * pltpu.roll(x, part, 1), weight * pltpu.roll(x, (part + 1) % LANES, 1)

        last = turned(first - 1)
        for tile in range(first, first + count):
            now = turned(tile)
            mixed = jnp.where(near_mask, last[0], now[0]) + jnp.where(far_mask, last[1], now[1])
            last = now
            out_ref[:, place * ROWS : (place + 1) * ROWS, pl.ds((tile - first) * LANES, LANES)] = (
                mixed.reshape(bricks, ROWS, LANES).astype(bf16)
            )


def frame_side(raw, order, dark, gain, band, offset, fraction, lo, hi):
    _, frame_rows, columns = raw.shape
    steps = frame_rows // BLOCK_ROWS
    bricks = frame_rows // ROWS
    per = BLOCK_ROWS // 16
    last = frame_rows // 16 - 1
    smem = pl.BlockSpec(memory_space=pltpu.SMEM)
    first, count = lo // LANES, (hi - lo) // LANES
    if lo == 0:
        columns = hi

    def three(lead):
        zeros = (0,) * len(lead)
        return [
            pl.BlockSpec(lead + (16, columns), lambda i: zeros + (jnp.maximum(per * i - 1, 0), 0)),
            pl.BlockSpec(lead + (BLOCK_ROWS, columns), lambda i: zeros + (i, 0)),
            pl.BlockSpec(lead + (16, columns), lambda i: zeros + (jnp.minimum(per * i + per, last), 0)),
        ]

    return pl.pallas_call(
        functools.partial(frame_kernel, first, count),
        grid=(steps,),
        in_specs=[smem, smem, smem]
        + three((2,)) + three(()) + three(())
        + [pl.BlockSpec((band.shape[0], columns), lambda i: (0, 0))],
        out_specs=pl.BlockSpec((BLOCK_ROWS // ROWS, 2 * ROWS, hi - lo), lambda i: (i, 0, 0)),
        out_shape=jax.ShapeDtypeStruct((bricks, 2 * ROWS, hi - lo), jnp.bfloat16),
        scratch_shapes=[
            pltpu.VMEM((2, BLOCK_ROWS, (LEAD + count) * LANES), jnp.float32),
            pltpu.VMEM((2, min(first, LEAD) + count, BLOCK_ROWS + 16, LANES), jnp.float32),
        ],
        compiler_params=pltpu.CompilerParams(vmem_limit_bytes=VMEM if lo == 0 else LATER_VMEM),
        cost_estimate=pl.CostEstimate(
            flops=8_000_000_000, bytes_accessed=6_500_000, transcendentals=0
        ),
        name="frame_side",
    )(order, offset, fraction, raw, raw, raw, dark, dark, dark, gain, gain, gain, band)


def stages(planes, half):
    halo = 2 * ITERS * half
    total = planes + 2 * halo

    def cut(lo, hi, most):
        parts = -(-(hi - lo) // most)
        size = -(-(hi - lo) // (2 * parts)) * 2
        return [(at, min(size, hi - at)) for at in range(lo, hi, size)]

    inner, below, above = [], [], []
    for stage in range(1, 2 * ITERS + 1):
        reach = stage * half
        lo, hi = halo + reach, total - halo - reach
        inner.append([cut(lo, hi, GROUP)])
        below.append([cut(reach, lo, GROUP)])
        above.append([cut(hi, total - reach, GROUP)])
    return inner, below, above


def flat(stage):
    return [group for groups in stage for group in groups]


def bands_kernel(taps, lat_taps, plans, psf_ref, lateral_ref, index_ref, *outs):
    matrices, (tl_ref, tm_ref) = outs[:-2], outs[-2:]
    f32 = jnp.float32
    bf16 = jnp.bfloat16
    half = taps // 2
    width = SPAN * ROWS
    index = index_ref[...]
    raw = []
    for tap in range(taps):
        value = jnp.zeros(index.shape, f32)
        for kernel in range(psf_ref.shape[0]):
            value = jnp.where(index == kernel, psf_ref[kernel, tap], value)
        raw.append(value)
    total = functools.reduce(lambda a, b: a + b, raw)
    total = jnp.where(total > 0.0, total, 1.0)
    unit = [value / total for value in raw]
    row = lax.broadcasted_iota(jnp.int32, (width, width), 0)
    col = lax.broadcasted_iota(jnp.int32, (width, width), 1)

    def banded(start, gap, order):
        m = jnp.zeros((width, width), f32)
        for tap in range(taps):
            values = unit[tap][:, start * ROWS : start * ROWS + width]
            m = jnp.where(gap == ROWS * order(tap), values, m)
        return m

    for which, plan in enumerate(plans):
        slot = [0, 0]
        for number, stage in enumerate(plan):
            kind = number % 2
            target = matrices[2 * which + kind]
            for at, _ in flat(stage):
                if kind == 0:
                    m = banded(at, row - col, lambda tap: tap).T
                else:
                    m = banded(at - half, col - row, lambda tap: 2 * half - tap)
                target[slot[kind]] = m[: GROUP * ROWS].astype(bf16)
                slot[kind] += 1

    lateral_total = lateral_ref[0]
    for tap in range(1, lat_taps):
        lateral_total = lateral_total + lateral_ref[tap]
    k = lax.broadcasted_iota(jnp.int32, tl_ref.shape, 0)
    j = lax.broadcasted_iota(jnp.int32, tl_ref.shape, 1)
    place = k - LANES - j + lat_taps // 2
    forward = jnp.zeros(tl_ref.shape, f32)
    backward = jnp.zeros(tl_ref.shape, f32)
    for tap in range(lat_taps):
        forward = jnp.where(place == tap, lateral_ref[tap], forward)
        backward = jnp.where(place == lat_taps - 1 - tap, lateral_ref[tap], backward)
    scale = jnp.full((1, TILE), lateral_total, f32)
    tl_ref[...] = (forward / scale).astype(bf16)
    tm_ref[...] = (backward / scale).astype(bf16)


def bands(psf_bank, lateral_psf, band_index, planes, halo):
    plans = stages(planes, psf_bank.shape[1] // 2)
    spread = jnp.pad(band_index, (halo, halo + SPAN), constant_values=-1)
    first = lax.axis_index("cam") * planes
    length = planes + 2 * halo + SPAN
    mine = lax.dynamic_slice_in_dim(spread, first, length, 0)
    index = jnp.broadcast_to(mine[:, None], (length, ROWS)).reshape(1, length * ROWS)
    smem = pl.BlockSpec(memory_space=pltpu.SMEM)
    vmem = pl.BlockSpec(memory_space=pltpu.VMEM)
    counts = [
        sum(len(flat(stage)) for stage in plan[kind::2]) for plan in plans for kind in range(2)
    ]
    strip = jax.ShapeDtypeStruct((TILE + 2 * LANES, TILE), jnp.bfloat16)
    return pl.pallas_call(
        functools.partial(bands_kernel, psf_bank.shape[1], lateral_psf.shape[0], plans),
        in_specs=[smem, smem, vmem],
        out_specs=[vmem] * (len(counts) + 2),
        out_shape=[
            jax.ShapeDtypeStruct((n, GROUP * ROWS, SPAN * ROWS), jnp.bfloat16) for n in counts
        ]
        + [strip, strip],
        compiler_params=pltpu.CompilerParams(vmem_limit_bytes=BANDS_VMEM),
        cost_estimate=pl.CostEstimate(
            flops=2_000_000_000, bytes_accessed=2_000_000, transcendentals=0
        ),
        name="bands",
    )(psf_bank, lateral_psf, index)


def restore_kernel(plan, side, half, counts, cut, *refs):
    inside = side == 0
    parts = []
    for count in counts:
        parts.append(refs[:count])
        refs = refs[count:]
    g, gt, tl, tm = refs[:4]
    refs = refs[4:]
    f32 = jnp.float32
    bf16 = jnp.bfloat16
    halo = 2 * ITERS * half
    if not inside:
        q_in, e_in = refs[:2]
        refs = refs[2:]
    buffers = refs[-8:]
    mf, ef, mb, qb, pad, pad_back, done, sems = buffers
    if inside:
        canvas, q_out, e_out = refs[-11:-8]
    else:
        canvas = refs[-9]
    size, columns = mf.shape
    total = size // ROWS
    tiles = -(-columns // TILE)

    for buffer in (pad, pad_back):
        buffer[:, :LANES] = jnp.zeros((size, LANES), bf16)
        buffer[:, LANES + columns :] = jnp.zeros((size, LANES), bf16)

    at_column = 0
    reach = (2 * ITERS - 1) * half
    for part in parts:
        width = part[0].shape[-1] if part is parts[-1] else 2 * LANES
        skip = part[0].shape[-1] - width
        if inside:
            loads = [(part[0], 0, part[0].shape[0], halo)]
        elif side < 0:
            loads = [(part[0], 0, part[0].shape[0], 0), (part[1], 0, reach // 2, halo)]
        else:
            own = part[0].shape[0]
            loads = [
                (part[0], own - reach // 2, own, total - halo - reach),
                (part[1], 0, part[1].shape[0], total - halo),
            ]
        for ref, lo, hi, plane in loads:
            rows = slice(plane * ROWS, plane * ROWS + (hi - lo) * ref.shape[1])
            for col in range(0, width, TILE):
                end = min(col + TILE, width)
                whole = ref[lo:hi, :, skip + col : skip + end].reshape(-1, end - col)
                there = slice(at_column + col, at_column + end)
                mb[rows, there] = whole
                mf[rows, there] = whole.astype(f32)
        at_column += width

    q_rows = slice((halo + half) * ROWS, (total - halo - half) * ROWS)
    e_width = half * (2 * ITERS - 2) * ROWS
    e_low = (halo + 2 * half) * ROWS
    e_high = (total - halo - 2 * half) * ROWS - e_width
    if not inside:
        q_height = halo * ROWS
        q_from = 0 if side < 0 else q_in.shape[0] - q_height
        q_to = q_rows.start + q_from
        qb[q_to : q_to + q_height, :] = q_in[q_from : q_from + q_height, :]
        e_from, e_to = (0, e_low) if side < 0 else (e_width, e_high)
        e_first = e_in[e_from : e_from + e_width, :]
        ef[e_to : e_to + e_width, :] = e_first
        mb[e_to : e_to + e_width, :] = e_first.astype(bf16)

    copies = []
    base = canvas.shape[-1] - columns if cut else 0
    limit = canvas.shape[-1] if cut else columns - LANES
    top = ITERS * 2 * half

    def wide(tile):
        return min(TILE, columns - tile * TILE)

    def columns_of(tile):
        return slice(tile * TILE, tile * TILE + wide(tile))

    def within(tile):
        return slice(LANES + tile * TILE, LANES + tile * TILE + wide(tile))

    def around(tile):
        return slice(tile * TILE, tile * TILE + wide(tile) + 2 * LANES)

    def lateral(rows, source, matrix, tile):
        band = matrix[: wide(tile) + 2 * LANES, : wide(tile)]
        return jnp.dot(source[rows, around(tile)], band, preferred_element_type=f32)

    def rows_of(groups):
        return slice(groups[0][0] * ROWS, (groups[-1][0] + groups[-1][1]) * ROWS)

    def axial(matrices, skip, stage, source, target, tile):
        for number, (first, count) in enumerate(flat(stage)):
            low = (first - half) * ROWS
            high = (first + count + half) * ROWS
            r = jnp.dot(
                matrices[skip + number, : count * ROWS, : high - low],
                source[low:high, columns_of(tile)],
                preferred_element_type=f32,
            )
            target[first * ROWS : (first + count) * ROWS, within(tile)] = r.astype(bf16)

    for sweep in range(ITERS):
        ahead, back = plan[2 * sweep], plan[2 * sweep + 1]
        skip_ahead = sum(len(flat(stage)) for stage in plan[0 : 2 * sweep : 2])
        skip_back = sum(len(flat(stage)) for stage in plan[1 : 2 * sweep : 2])
        final = sweep == ITERS - 1

        def ratio(tile):
            cols = columns_of(tile)
            for groups in ahead:
                rows = rows_of(groups)
                b = lateral(rows, pad, tl, tile) + BACKGROUND
                guess = pl.reciprocal(b, approx=True)
                guess = guess * (2.0 - b * guess)
                qb[rows, cols] = (mf[rows, cols] * guess).astype(bf16)

        def update(tile):
            cols = columns_of(tile)
            for groups in back:
                rows = rows_of(groups)
                d = lateral(rows, pad_back, tm, tile)
                e = (mf if sweep == 0 else ef)[rows, cols] * d
                if not final:
                    ef[rows, cols] = e
                    mb[rows, cols] = e.astype(bf16)
                    continue
                start = base + tile * TILE
                drop = cut if tile == 0 else 0
                keep = min(wide(tile), limit - start)
                if keep > drop:
                    first, count = groups[0][0] - top, e.shape[0] // ROWS
                    where = (slice(first, first + count), slice(None))
                    here = slice(tile * TILE + drop, tile * TILE + keep)
                    done[where + (here,)] = e.reshape(-1, ROWS, wide(tile))[:, :, drop:keep].astype(bf16)
                    copy = pltpu.make_async_copy(
                        done.at[where + (here,)],
                        canvas.at[where + (slice(start + drop, start + keep),)],
                        sems.at[len(copies)],
                    )
                    copy.start()
                    copies.append(copy)

        for step in range(tiles + 5):
            if step < tiles:
                axial(g, skip_ahead, ahead, mb, pad, step)
            if 0 <= step - 2 < tiles:
                ratio(step - 2)
            if 0 <= step - 3 < tiles:
                axial(gt, skip_back, back, qb, pad_back, step - 3)
            if 0 <= step - 5 < tiles:
                update(step - 5)

    if inside:
        q_out[...] = qb[q_rows, :]
        e_out[:e_width, :] = ef[e_low : e_low + e_width, :]
        e_out[e_width:, :] = ef[e_high : e_high + e_width, :]
    for copy in copies:
        copy.wait()


def restore(parts, matrices, state, canvas, plan, side, planes, half, columns):
    inside = side == 0
    later = len(parts) > 1
    width = parts[-1][0].shape[-1] + (2 * LANES if later else 0)
    halo = 2 * ITERS * half
    height = (planes + 2 * halo) * ROWS
    bf16 = jnp.bfloat16
    vmem = pl.BlockSpec(memory_space=pltpu.VMEM)
    hbm = pl.BlockSpec(memory_space=pltpu.HBM)
    operands = [array for part in parts for array in part] + [*matrices, *state]
    specs = [vmem] * len(operands)
    aliases = {}
    if canvas is not None:
        aliases = {len(operands): 0}
        operands.append(canvas)
        specs.append(hbm)
    results = [jax.ShapeDtypeStruct((planes, ROWS, columns), bf16)]
    if inside:
        results += [
            jax.ShapeDtypeStruct(((planes - 2 * half) * ROWS, width), bf16),
            jax.ShapeDtypeStruct((2 * half * (2 * ITERS - 2) * ROWS, width), jnp.float32),
        ]
    return pl.pallas_call(
        functools.partial(
            restore_kernel, plan, side, half, [len(part) for part in parts], LANES if later else 0
        ),
        in_specs=specs,
        out_specs=[hbm] + [vmem] * (len(results) - 1),
        out_shape=results,
        input_output_aliases=aliases,
        scratch_shapes=[
            pltpu.VMEM((height, width), jnp.float32),
            pltpu.VMEM((height, width), jnp.float32),
            pltpu.VMEM((height, width), bf16),
            pltpu.VMEM((height, width), bf16),
            pltpu.VMEM((height, width + 2 * LANES), bf16),
            pltpu.VMEM((height, width + 2 * LANES), bf16),
            pltpu.VMEM((planes, ROWS, width), bf16),
            pltpu.SemaphoreType.DMA((-(-width // TILE),)),
        ],
        compiler_params=pltpu.CompilerParams(vmem_limit_bytes=RESTORE_VMEM),
        cost_estimate=pl.CostEstimate(
            flops=5_000_000_000, bytes_accessed=8_000_000, transcendentals=0
        ),
        name=("low_end", "inside", "high_end")[side + 1],
    )(*operands)


def local(
    raw_frames,
    frame_order,
    dark_frame,
    flat_gain,
    stripe_band,
    shear_offset,
    shear_fraction,
    band_index,
    psf_bank,
    lateral_psf,
):
    half = psf_bank.shape[1] // 2
    planes = shear_offset.shape[0]
    columns = raw_frames.shape[-1]
    halo = 2 * ITERS * half
    plans = stages(planes, half)
    count = lax.axis_size("cam")
    forward = [(i, i + 1) for i in range(count - 1)]
    backward = [(i + 1, i) for i in range(count - 1)]
    *axial, forward_lateral, backward_lateral = bands(psf_bank, lateral_psf, band_index, planes, halo)
    matrices = [
        (*axial[2 * which : 2 * which + 2], forward_lateral, backward_lateral) for which in range(3)
    ]
    depth = halo // 2
    first_piece = frame_side(
        raw_frames, frame_order, dark_frame, flat_gain, stripe_band, shear_offset, shear_fraction, 0, SPLIT
    )
    first_piece, later_order = lax.optimization_barrier((first_piece, frame_order))
    second_piece = frame_side(
        raw_frames, later_order, dark_frame, flat_gain, stripe_band, shear_offset, shear_fraction,
        SPLIT, columns,
    )
    def exchange(piece):
        return lax.all_to_all(piece, "brick", split_axis=0, concat_axis=0, tiled=True)

    def with_halo(centre):
        low = lax.ppermute(centre[-depth:], "cam", forward)
        high = lax.ppermute(centre[:depth], "cam", backward)
        return low, centre, high

    def inside(parts, canvas):
        centres = [(centre,) for _, centre, _ in parts]
        canvas, *state = restore(
            centres, matrices[0], (), canvas, plans[0], 0, planes, half, columns
        )
        return canvas, state

    def ends(parts, state, canvas):
        lower = [(low, centre) for low, centre, _ in parts]
        upper = [(centre, high) for _, centre, high in parts]
        for which, side, given in ((1, -1, lower), (2, 1, upper)):
            (canvas,) = restore(
                given, matrices[which], state, canvas, plans[which], side, planes, half, columns
            )
        return canvas

    first, second_piece, matrices = lax.optimization_barrier(
        (exchange(first_piece), second_piece, matrices)
    )
    first_part = with_halo(first)
    canvas, first_state = inside([first_part], None)
    second, first_state = lax.optimization_barrier((exchange(second_piece), first_state))
    second_part = with_halo(second)
    canvas, second_state = inside([first_part, second_part], canvas)
    canvas = ends([first_part], first_state, canvas)
    return ends([first_part, second_part], second_state, canvas)


def solution(mesh):
    placed = (
        P(("cam", "brick"), None, None),
        P(("cam", "brick"), None),
        P(),
        P(),
        P(),
        P("cam"),
        P("cam"),
        P(),
        P(),
        P(),
    )
    return jax.shard_map(
        local, mesh=mesh, in_specs=placed, out_specs=P("cam", "brick", None), check_vma=False
    )
```

```python
import functools

import jax
import jax.numpy as jnp
from jax import lax
from jax.experimental import pallas as pl
from jax.experimental.pallas import tpu as pltpu
from jax.sharding import PartitionSpec as P

SHEAR = 512
ITERS = 2
BACKGROUND = 1.0

LANES = 128
TILE = 256
ROWS = 8
BLOCK_ROWS = 128
LEAD = SHEAR // LANES + 1
SPLIT = 1152
VMEM = 60 * 1024 * 1024
BANDS_VMEM = 20 * 1024 * 1024
RESTORE_VMEM = 26 * 1024 * 1024
LATER_VMEM = 20 * 1024 * 1024
GROUP = 20
SPAN = 32


def frame_kernel(
    first, count,
    order_ref, offset_ref, fraction_ref,
    raw_prev, raw_main, raw_next,
    dark_prev, dark_main, dark_next,
    gain_prev, gain_main, gain_next,
    band_ref, out_ref, scratch, level,
):
    step = pl.program_id(0)
    steps = pl.num_programs(0)
    rows = BLOCK_ROWS + 16
    brick = lax.axis_index("brick")
    f32 = jnp.float32
    bf16 = jnp.bfloat16
    base = first - LEAD

    @pl.when(step == 0)
    def _():
        if base < 0:
            scratch[:, :, : -base * LANES] = jnp.zeros((2, BLOCK_ROWS, -base * LANES), f32)

    has_prev = (step > 0).astype(f32)
    has_next = (step < steps - 1).astype(f32)
    frames = [jnp.where(order_ref[0, 0] == place, 0, 1) for place in range(2)]

    used = range(max(base, 0), first + count)
    for tile in used:
        cols = pl.ds(tile * LANES, LANES)
        for part, keep, start in ((0, slice(8, 16), 0), (1, slice(None), 8), (2, slice(0, 8), rows - 8)):
            dark = (dark_prev, dark_main, dark_next)[part][:, cols].astype(f32)[keep]
            gain = (gain_prev, gain_main, gain_next)[part][:, cols].astype(f32)[keep]
            if part != 1:
                gain = gain * (has_prev, None, has_next)[part]
            raw = (raw_prev, raw_main, raw_next)[part]
            for place in range(2):
                f = (raw[frames[place], :, cols].astype(f32)[keep] - dark) * gain
                level[place, tile - used[0], start : start + f.shape[0], :] = f

    zero = jnp.minimum(step, 0)
    taps = band_ref.shape[0]
    for tile in used:
        band = band_ref[:, pl.ds(tile * LANES, LANES)]
        for place in range(2):
            here = tile - used[0]
            out = level[place, here, 8 : 8 + BLOCK_ROWS, :] * (1.0 + band[taps // 2 : taps // 2 + 1])
            for tap in range(taps):
                if tap != taps // 2:
                    shifted = level[place, here, pl.ds(zero + 8 + tap - taps // 2, BLOCK_ROWS), :]
                    out = out + band[tap : tap + 1] * shifted
            scratch[place, :, pl.ds((tile - base) * LANES, LANES)] = out.astype(bf16).astype(f32)

    lane = lax.broadcasted_iota(jnp.int32, (BLOCK_ROWS, LANES), 1)
    bricks = BLOCK_ROWS // ROWS
    for place in range(2):
        amount = offset_ref[brick * 2 + place]
        weight = fraction_ref[brick * 2 + place]
        whole = amount // LANES
        part = amount % LANES
        near_mask = lane < part
        far_mask = lane < part + 1

        def turned(tile):
            start = (tile - base - whole) * LANES
            x = scratch[place, :, pl.ds(pl.multiple_of(start, LANES), LANES)]
            return (1.0 - weight) * pltpu.roll(x, part, 1), weight * pltpu.roll(x, (part + 1) % LANES, 1)

        last = turned(first - 1)
        for tile in range(first, first + count):
            now = turned(tile)
            mixed = jnp.where(near_mask, last[0], now[0]) + jnp.where(far_mask, last[1], now[1])
            last = now
            out_ref[:, place * ROWS : (place + 1) * ROWS, pl.ds((tile - first) * LANES, LANES)] = (
                mixed.reshape(bricks, ROWS, LANES).astype(bf16)
            )


def frame_side(raw, order, dark, gain, band, offset, fraction, lo, hi):
    _, frame_rows, columns = raw.shape
    steps = frame_rows // BLOCK_ROWS
    bricks = frame_rows // ROWS
    per = BLOCK_ROWS // 16
    last = frame_rows // 16 - 1
    smem = pl.BlockSpec(memory_space=pltpu.SMEM)
    first, count = lo // LANES, (hi - lo) // LANES
    if lo == 0:
        columns = hi

    def three(lead):
        zeros = (0,) * len(lead)
        return [
            pl.BlockSpec(lead + (16, columns), lambda i: zeros + (jnp.maximum(per * i - 1, 0), 0)),
            pl.BlockSpec(lead + (BLOCK_ROWS, columns), lambda i: zeros + (i, 0)),
            pl.BlockSpec(lead + (16, columns), lambda i: zeros + (jnp.minimum(per * i + per, last), 0)),
        ]

    return pl.pallas_call(
        functools.partial(frame_kernel, first, count),
        grid=(steps,),
        in_specs=[smem, smem, smem]
        + three((2,)) + three(()) + three(())
        + [pl.BlockSpec((band.shape[0], columns), lambda i: (0, 0))],
        out_specs=pl.BlockSpec((BLOCK_ROWS // ROWS, 2 * ROWS, hi - lo), lambda i: (i, 0, 0)),
        out_shape=jax.ShapeDtypeStruct((bricks, 2 * ROWS, hi - lo), jnp.bfloat16),
        scratch_shapes=[
            pltpu.VMEM((2, BLOCK_ROWS, (LEAD + count) * LANES), jnp.float32),
            pltpu.VMEM((2, min(first, LEAD) + count, BLOCK_ROWS + 16, LANES), jnp.float32),
        ],
        compiler_params=pltpu.CompilerParams(vmem_limit_bytes=VMEM if lo == 0 else LATER_VMEM),
        cost_estimate=pl.CostEstimate(
            flops=8_000_000_000, bytes_accessed=6_500_000, transcendentals=0
        ),
        name="frame_side",
    )(order, offset, fraction, raw, raw, raw, dark, dark, dark, gain, gain, gain, band)


def stages(planes, half):
    halo = 2 * ITERS * half
    total = planes + 2 * halo

    def cut(lo, hi, most):
        parts = -(-(hi - lo) // most)
        size = -(-(hi - lo) // (2 * parts)) * 2
        return [(at, min(size, hi - at)) for at in range(lo, hi, size)]

    inner, outer = [], []
    for stage in range(1, 2 * ITERS + 1):
        reach = stage * half
        lo, hi = halo + reach, total - halo - reach
        inner.append([cut(lo, hi, GROUP)])
        outer.append([cut(reach, lo, GROUP), cut(hi, total - reach, GROUP)])
    return inner, outer


def flat(stage):
    return [group for groups in stage for group in groups]


def bands_kernel(taps, lat_taps, plans, psf_ref, lateral_ref, index_ref, *outs):
    matrices, (tl_ref, tm_ref) = outs[:-2], outs[-2:]
    f32 = jnp.float32
    bf16 = jnp.bfloat16
    half = taps // 2
    width = SPAN * ROWS
    index = index_ref[...]
    raw = []
    for tap in range(taps):
        value = jnp.zeros(index.shape, f32)
        for kernel in range(psf_ref.shape[0]):
            value = jnp.where(index == kernel, psf_ref[kernel, tap], value)
        raw.append(value)
    total = functools.reduce(lambda a, b: a + b, raw)
    total = jnp.where(total > 0.0, total, 1.0)
    unit = [value / total for value in raw]
    row = lax.broadcasted_iota(jnp.int32, (width, width), 0)
    col = lax.broadcasted_iota(jnp.int32, (width, width), 1)

    def banded(start, gap, order):
        m = jnp.zeros((width, width), f32)
        for tap in range(taps):
            values = unit[tap][:, start * ROWS : start * ROWS + width]
            m = jnp.where(gap == ROWS * order(tap), values, m)
        return m

    for which, plan in enumerate(plans):
        slot = [0, 0]
        for number, stage in enumerate(plan):
            kind = number % 2
            target = matrices[2 * which + kind]
            for at, _ in flat(stage):
                if kind == 0:
                    m = banded(at, row - col, lambda tap: tap).T
                else:
                    m = banded(at - half, col - row, lambda tap: 2 * half - tap)
                target[slot[kind]] = m[: GROUP * ROWS].astype(bf16)
                slot[kind] += 1

    lateral_total = lateral_ref[0]
    for tap in range(1, lat_taps):
        lateral_total = lateral_total + lateral_ref[tap]
    k = lax.broadcasted_iota(jnp.int32, tl_ref.shape, 0)
    j = lax.broadcasted_iota(jnp.int32, tl_ref.shape, 1)
    place = k - LANES - j + lat_taps // 2
    forward = jnp.zeros(tl_ref.shape, f32)
    backward = jnp.zeros(tl_ref.shape, f32)
    for tap in range(lat_taps):
        forward = jnp.where(place == tap, lateral_ref[tap], forward)
        backward = jnp.where(place == lat_taps - 1 - tap, lateral_ref[tap], backward)
    scale = jnp.full((1, TILE), lateral_total, f32)
    tl_ref[...] = (forward / scale).astype(bf16)
    tm_ref[...] = (backward / scale).astype(bf16)


def bands(psf_bank, lateral_psf, band_index, planes, halo):
    plans = stages(planes, psf_bank.shape[1] // 2)
    spread = jnp.pad(band_index, (halo, halo + SPAN), constant_values=-1)
    first = lax.axis_index("cam") * planes
    length = planes + 2 * halo + SPAN
    mine = lax.dynamic_slice_in_dim(spread, first, length, 0)
    index = jnp.broadcast_to(mine[:, None], (length, ROWS)).reshape(1, length * ROWS)
    smem = pl.BlockSpec(memory_space=pltpu.SMEM)
    vmem = pl.BlockSpec(memory_space=pltpu.VMEM)
    counts = [
        sum(len(flat(stage)) for stage in plan[kind::2]) for plan in plans for kind in range(2)
    ]
    strip = jax.ShapeDtypeStruct((TILE + 2 * LANES, TILE), jnp.bfloat16)
    return pl.pallas_call(
        functools.partial(bands_kernel, psf_bank.shape[1], lateral_psf.shape[0], plans),
        in_specs=[smem, smem, vmem],
        out_specs=[vmem] * (len(counts) + 2),
        out_shape=[
            jax.ShapeDtypeStruct((n, GROUP * ROWS, SPAN * ROWS), jnp.bfloat16) for n in counts
        ]
        + [strip, strip],
        compiler_params=pltpu.CompilerParams(vmem_limit_bytes=BANDS_VMEM),
        cost_estimate=pl.CostEstimate(
            flops=2_000_000_000, bytes_accessed=2_000_000, transcendentals=0
        ),
        name="bands",
    )(psf_bank, lateral_psf, index)


def restore_kernel(plan, inside, half, counts, cut, *refs):
    parts = []
    for count in counts:
        parts.append(refs[:count])
        refs = refs[count:]
    g, gt, tl, tm = refs[:4]
    refs = refs[4:]
    f32 = jnp.float32
    bf16 = jnp.bfloat16
    halo = 2 * ITERS * half
    if not inside:
        q_in, e_in = refs[:2]
        refs = refs[2:]
    buffers = refs[-8:]
    mf, ef, mb, qb, pad, pad_back, done, sems = buffers
    if inside:
        canvas, q_out, e_out = refs[-11:-8]
    else:
        canvas = refs[-9]
    size, columns = mf.shape
    total = size // ROWS
    tiles = -(-columns // TILE)

    for buffer in (pad, pad_back):
        buffer[:, :LANES] = jnp.zeros((size, LANES), bf16)
        buffer[:, LANES + columns :] = jnp.zeros((size, LANES), bf16)

    at_column = 0
    reach = (2 * ITERS - 1) * half
    for part in parts:
        width = part[0].shape[-1] if part is parts[-1] else 2 * LANES
        skip = part[0].shape[-1] - width
        if inside:
            loads = [(part[0], 0, part[0].shape[0], halo)]
        else:
            low, own, high = part
            count = own.shape[0]
            loads = [
                (low, 0, low.shape[0], 0),
                (own, 0, reach // 2, halo),
                (own, count - reach // 2, count, total - halo - reach),
                (high, 0, high.shape[0], total - halo),
            ]
        for ref, lo, hi, plane in loads:
            rows = slice(plane * ROWS, plane * ROWS + (hi - lo) * ref.shape[1])
            for col in range(0, width, TILE):
                end = min(col + TILE, width)
                whole = ref[lo:hi, :, skip + col : skip + end].reshape(-1, end - col)
                there = slice(at_column + col, at_column + end)
                mb[rows, there] = whole
                mf[rows, there] = whole.astype(f32)
        at_column += width

    q_rows = slice((halo + half) * ROWS, (total - halo - half) * ROWS)
    e_width = half * (2 * ITERS - 2) * ROWS
    e_low = (halo + 2 * half) * ROWS
    e_high = (total - halo - 2 * half) * ROWS - e_width
    if not inside:
        q_height = halo * ROWS
        for q_from in (0, q_in.shape[0] - q_height):
            q_to = q_rows.start + q_from
            qb[q_to : q_to + q_height, :] = q_in[q_from : q_from + q_height, :]
        for e_from, e_to in ((0, e_low), (e_width, e_high)):
            e_first = e_in[e_from : e_from + e_width, :]
            ef[e_to : e_to + e_width, :] = e_first
            mb[e_to : e_to + e_width, :] = e_first.astype(bf16)

    copies = []
    base = canvas.shape[-1] - columns if cut else 0
    limit = canvas.shape[-1] if cut else columns - LANES
    top = ITERS * 2 * half

    def wide(tile):
        return min(TILE, columns - tile * TILE)

    def columns_of(tile):
        return slice(tile * TILE, tile * TILE + wide(tile))

    def within(tile):
        return slice(LANES + tile * TILE, LANES + tile * TILE + wide(tile))

    def around(tile):
        return slice(tile * TILE, tile * TILE + wide(tile) + 2 * LANES)

    def lateral(rows, source, matrix, tile):
        band = matrix[: wide(tile) + 2 * LANES, : wide(tile)]
        return jnp.dot(source[rows, around(tile)], band, preferred_element_type=f32)

    def rows_of(groups):
        return slice(groups[0][0] * ROWS, (groups[-1][0] + groups[-1][1]) * ROWS)

    def axial(matrices, skip, stage, source, target, tile):
        for number, (first, count) in enumerate(flat(stage)):
            low = (first - half) * ROWS
            high = (first + count + half) * ROWS
            r = jnp.dot(
                matrices[skip + number, : count * ROWS, : high - low],
                source[low:high, columns_of(tile)],
                preferred_element_type=f32,
            )
            target[first * ROWS : (first + count) * ROWS, within(tile)] = r.astype(bf16)

    for sweep in range(ITERS):
        ahead, back = plan[2 * sweep], plan[2 * sweep + 1]
        skip_ahead = sum(len(flat(stage)) for stage in plan[0 : 2 * sweep : 2])
        skip_back = sum(len(flat(stage)) for stage in plan[1 : 2 * sweep : 2])
        final = sweep == ITERS - 1

        def ratio(tile):
            cols = columns_of(tile)
            for groups in ahead:
                rows = rows_of(groups)
                b = lateral(rows, pad, tl, tile) + BACKGROUND
                guess = pl.reciprocal(b, approx=True)
                guess = guess * (2.0 - b * guess)
                qb[rows, cols] = (mf[rows, cols] * guess).astype(bf16)

        def update(tile):
            cols = columns_of(tile)
            for groups in back:
                rows = rows_of(groups)
                d = lateral(rows, pad_back, tm, tile)
                e = (mf if sweep == 0 else ef)[rows, cols] * d
                if not final:
                    ef[rows, cols] = e
                    mb[rows, cols] = e.astype(bf16)
                    continue
                start = base + tile * TILE
                drop = cut if tile == 0 else 0
                keep = min(wide(tile), limit - start)
                if keep > drop:
                    first, count = groups[0][0] - top, e.shape[0] // ROWS
                    where = (slice(first, first + count), slice(None))
                    here = slice(tile * TILE + drop, tile * TILE + keep)
                    done[where + (here,)] = e.reshape(-1, ROWS, wide(tile))[:, :, drop:keep].astype(bf16)
                    copy = pltpu.make_async_copy(
                        done.at[where + (here,)],
                        canvas.at[where + (slice(start + drop, start + keep),)],
                        sems.at[len(copies)],
                    )
                    copy.start()
                    copies.append(copy)

        for step in range(tiles + 5):
            if step < tiles:
                axial(g, skip_ahead, ahead, mb, pad, step)
            if 0 <= step - 2 < tiles:
                ratio(step - 2)
            if 0 <= step - 3 < tiles:
                axial(gt, skip_back, back, qb, pad_back, step - 3)
            if 0 <= step - 5 < tiles:
                update(step - 5)

    if inside:
        q_out[...] = qb[q_rows, :]
        e_out[:e_width, :] = ef[e_low : e_low + e_width, :]
        e_out[e_width:, :] = ef[e_high : e_high + e_width, :]
    for copy in copies:
        copy.wait()


def restore(parts, matrices, state, canvas, plan, inside, planes, half, columns):
    later = len(parts) > 1
    width = parts[-1][0].shape[-1] + (2 * LANES if later else 0)
    halo = 2 * ITERS * half
    height = (planes + 2 * halo) * ROWS
    bf16 = jnp.bfloat16
    vmem = pl.BlockSpec(memory_space=pltpu.VMEM)
    hbm = pl.BlockSpec(memory_space=pltpu.HBM)
    operands = [array for part in parts for array in part] + [*matrices, *state]
    specs = [vmem] * len(operands)
    aliases = {}
    if canvas is not None:
        aliases = {len(operands): 0}
        operands.append(canvas)
        specs.append(hbm)
    results = [jax.ShapeDtypeStruct((planes, ROWS, columns), bf16)]
    if inside:
        results += [
            jax.ShapeDtypeStruct(((planes - 2 * half) * ROWS, width), bf16),
            jax.ShapeDtypeStruct((2 * half * (2 * ITERS - 2) * ROWS, width), jnp.float32),
        ]
    return pl.pallas_call(
        functools.partial(
            restore_kernel, plan, inside, half, [len(part) for part in parts], LANES if later else 0
        ),
        in_specs=specs,
        out_specs=[hbm] + [vmem] * (len(results) - 1),
        out_shape=results,
        input_output_aliases=aliases,
        scratch_shapes=[
            pltpu.VMEM((height, width), jnp.float32),
            pltpu.VMEM((height, width), jnp.float32),
            pltpu.VMEM((height, width), bf16),
            pltpu.VMEM((height, width), bf16),
            pltpu.VMEM((height, width + 2 * LANES), bf16),
            pltpu.VMEM((height, width + 2 * LANES), bf16),
            pltpu.VMEM((planes, ROWS, width), bf16),
            pltpu.SemaphoreType.DMA((-(-width // TILE) * (1 if inside else 2),)),
        ],
        compiler_params=pltpu.CompilerParams(vmem_limit_bytes=RESTORE_VMEM),
        cost_estimate=pl.CostEstimate(
            flops=5_000_000_000, bytes_accessed=8_000_000, transcendentals=0
        ),
        name="inside" if inside else "ends",
    )(*operands)


def local(
    raw_frames,
    frame_order,
    dark_frame,
    flat_gain,
    stripe_band,
    shear_offset,
    shear_fraction,
    band_index,
    psf_bank,
    lateral_psf,
):
    half = psf_bank.shape[1] // 2
    planes = shear_offset.shape[0]
    columns = raw_frames.shape[-1]
    halo = 2 * ITERS * half
    plans = stages(planes, half)
    count = lax.axis_size("cam")
    forward = [(i, i + 1) for i in range(count - 1)]
    backward = [(i + 1, i) for i in range(count - 1)]
    *axial, forward_lateral, backward_lateral = bands(psf_bank, lateral_psf, band_index, planes, halo)
    matrices = [
        (*axial[2 * which : 2 * which + 2], forward_lateral, backward_lateral) for which in range(2)
    ]
    depth = halo // 2
    first_piece = frame_side(
        raw_frames, frame_order, dark_frame, flat_gain, stripe_band, shear_offset, shear_fraction, 0, SPLIT
    )
    first_piece, later_order = lax.optimization_barrier((first_piece, frame_order))
    second_piece = frame_side(
        raw_frames, later_order, dark_frame, flat_gain, stripe_band, shear_offset, shear_fraction,
        SPLIT, columns,
    )
    def exchange(piece):
        return lax.all_to_all(piece, "brick", split_axis=0, concat_axis=0, tiled=True)

    def with_halo(centre):
        low = lax.ppermute(centre[-depth:], "cam", forward)
        high = lax.ppermute(centre[:depth], "cam", backward)
        return low, centre, high

    def inside(parts, canvas):
        centres = [(centre,) for _, centre, _ in parts]
        canvas, *state = restore(
            centres, matrices[0], (), canvas, plans[0], True, planes, half, columns
        )
        return canvas, state

    def ends(parts, state, canvas):
        return restore(
            parts, matrices[1], state, canvas, plans[1], False, planes, half, columns
        )[0]

    first, second_piece, matrices = lax.optimization_barrier(
        (exchange(first_piece), second_piece, matrices)
    )
    first_part = with_halo(first)
    canvas, first_state = inside([first_part], None)
    second, first_state = lax.optimization_barrier((exchange(second_piece), first_state))
    second_part = with_halo(second)
    canvas, second_state = inside([first_part, second_part], canvas)
    canvas = ends([first_part], first_state, canvas)
    return ends([first_part, second_part], second_state, canvas)


def solution(mesh):
    placed = (
        P(("cam", "brick"), None, None),
        P(("cam", "brick"), None),
        P(),
        P(),
        P(),
        P("cam"),
        P("cam"),
        P(),
        P(),
        P(),
    )
    return jax.shard_map(
        local, mesh=mesh, in_specs=placed, out_specs=P("cam", "brick", None), check_vma=False
    )
```

```python
import functools

import jax
import jax.numpy as jnp
from jax import lax
from jax.experimental import pallas as pl
from jax.experimental.pallas import tpu as pltpu
from jax.sharding import PartitionSpec as P

SHEAR = 512
ITERS = 2
BACKGROUND = 1.0

LANES = 128
TILE = 256
ROWS = 8
BLOCK_ROWS = 128
LEAD = SHEAR // LANES + 1
SPLIT = 1152
VMEM = 60 * 1024 * 1024
BANDS_VMEM = 20 * 1024 * 1024
RESTORE_VMEM = 26 * 1024 * 1024
LATER_VMEM = 20 * 1024 * 1024
GROUP = 20
SPAN = 32


def frame_kernel(
    first, count,
    order_ref, offset_ref, fraction_ref,
    raw_prev, raw_main, raw_next,
    dark_prev, dark_main, dark_next,
    gain_prev, gain_main, gain_next,
    band_ref, out_ref, scratch, level,
):
    step = pl.program_id(0)
    steps = pl.num_programs(0)
    rows = BLOCK_ROWS + 16
    brick = lax.axis_index("brick")
    f32 = jnp.float32
    bf16 = jnp.bfloat16
    base = first - LEAD

    @pl.when(step == 0)
    def _():
        if base < 0:
            scratch[:, :, : -base * LANES] = jnp.zeros((2, BLOCK_ROWS, -base * LANES), f32)

    has_prev = (step > 0).astype(f32)
    has_next = (step < steps - 1).astype(f32)
    frames = [jnp.where(order_ref[0, 0] == place, 0, 1) for place in range(2)]

    used = range(max(base, 0), first + count)
    for tile in used:
        cols = pl.ds(tile * LANES, LANES)
        for part, keep, start in ((0, slice(8, 16), 0), (1, slice(None), 8), (2, slice(0, 8), rows - 8)):
            dark = (dark_prev, dark_main, dark_next)[part][:, cols].astype(f32)[keep]
            gain = (gain_prev, gain_main, gain_next)[part][:, cols].astype(f32)[keep]
            if part != 1:
                gain = gain * (has_prev, None, has_next)[part]
            raw = (raw_prev, raw_main, raw_next)[part]
            for place in range(2):
                f = (raw[frames[place], :, cols].astype(f32)[keep] - dark) * gain
                level[place, tile - used[0], start : start + f.shape[0], :] = f

    zero = jnp.minimum(step, 0)
    taps = band_ref.shape[0]
    for tile in used:
        band = band_ref[:, pl.ds(tile * LANES, LANES)]
        for place in range(2):
            here = tile - used[0]
            out = level[place, here, 8 : 8 + BLOCK_ROWS, :] * (1.0 + band[taps // 2 : taps // 2 + 1])
            for tap in range(taps):
                if tap != taps // 2:
                    shifted = level[place, here, pl.ds(zero + 8 + tap - taps // 2, BLOCK_ROWS), :]
                    out = out + band[tap : tap + 1] * shifted
            scratch[place, :, pl.ds((tile - base) * LANES, LANES)] = out.astype(bf16).astype(f32)

    lane = lax.broadcasted_iota(jnp.int32, (BLOCK_ROWS, LANES), 1)
    bricks = BLOCK_ROWS // ROWS
    for place in range(2):
        amount = offset_ref[brick * 2 + place]
        weight = fraction_ref[brick * 2 + place]
        whole = amount // LANES
        part = amount % LANES
        near_mask = lane < part
        far_mask = lane < part + 1

        def turned(tile):
            start = (tile - base - whole) * LANES
            x = scratch[place, :, pl.ds(pl.multiple_of(start, LANES), LANES)]
            return (1.0 - weight) * pltpu.roll(x, part, 1), weight * pltpu.roll(x, (part + 1) % LANES, 1)

        last = turned(first - 1)
        for tile in range(first, first + count):
            now = turned(tile)
            mixed = jnp.where(near_mask, last[0], now[0]) + jnp.where(far_mask, last[1], now[1])
            last = now
            out_ref[:, place * ROWS : (place + 1) * ROWS, pl.ds((tile - first) * LANES, LANES)] = (
                mixed.reshape(bricks, ROWS, LANES).astype(bf16)
            )


def frame_side(raw, order, dark, gain, band, offset, fraction, lo, hi):
    _, frame_rows, columns = raw.shape
    steps = frame_rows // BLOCK_ROWS
    bricks = frame_rows // ROWS
    per = BLOCK_ROWS // 16
    last = frame_rows // 16 - 1
    smem = pl.BlockSpec(memory_space=pltpu.SMEM)
    first, count = lo // LANES, (hi - lo) // LANES
    if lo == 0:
        columns = hi

    def three(lead):
        zeros = (0,) * len(lead)
        return [
            pl.BlockSpec(lead + (16, columns), lambda i: zeros + (jnp.maximum(per * i - 1, 0), 0)),
            pl.BlockSpec(lead + (BLOCK_ROWS, columns), lambda i: zeros + (i, 0)),
            pl.BlockSpec(lead + (16, columns), lambda i: zeros + (jnp.minimum(per * i + per, last), 0)),
        ]

    return pl.pallas_call(
        functools.partial(frame_kernel, first, count),
        grid=(steps,),
        in_specs=[smem, smem, smem]
        + three((2,)) + three(()) + three(())
        + [pl.BlockSpec((band.shape[0], columns), lambda i: (0, 0))],
        out_specs=pl.BlockSpec((BLOCK_ROWS // ROWS, 2 * ROWS, hi - lo), lambda i: (i, 0, 0)),
        out_shape=jax.ShapeDtypeStruct((bricks, 2 * ROWS, hi - lo), jnp.bfloat16),
        scratch_shapes=[
            pltpu.VMEM((2, BLOCK_ROWS, (LEAD + count) * LANES), jnp.float32),
            pltpu.VMEM((2, min(first, LEAD) + count, BLOCK_ROWS + 16, LANES), jnp.float32),
        ],
        compiler_params=pltpu.CompilerParams(vmem_limit_bytes=VMEM if lo == 0 else LATER_VMEM),
        cost_estimate=pl.CostEstimate(
            flops=8_000_000_000, bytes_accessed=6_500_000, transcendentals=0
        ),
        name="frame_side",
    )(order, offset, fraction, raw, raw, raw, dark, dark, dark, gain, gain, gain, band)


def stages(planes, half):
    halo = 2 * ITERS * half
    total = planes + 2 * halo

    def cut(lo, hi, most):
        parts = -(-(hi - lo) // most)
        size = -(-(hi - lo) // (2 * parts)) * 2
        return [(at, min(size, hi - at)) for at in range(lo, hi, size)]

    inner, outer = [], []
    for stage in range(1, 2 * ITERS + 1):
        reach = stage * half
        lo, hi = halo + reach, total - halo - reach
        inner.append([cut(lo, hi, GROUP)])
        outer.append([cut(reach, lo, GROUP), cut(hi, total - reach, GROUP)])
    return inner, outer


def flat(stage):
    return [group for groups in stage for group in groups]


def bands_kernel(taps, lat_taps, plans, psf_ref, lateral_ref, index_ref, *outs):
    matrices, (tl_ref, tm_ref) = outs[:-2], outs[-2:]
    f32 = jnp.float32
    bf16 = jnp.bfloat16
    half = taps // 2
    width = SPAN * ROWS
    index = index_ref[...]
    raw = []
    for tap in range(taps):
        value = jnp.zeros(index.shape, f32)
        for kernel in range(psf_ref.shape[0]):
            value = jnp.where(index == kernel, psf_ref[kernel, tap], value)
        raw.append(value)
    total = functools.reduce(lambda a, b: a + b, raw)
    total = jnp.where(total > 0.0, total, 1.0)
    unit = [value / total for value in raw]
    row = lax.broadcasted_iota(jnp.int32, (width, width), 0)
    col = lax.broadcasted_iota(jnp.int32, (width, width), 1)

    def banded(start, gap, order):
        m = jnp.zeros((width, width), f32)
        for tap in range(taps):
            values = unit[tap][:, start * ROWS : start * ROWS + width]
            m = jnp.where(gap == ROWS * order(tap), values, m)
        return m

    for which, plan in enumerate(plans):
        slot = [0, 0]
        for number, stage in enumerate(plan):
            kind = number % 2
            target = matrices[2 * which + kind]
            for at, _ in flat(stage):
                if kind == 0:
                    m = banded(at, row - col, lambda tap: tap).T
                else:
                    m = banded(at - half, col - row, lambda tap: 2 * half - tap)
                target[slot[kind]] = m[: GROUP * ROWS].astype(bf16)
                slot[kind] += 1

    lateral_total = lateral_ref[0]
    for tap in range(1, lat_taps):
        lateral_total = lateral_total + lateral_ref[tap]
    k = lax.broadcasted_iota(jnp.int32, tl_ref.shape, 0)
    j = lax.broadcasted_iota(jnp.int32, tl_ref.shape, 1)
    place = k - LANES - j + lat_taps // 2
    forward = jnp.zeros(tl_ref.shape, f32)
    backward = jnp.zeros(tl_ref.shape, f32)
    for tap in range(lat_taps):
        forward = jnp.where(place == tap, lateral_ref[tap], forward)
        backward = jnp.where(place == lat_taps - 1 - tap, lateral_ref[tap], backward)
    scale = jnp.full((1, TILE), lateral_total, f32)
    tl_ref[...] = (forward / scale).astype(bf16)
    tm_ref[...] = (backward / scale).astype(bf16)


def bands(psf_bank, lateral_psf, band_index, planes, halo):
    plans = stages(planes, psf_bank.shape[1] // 2)
    spread = jnp.pad(band_index, (halo, halo + SPAN), constant_values=-1)
    first = lax.axis_index("cam") * planes
    length = planes + 2 * halo + SPAN
    mine = lax.dynamic_slice_in_dim(spread, first, length, 0)
    index = jnp.broadcast_to(mine[:, None], (length, ROWS)).reshape(1, length * ROWS)
    smem = pl.BlockSpec(memory_space=pltpu.SMEM)
    vmem = pl.BlockSpec(memory_space=pltpu.VMEM)
    counts = [
        sum(len(flat(stage)) for stage in plan[kind::2]) for plan in plans for kind in range(2)
    ]
    strip = jax.ShapeDtypeStruct((TILE + 2 * LANES, TILE), jnp.bfloat16)
    return pl.pallas_call(
        functools.partial(bands_kernel, psf_bank.shape[1], lateral_psf.shape[0], plans),
        in_specs=[smem, smem, vmem],
        out_specs=[vmem] * (len(counts) + 2),
        out_shape=[
            jax.ShapeDtypeStruct((n, GROUP * ROWS, SPAN * ROWS), jnp.bfloat16) for n in counts
        ]
        + [strip, strip],
        compiler_params=pltpu.CompilerParams(vmem_limit_bytes=BANDS_VMEM),
        cost_estimate=pl.CostEstimate(
            flops=2_000_000_000, bytes_accessed=2_000_000, transcendentals=0
        ),
        name="bands",
    )(psf_bank, lateral_psf, index)


def restore_kernel(plan, inside, half, counts, cut, *refs):
    parts = []
    for count in counts:
        parts.append(refs[:count])
        refs = refs[count:]
    g, gt, tl, tm = refs[:4]
    refs = refs[4:]
    f32 = jnp.float32
    bf16 = jnp.bfloat16
    halo = 2 * ITERS * half
    if not inside:
        q_in, e_in = refs[:2]
        refs = refs[2:]
    buffers = refs[-8:]
    mf, ef, mb, qb, pad, pad_back, done, sems = buffers
    if inside:
        canvas, q_out, e_out = refs[-11:-8]
    else:
        canvas = refs[-9]
    size, columns = mf.shape
    total = size // ROWS
    tiles = -(-columns // TILE)

    for buffer in (pad, pad_back):
        buffer[:, :LANES] = jnp.zeros((size, LANES), bf16)
        buffer[:, LANES + columns :] = jnp.zeros((size, LANES), bf16)

    at_column = 0
    reach = (2 * ITERS - 1) * half
    for part in parts:
        width = part[0].shape[-1] if part is parts[-1] else 2 * LANES
        skip = part[0].shape[-1] - width
        if inside:
            loads = [(part[0], 0, part[0].shape[0], halo)]
        else:
            low, own, high = part
            count = own.shape[0]
            loads = [
                (low, 0, low.shape[0], 0),
                (own, 0, reach // 2, halo),
                (own, count - reach // 2, count, total - halo - reach),
                (high, 0, high.shape[0], total - halo),
            ]
        for ref, lo, hi, plane in loads:
            rows = slice(plane * ROWS, plane * ROWS + (hi - lo) * ref.shape[1])
            for col in range(0, width, TILE):
                end = min(col + TILE, width)
                whole = ref[lo:hi, :, skip + col : skip + end].reshape(-1, end - col)
                there = slice(at_column + col, at_column + end)
                mb[rows, there] = whole
                mf[rows, there] = whole.astype(f32)
        at_column += width

    q_rows = slice((halo + half) * ROWS, (total - halo - half) * ROWS)
    e_width = half * (2 * ITERS - 2) * ROWS
    e_low = (halo + 2 * half) * ROWS
    e_high = (total - halo - 2 * half) * ROWS - e_width
    if not inside:
        q_height = halo * ROWS
        for q_from in (0, q_in.shape[0] - q_height):
            q_to = q_rows.start + q_from
            qb[q_to : q_to + q_height, :] = q_in[q_from : q_from + q_height, :]
        for e_from, e_to in ((0, e_low), (e_width, e_high)):
            e_first = e_in[e_from : e_from + e_width, :]
            ef[e_to : e_to + e_width, :] = e_first
            mb[e_to : e_to + e_width, :] = e_first.astype(bf16)

    copies = []
    base = canvas.shape[-1] - columns if cut else 0
    limit = canvas.shape[-1] if cut else columns - LANES
    top = ITERS * 2 * half

    def wide(tile):
        return min(TILE, columns - tile * TILE)

    def columns_of(tile):
        return slice(tile * TILE, tile * TILE + wide(tile))

    def within(tile):
        return slice(LANES + tile * TILE, LANES + tile * TILE + wide(tile))

    def around(tile):
        return slice(tile * TILE, tile * TILE + wide(tile) + 2 * LANES)

    def lateral(rows, source, matrix, tile):
        band = matrix[: wide(tile) + 2 * LANES, : wide(tile)]
        return jnp.dot(source[rows, around(tile)], band, preferred_element_type=f32)

    def rows_of(groups):
        return slice(groups[0][0] * ROWS, (groups[-1][0] + groups[-1][1]) * ROWS)

    def axial(matrices, skip, stage, source, target, tile):
        for number, (first, count) in enumerate(flat(stage)):
            low = (first - half) * ROWS
            high = (first + count + half) * ROWS
            r = jnp.dot(
                matrices[skip + number, : count * ROWS, : high - low],
                source[low:high, columns_of(tile)],
                preferred_element_type=f32,
            )
            target[first * ROWS : (first + count) * ROWS, within(tile)] = r.astype(bf16)

    def calls(sweep):
        ahead, back = plan[2 * sweep], plan[2 * sweep + 1]
        skip_ahead = sum(len(flat(stage)) for stage in plan[0 : 2 * sweep : 2])
        skip_back = sum(len(flat(stage)) for stage in plan[1 : 2 * sweep : 2])
        final = sweep == ITERS - 1

        def ratio(tile):
            cols = columns_of(tile)
            for groups in ahead:
                rows = rows_of(groups)
                b = lateral(rows, pad, tl, tile) + BACKGROUND
                guess = pl.reciprocal(b, approx=True)
                guess = guess * (2.0 - b * guess)
                qb[rows, cols] = (mf[rows, cols] * guess).astype(bf16)

        def update(tile):
            cols = columns_of(tile)
            for groups in back:
                rows = rows_of(groups)
                d = lateral(rows, pad_back, tm, tile)
                e = (mf if sweep == 0 else ef)[rows, cols] * d
                if not final:
                    ef[rows, cols] = e
                    mb[rows, cols] = e.astype(bf16)
                    continue
                start = base + tile * TILE
                drop = cut if tile == 0 else 0
                keep = min(wide(tile), limit - start)
                if keep > drop:
                    first, count = groups[0][0] - top, e.shape[0] // ROWS
                    where = (slice(first, first + count), slice(None))
                    here = slice(tile * TILE + drop, tile * TILE + keep)
                    done[where + (here,)] = e.reshape(-1, ROWS, wide(tile))[:, :, drop:keep].astype(bf16)
                    copy = pltpu.make_async_copy(
                        done.at[where + (here,)],
                        canvas.at[where + (slice(start + drop, start + keep),)],
                        sems.at[len(copies)],
                    )
                    copy.start()
                    copies.append(copy)

        return (
            (0, functools.partial(axial, g, skip_ahead, ahead, mb, pad)),
            (2, ratio),
            (3, functools.partial(axial, gt, skip_back, back, qb, pad_back)),
            (5, update),
        )

    waves = [(6 * sweep + lag, call) for sweep in range(ITERS) for lag, call in calls(sweep)]
    for step in range(tiles + max(lag for lag, _ in waves)):
        for lag, call in waves:
            if 0 <= step - lag < tiles:
                call(step - lag)

    if inside:
        q_out[...] = qb[q_rows, :]
        e_out[:e_width, :] = ef[e_low : e_low + e_width, :]
        e_out[e_width:, :] = ef[e_high : e_high + e_width, :]
    for copy in copies:
        copy.wait()


def restore(parts, matrices, state, canvas, plan, inside, planes, half, columns):
    later = len(parts) > 1
    width = parts[-1][0].shape[-1] + (2 * LANES if later else 0)
    halo = 2 * ITERS * half
    height = (planes + 2 * halo) * ROWS
    bf16 = jnp.bfloat16
    vmem = pl.BlockSpec(memory_space=pltpu.VMEM)
    hbm = pl.BlockSpec(memory_space=pltpu.HBM)
    operands = [array for part in parts for array in part] + [*matrices, *state]
    specs = [vmem] * len(operands)
    aliases = {}
    if canvas is not None:
        aliases = {len(operands): 0}
        operands.append(canvas)
        specs.append(hbm)
    results = [jax.ShapeDtypeStruct((planes, ROWS, columns), bf16)]
    if inside:
        results += [
            jax.ShapeDtypeStruct(((planes - 2 * half) * ROWS, width), bf16),
            jax.ShapeDtypeStruct((2 * half * (2 * ITERS - 2) * ROWS, width), jnp.float32),
        ]
    return pl.pallas_call(
        functools.partial(
            restore_kernel, plan, inside, half, [len(part) for part in parts], LANES if later else 0
        ),
        in_specs=specs,
        out_specs=[hbm] + [vmem] * (len(results) - 1),
        out_shape=results,
        input_output_aliases=aliases,
        scratch_shapes=[
            pltpu.VMEM((height, width), jnp.float32),
            pltpu.VMEM((height, width), jnp.float32),
            pltpu.VMEM((height, width), bf16),
            pltpu.VMEM((height, width), bf16),
            pltpu.VMEM((height, width + 2 * LANES), bf16),
            pltpu.VMEM((height, width + 2 * LANES), bf16),
            pltpu.VMEM((planes, ROWS, width), bf16),
            pltpu.SemaphoreType.DMA((-(-width // TILE) * (1 if inside else 2),)),
        ],
        compiler_params=pltpu.CompilerParams(vmem_limit_bytes=RESTORE_VMEM),
        cost_estimate=pl.CostEstimate(
            flops=5_000_000_000, bytes_accessed=8_000_000, transcendentals=0
        ),
        name="inside" if inside else "ends",
    )(*operands)


def local(
    raw_frames,
    frame_order,
    dark_frame,
    flat_gain,
    stripe_band,
    shear_offset,
    shear_fraction,
    band_index,
    psf_bank,
    lateral_psf,
):
    half = psf_bank.shape[1] // 2
    planes = shear_offset.shape[0]
    columns = raw_frames.shape[-1]
    halo = 2 * ITERS * half
    plans = stages(planes, half)
    count = lax.axis_size("cam")
    forward = [(i, i + 1) for i in range(count - 1)]
    backward = [(i + 1, i) for i in range(count - 1)]
    *axial, forward_lateral, backward_lateral = bands(psf_bank, lateral_psf, band_index, planes, halo)
    matrices = [
        (*axial[2 * which : 2 * which + 2], forward_lateral, backward_lateral) for which in range(2)
    ]
    depth = halo // 2
    first_piece = frame_side(
        raw_frames, frame_order, dark_frame, flat_gain, stripe_band, shear_offset, shear_fraction, 0, SPLIT
    )
    first_piece, later_order = lax.optimization_barrier((first_piece, frame_order))
    second_piece = frame_side(
        raw_frames, later_order, dark_frame, flat_gain, stripe_band, shear_offset, shear_fraction,
        SPLIT, columns,
    )
    def exchange(piece):
        return lax.all_to_all(piece, "brick", split_axis=0, concat_axis=0, tiled=True)

    def with_halo(centre):
        low = lax.ppermute(centre[-depth:], "cam", forward)
        high = lax.ppermute(centre[:depth], "cam", backward)
        return low, centre, high

    def inside(parts, canvas):
        centres = [(centre,) for _, centre, _ in parts]
        canvas, *state = restore(
            centres, matrices[0], (), canvas, plans[0], True, planes, half, columns
        )
        return canvas, state

    def ends(parts, state, canvas):
        return restore(
            parts, matrices[1], state, canvas, plans[1], False, planes, half, columns
        )[0]

    first, second_piece, matrices = lax.optimization_barrier(
        (exchange(first_piece), second_piece, matrices)
    )
    first_part = with_halo(first)
    canvas, first_state = inside([first_part], None)
    second, first_state = lax.optimization_barrier((exchange(second_piece), first_state))
    second_part = with_halo(second)
    canvas, second_state = inside([first_part, second_part], canvas)
    canvas = ends([first_part], first_state, canvas)
    return ends([first_part, second_part], second_state, canvas)


def solution(mesh):
    placed = (
        P(("cam", "brick"), None, None),
        P(("cam", "brick"), None),
        P(),
        P(),
        P(),
        P("cam"),
        P("cam"),
        P(),
        P(),
        P(),
    )
    return jax.shard_map(
        local, mesh=mesh, in_specs=placed, out_specs=P("cam", "brick", None), check_vma=False
    )
```

```python
import functools

import jax
import jax.numpy as jnp
from jax import lax
from jax.experimental import pallas as pl
from jax.experimental.pallas import tpu as pltpu
from jax.sharding import PartitionSpec as P

SHEAR = 512
ITERS = 2
BACKGROUND = 1.0

LANES = 128
TILE = 256
ROWS = 8
BLOCK_ROWS = 128
LEAD = SHEAR // LANES + 1
SPLIT = 1152
VMEM = 60 * 1024 * 1024
BANDS_VMEM = 20 * 1024 * 1024
RESTORE_VMEM = 26 * 1024 * 1024
LATER_VMEM = 20 * 1024 * 1024
GROUP = 20
SPAN = 32


def frame_kernel(
    first, count,
    order_ref, offset_ref, fraction_ref,
    raw_prev, raw_main, raw_next,
    dark_prev, dark_main, dark_next,
    gain_prev, gain_main, gain_next,
    band_ref, out_ref, scratch, level,
):
    step = pl.program_id(0)
    steps = pl.num_programs(0)
    rows = BLOCK_ROWS + 16
    brick = lax.axis_index("brick")
    f32 = jnp.float32
    bf16 = jnp.bfloat16
    base = first - LEAD

    @pl.when(step == 0)
    def _():
        if base < 0:
            scratch[:, :, : -base * LANES] = jnp.zeros((2, BLOCK_ROWS, -base * LANES), f32)

    has_prev = (step > 0).astype(f32)
    has_next = (step < steps - 1).astype(f32)
    frames = [jnp.where(order_ref[0, 0] == place, 0, 1) for place in range(2)]

    used = range(max(base, 0), first + count)
    for tile in used:
        cols = pl.ds(tile * LANES, LANES)
        for part, keep, start in ((0, slice(8, 16), 0), (1, slice(None), 8), (2, slice(0, 8), rows - 8)):
            dark = (dark_prev, dark_main, dark_next)[part][:, cols].astype(f32)[keep]
            gain = (gain_prev, gain_main, gain_next)[part][:, cols].astype(f32)[keep]
            if part != 1:
                gain = gain * (has_prev, None, has_next)[part]
            raw = (raw_prev, raw_main, raw_next)[part]
            for place in range(2):
                f = (raw[frames[place], :, cols].astype(f32)[keep] - dark) * gain
                level[place, tile - used[0], start : start + f.shape[0], :] = f

    zero = jnp.minimum(step, 0)
    taps = band_ref.shape[0]
    for tile in used:
        band = band_ref[:, pl.ds(tile * LANES, LANES)]
        for place in range(2):
            here = tile - used[0]
            out = level[place, here, 8 : 8 + BLOCK_ROWS, :] * (1.0 + band[taps // 2 : taps // 2 + 1])
            for tap in range(taps):
                if tap != taps // 2:
                    shifted = level[place, here, pl.ds(zero + 8 + tap - taps // 2, BLOCK_ROWS), :]
                    out = out + band[tap : tap + 1] * shifted
            scratch[place, :, pl.ds((tile - base) * LANES, LANES)] = out.astype(bf16).astype(f32)

    lane = lax.broadcasted_iota(jnp.int32, (BLOCK_ROWS, LANES), 1)
    bricks = BLOCK_ROWS // ROWS
    for place in range(2):
        amount = offset_ref[brick * 2 + place]
        weight = fraction_ref[brick * 2 + place]
        whole = amount // LANES
        part = amount % LANES
        near_mask = lane < part
        far_mask = lane < part + 1

        def turned(tile):
            start = (tile - base - whole) * LANES
            x = scratch[place, :, pl.ds(pl.multiple_of(start, LANES), LANES)]
            return (1.0 - weight) * pltpu.roll(x, part, 1), weight * pltpu.roll(x, (part + 1) % LANES, 1)

        last = turned(first - 1)
        for tile in range(first, first + count):
            now = turned(tile)
            mixed = jnp.where(near_mask, last[0], now[0]) + jnp.where(far_mask, last[1], now[1])
            last = now
            out_ref[:, place * ROWS : (place + 1) * ROWS, pl.ds((tile - first) * LANES, LANES)] = (
                mixed.reshape(bricks, ROWS, LANES).astype(bf16)
            )


def frame_side(raw, order, dark, gain, band, offset, fraction, lo, hi):
    _, frame_rows, columns = raw.shape
    steps = frame_rows // BLOCK_ROWS
    bricks = frame_rows // ROWS
    per = BLOCK_ROWS // 16
    last = frame_rows // 16 - 1
    smem = pl.BlockSpec(memory_space=pltpu.SMEM)
    first, count = lo // LANES, (hi - lo) // LANES
    if lo == 0:
        columns = hi

    def three(lead):
        zeros = (0,) * len(lead)
        return [
            pl.BlockSpec(lead + (16, columns), lambda i: zeros + (jnp.maximum(per * i - 1, 0), 0)),
            pl.BlockSpec(lead + (BLOCK_ROWS, columns), lambda i: zeros + (i, 0)),
            pl.BlockSpec(lead + (16, columns), lambda i: zeros + (jnp.minimum(per * i + per, last), 0)),
        ]

    return pl.pallas_call(
        functools.partial(frame_kernel, first, count),
        grid=(steps,),
        in_specs=[smem, smem, smem]
        + three((2,)) + three(()) + three(())
        + [pl.BlockSpec((band.shape[0], columns), lambda i: (0, 0))],
        out_specs=pl.BlockSpec((BLOCK_ROWS // ROWS, 2 * ROWS, hi - lo), lambda i: (i, 0, 0)),
        out_shape=jax.ShapeDtypeStruct((bricks, 2 * ROWS, hi - lo), jnp.bfloat16),
        scratch_shapes=[
            pltpu.VMEM((2, BLOCK_ROWS, (LEAD + count) * LANES), jnp.float32),
            pltpu.VMEM((2, min(first, LEAD) + count, BLOCK_ROWS + 16, LANES), jnp.float32),
        ],
        compiler_params=pltpu.CompilerParams(vmem_limit_bytes=VMEM if lo == 0 else LATER_VMEM),
        cost_estimate=pl.CostEstimate(
            flops=8_000_000_000, bytes_accessed=6_500_000, transcendentals=0
        ),
        name="frame_side",
    )(order, offset, fraction, raw, raw, raw, dark, dark, dark, gain, gain, gain, band)


def stages(planes, half):
    halo = 2 * ITERS * half
    total = planes + 2 * halo

    def cut(lo, hi, most):
        parts = -(-(hi - lo) // most)
        size = -(-(hi - lo) // (2 * parts)) * 2
        return [(at, min(size, hi - at)) for at in range(lo, hi, size)]

    inner, outer = [], []
    for stage in range(1, 2 * ITERS + 1):
        reach = stage * half
        lo, hi = halo + reach, total - halo - reach
        inner.append([cut(lo, hi, GROUP)])
        outer.append([cut(reach, lo, GROUP), cut(hi, total - reach, GROUP)])
    return inner, outer


def flat(stage):
    return [group for groups in stage for group in groups]


def bands_kernel(taps, lat_taps, plans, psf_ref, lateral_ref, index_ref, *outs):
    matrices, (tl_ref, tm_ref) = outs[:-2], outs[-2:]
    f32 = jnp.float32
    bf16 = jnp.bfloat16
    half = taps // 2
    width = SPAN * ROWS
    index = index_ref[...]
    raw = []
    for tap in range(taps):
        value = jnp.zeros(index.shape, f32)
        for kernel in range(psf_ref.shape[0]):
            value = jnp.where(index == kernel, psf_ref[kernel, tap], value)
        raw.append(value)
    total = functools.reduce(lambda a, b: a + b, raw)
    total = jnp.where(total > 0.0, total, 1.0)
    unit = [value / total for value in raw]
    row = lax.broadcasted_iota(jnp.int32, (width, width), 0)
    col = lax.broadcasted_iota(jnp.int32, (width, width), 1)

    def banded(start, gap, order):
        m = jnp.zeros((width, width), f32)
        for tap in range(taps):
            values = unit[tap][:, start * ROWS : start * ROWS + width]
            m = jnp.where(gap == ROWS * order(tap), values, m)
        return m

    for which, plan in enumerate(plans):
        slot = [0, 0]
        for number, stage in enumerate(plan):
            kind = number % 2
            target = matrices[2 * which + kind]
            for at, _ in flat(stage):
                if kind == 0:
                    m = banded(at, row - col, lambda tap: tap).T
                else:
                    m = banded(at - half, col - row, lambda tap: 2 * half - tap)
                target[slot[kind]] = m[: GROUP * ROWS].astype(bf16)
                slot[kind] += 1

    lateral_total = lateral_ref[0]
    for tap in range(1, lat_taps):
        lateral_total = lateral_total + lateral_ref[tap]
    k = lax.broadcasted_iota(jnp.int32, tl_ref.shape, 0)
    j = lax.broadcasted_iota(jnp.int32, tl_ref.shape, 1)
    place = k - LANES - j + lat_taps // 2
    forward = jnp.zeros(tl_ref.shape, f32)
    backward = jnp.zeros(tl_ref.shape, f32)
    for tap in range(lat_taps):
        forward = jnp.where(place == tap, lateral_ref[tap], forward)
        backward = jnp.where(place == lat_taps - 1 - tap, lateral_ref[tap], backward)
    scale = jnp.full((1, TILE), lateral_total, f32)
    tl_ref[...] = (forward / scale).astype(bf16)
    tm_ref[...] = (backward / scale).astype(bf16)


def bands(psf_bank, lateral_psf, band_index, planes, halo):
    plans = stages(planes, psf_bank.shape[1] // 2)
    spread = jnp.pad(band_index, (halo, halo + SPAN), constant_values=-1)
    first = lax.axis_index("cam") * planes
    length = planes + 2 * halo + SPAN
    mine = lax.dynamic_slice_in_dim(spread, first, length, 0)
    index = jnp.broadcast_to(mine[:, None], (length, ROWS)).reshape(1, length * ROWS)
    smem = pl.BlockSpec(memory_space=pltpu.SMEM)
    vmem = pl.BlockSpec(memory_space=pltpu.VMEM)
    counts = [
        sum(len(flat(stage)) for stage in plan[kind::2]) for plan in plans for kind in range(2)
    ]
    strip = jax.ShapeDtypeStruct((TILE + 2 * LANES, TILE), jnp.bfloat16)
    return pl.pallas_call(
        functools.partial(bands_kernel, psf_bank.shape[1], lateral_psf.shape[0], plans),
        in_specs=[smem, smem, vmem],
        out_specs=[vmem] * (len(counts) + 2),
        out_shape=[
            jax.ShapeDtypeStruct((n, GROUP * ROWS, SPAN * ROWS), jnp.bfloat16) for n in counts
        ]
        + [strip, strip],
        compiler_params=pltpu.CompilerParams(vmem_limit_bytes=BANDS_VMEM),
        cost_estimate=pl.CostEstimate(
            flops=2_000_000_000, bytes_accessed=2_000_000, transcendentals=0
        ),
        name="bands",
    )(psf_bank, lateral_psf, index)


def restore_kernel(plan, inside, half, counts, cut, *refs):
    parts = []
    for count in counts:
        parts.append(refs[:count])
        refs = refs[count:]
    g, gt, tl, tm = refs[:4]
    refs = refs[4:]
    f32 = jnp.float32
    bf16 = jnp.bfloat16
    halo = 2 * ITERS * half
    if not inside:
        q_in, e_in = refs[:2]
        refs = refs[2:]
    buffers = refs[-8:]
    mf, ef, mb, qb, pad, pad_back, done, sems = buffers
    if inside:
        canvas, q_out, e_out = refs[-11:-8]
    else:
        canvas = refs[-9]
    size, columns = mf.shape
    total = size // ROWS
    tiles = -(-columns // TILE)

    for buffer in (pad, pad_back):
        edge = jnp.zeros((buffer.shape[0], LANES), bf16)
        buffer[:, :LANES] = edge
        buffer[:, LANES + columns :] = edge

    at_column = 0
    reach = (2 * ITERS - 1) * half
    for part in parts:
        width = part[0].shape[-1] if part is parts[-1] else 2 * LANES
        skip = part[0].shape[-1] - width
        if inside:
            loads = [(part[0], 0, part[0].shape[0], halo)]
        else:
            low, own, high = part
            count = own.shape[0]
            loads = [
                (low, 0, low.shape[0], 0),
                (own, 0, reach // 2, halo),
                (own, count - reach // 2, count, total - halo - reach),
                (high, 0, high.shape[0], total - halo),
            ]
        for ref, lo, hi, plane in loads:
            rows = slice(plane * ROWS, plane * ROWS + (hi - lo) * ref.shape[1])
            for col in range(0, width, TILE):
                end = min(col + TILE, width)
                whole = ref[lo:hi, :, skip + col : skip + end].reshape(-1, end - col)
                there = slice(at_column + col, at_column + end)
                mb[rows, there] = whole
                mf[rows, there] = whole.astype(f32)
        at_column += width

    q_rows = slice((halo + half) * ROWS, (total - halo - half) * ROWS)
    e_width = half * (2 * ITERS - 2) * ROWS
    e_low = (halo + 2 * half) * ROWS
    e_high = (total - halo - 2 * half) * ROWS - e_width
    if not inside:
        q_height = halo * ROWS
        for q_from in (0, q_in.shape[0] - q_height):
            q_to = q_rows.start + q_from
            qb[q_to : q_to + q_height, :] = q_in[q_from : q_from + q_height, :]
        for e_from, e_to in ((0, e_low), (e_width, e_high)):
            e_first = e_in[e_from : e_from + e_width, :]
            ef[e_to : e_to + e_width, :] = e_first
            mb[e_to : e_to + e_width, :] = e_first.astype(bf16)

    copies = []
    base = canvas.shape[-1] - columns if cut else 0
    limit = canvas.shape[-1] if cut else columns - LANES
    top = ITERS * 2 * half

    def wide(tile):
        return min(TILE, columns - tile * TILE)

    def columns_of(tile):
        return slice(tile * TILE, tile * TILE + wide(tile))

    def within(tile):
        return slice(LANES + tile * TILE, LANES + tile * TILE + wide(tile))

    def around(tile):
        return slice(tile * TILE, tile * TILE + wide(tile) + 2 * LANES)

    def lateral(stage, source, matrix, tile):
        band = matrix[: wide(tile) + 2 * LANES, : wide(tile)]
        height = sum(count for _, count in flat(stage)) * ROWS
        whole = jnp.dot(source[:height, around(tile)], band, preferred_element_type=f32)
        start = 0
        for groups in stage:
            rows = rows_of(groups)
            stop = start + rows.stop - rows.start
            yield groups, rows, whole[start:stop]
            start = stop

    def rows_of(groups):
        return slice(groups[0][0] * ROWS, (groups[-1][0] + groups[-1][1]) * ROWS)

    def axial(matrices, skip, stage, source, target, tile):
        place = 0
        for number, (first, count) in enumerate(flat(stage)):
            low = (first - half) * ROWS
            high = (first + count + half) * ROWS
            r = jnp.dot(
                matrices[skip + number, : count * ROWS, : high - low],
                source[low:high, columns_of(tile)],
                preferred_element_type=f32,
            )
            target[place : place + count * ROWS, within(tile)] = r.astype(bf16)
            place += count * ROWS

    def calls(sweep):
        ahead, back = plan[2 * sweep], plan[2 * sweep + 1]
        skip_ahead = sum(len(flat(stage)) for stage in plan[0 : 2 * sweep : 2])
        skip_back = sum(len(flat(stage)) for stage in plan[1 : 2 * sweep : 2])
        final = sweep == ITERS - 1

        def ratio(tile):
            cols = columns_of(tile)
            for _, rows, blurred in lateral(ahead, pad, tl, tile):
                b = blurred + BACKGROUND
                guess = pl.reciprocal(b, approx=True)
                guess = guess * (2.0 - b * guess)
                qb[rows, cols] = (mf[rows, cols] * guess).astype(bf16)

        def update(tile):
            cols = columns_of(tile)
            for groups, rows, d in lateral(back, pad_back, tm, tile):
                e = (mf if sweep == 0 else ef)[rows, cols] * d
                if not final:
                    ef[rows, cols] = e
                    mb[rows, cols] = e.astype(bf16)
                    continue
                start = base + tile * TILE
                drop = cut if tile == 0 else 0
                keep = min(wide(tile), limit - start)
                if keep > drop:
                    first, count = groups[0][0] - top, e.shape[0] // ROWS
                    where = (slice(first, first + count), slice(None))
                    here = slice(tile * TILE + drop, tile * TILE + keep)
                    done[where + (here,)] = e.reshape(-1, ROWS, wide(tile))[:, :, drop:keep].astype(bf16)
                    copy = pltpu.make_async_copy(
                        done.at[where + (here,)],
                        canvas.at[where + (slice(start + drop, start + keep),)],
                        sems.at[len(copies)],
                    )
                    copy.start()
                    copies.append(copy)

        return (
            (0, functools.partial(axial, g, skip_ahead, ahead, mb, pad)),
            (2, ratio),
            (3, functools.partial(axial, gt, skip_back, back, qb, pad_back)),
            (5, update),
        )

    waves = [(6 * sweep + lag, call) for sweep in range(ITERS) for lag, call in calls(sweep)]
    for step in range(tiles + max(lag for lag, _ in waves)):
        for lag, call in waves:
            if 0 <= step - lag < tiles:
                call(step - lag)

    if inside:
        q_out[...] = qb[q_rows, :]
        e_out[:e_width, :] = ef[e_low : e_low + e_width, :]
        e_out[e_width:, :] = ef[e_high : e_high + e_width, :]
    for copy in copies:
        copy.wait()


def restore(parts, matrices, state, canvas, plan, inside, planes, half, columns):
    later = len(parts) > 1
    width = parts[-1][0].shape[-1] + (2 * LANES if later else 0)
    halo = 2 * ITERS * half
    height = (planes + 2 * halo) * ROWS
    bf16 = jnp.bfloat16
    vmem = pl.BlockSpec(memory_space=pltpu.VMEM)
    hbm = pl.BlockSpec(memory_space=pltpu.HBM)
    operands = [array for part in parts for array in part] + [*matrices, *state]
    specs = [vmem] * len(operands)
    aliases = {}
    if canvas is not None:
        aliases = {len(operands): 0}
        operands.append(canvas)
        specs.append(hbm)
    tallest = max(sum(count for _, count in flat(stage)) for stage in plan) * ROWS
    results = [jax.ShapeDtypeStruct((planes, ROWS, columns), bf16)]
    if inside:
        results += [
            jax.ShapeDtypeStruct(((planes - 2 * half) * ROWS, width), bf16),
            jax.ShapeDtypeStruct((2 * half * (2 * ITERS - 2) * ROWS, width), jnp.float32),
        ]
    return pl.pallas_call(
        functools.partial(
            restore_kernel, plan, inside, half, [len(part) for part in parts], LANES if later else 0
        ),
        in_specs=specs,
        out_specs=[hbm] + [vmem] * (len(results) - 1),
        out_shape=results,
        input_output_aliases=aliases,
        scratch_shapes=[
            pltpu.VMEM((height, width), jnp.float32),
            pltpu.VMEM((height, width), jnp.float32),
            pltpu.VMEM((height, width), bf16),
            pltpu.VMEM((height, width), bf16),
            pltpu.VMEM((tallest, width + 2 * LANES), bf16),
            pltpu.VMEM((tallest, width + 2 * LANES), bf16),
            pltpu.VMEM((planes, ROWS, width), bf16),
            pltpu.SemaphoreType.DMA((-(-width // TILE) * (1 if inside else 2),)),
        ],
        compiler_params=pltpu.CompilerParams(vmem_limit_bytes=RESTORE_VMEM),
        cost_estimate=pl.CostEstimate(
            flops=5_000_000_000, bytes_accessed=8_000_000, transcendentals=0
        ),
        name="inside" if inside else "ends",
    )(*operands)


def local(
    raw_frames,
    frame_order,
    dark_frame,
    flat_gain,
    stripe_band,
    shear_offset,
    shear_fraction,
    band_index,
    psf_bank,
    lateral_psf,
):
    half = psf_bank.shape[1] // 2
    planes = shear_offset.shape[0]
    columns = raw_frames.shape[-1]
    halo = 2 * ITERS * half
    plans = stages(planes, half)
    count = lax.axis_size("cam")
    forward = [(i, i + 1) for i in range(count - 1)]
    backward = [(i + 1, i) for i in range(count - 1)]
    *axial, forward_lateral, backward_lateral = bands(psf_bank, lateral_psf, band_index, planes, halo)
    matrices = [
        (*axial[2 * which : 2 * which + 2], forward_lateral, backward_lateral) for which in range(2)
    ]
    depth = halo // 2
    first_piece = frame_side(
        raw_frames, frame_order, dark_frame, flat_gain, stripe_band, shear_offset, shear_fraction, 0, SPLIT
    )
    first_piece, later_order = lax.optimization_barrier((first_piece, frame_order))
    second_piece = frame_side(
        raw_frames, later_order, dark_frame, flat_gain, stripe_band, shear_offset, shear_fraction,
        SPLIT, columns,
    )
    def exchange(piece):
        return lax.all_to_all(piece, "brick", split_axis=0, concat_axis=0, tiled=True)

    def with_halo(centre):
        low = lax.ppermute(centre[-depth:], "cam", forward)
        high = lax.ppermute(centre[:depth], "cam", backward)
        return low, centre, high

    def inside(parts, canvas):
        centres = [(centre,) for _, centre, _ in parts]
        canvas, *state = restore(
            centres, matrices[0], (), canvas, plans[0], True, planes, half, columns
        )
        return canvas, state

    def ends(parts, state, canvas):
        return restore(
            parts, matrices[1], state, canvas, plans[1], False, planes, half, columns
        )[0]

    first, second_piece, matrices = lax.optimization_barrier(
        (exchange(first_piece), second_piece, matrices)
    )
    first_part = with_halo(first)
    canvas, first_state = inside([first_part], None)
    second, first_state = lax.optimization_barrier((exchange(second_piece), first_state))
    second_part = with_halo(second)
    canvas, second_state = inside([first_part, second_part], canvas)
    canvas = ends([first_part], first_state, canvas)
    return ends([first_part, second_part], second_state, canvas)


def solution(mesh):
    placed = (
        P(("cam", "brick"), None, None),
        P(("cam", "brick"), None),
        P(),
        P(),
        P(),
        P("cam"),
        P("cam"),
        P(),
        P(),
        P(),
    )
    return jax.shard_map(
        local, mesh=mesh, in_specs=placed, out_specs=P("cam", "brick", None), check_vma=False
    )
```

```python
import functools

import jax
import jax.numpy as jnp
from jax import lax
from jax.experimental import pallas as pl
from jax.experimental.pallas import tpu as pltpu
from jax.sharding import PartitionSpec as P

SHEAR = 512
ITERS = 2
BACKGROUND = 1.0

LANES = 128
TILE = 256
ROWS = 8
BLOCK_ROWS = 128
LEAD = SHEAR // LANES + 1
SPLIT = 1280
VMEM = 60 * 1024 * 1024
BANDS_VMEM = 20 * 1024 * 1024
RESTORE_VMEM = 26 * 1024 * 1024
LATER_VMEM = 20 * 1024 * 1024
GROUP = 20
SPAN = 32


def frame_kernel(
    first, count,
    order_ref, offset_ref, fraction_ref,
    raw_prev, raw_main, raw_next,
    dark_prev, dark_main, dark_next,
    gain_prev, gain_main, gain_next,
    band_ref, out_ref, scratch, level,
):
    step = pl.program_id(0)
    steps = pl.num_programs(0)
    rows = BLOCK_ROWS + 16
    brick = lax.axis_index("brick")
    f32 = jnp.float32
    bf16 = jnp.bfloat16
    base = first - LEAD

    @pl.when(step == 0)
    def _():
        if base < 0:
            scratch[:, :, : -base * LANES] = jnp.zeros((2, BLOCK_ROWS, -base * LANES), f32)

    has_prev = (step > 0).astype(f32)
    has_next = (step < steps - 1).astype(f32)
    frames = [jnp.where(order_ref[0, 0] == place, 0, 1) for place in range(2)]

    used = range(max(base, 0), first + count)
    for tile in used:
        cols = pl.ds(tile * LANES, LANES)
        for part, keep, start in ((0, slice(8, 16), 0), (1, slice(None), 8), (2, slice(0, 8), rows - 8)):
            dark = (dark_prev, dark_main, dark_next)[part][:, cols].astype(f32)[keep]
            gain = (gain_prev, gain_main, gain_next)[part][:, cols].astype(f32)[keep]
            if part != 1:
                gain = gain * (has_prev, None, has_next)[part]
            raw = (raw_prev, raw_main, raw_next)[part]
            for place in range(2):
                f = (raw[frames[place], :, cols].astype(f32)[keep] - dark) * gain
                level[place, tile - used[0], start : start + f.shape[0], :] = f

    zero = jnp.minimum(step, 0)
    taps = band_ref.shape[0]
    for tile in used:
        band = band_ref[:, pl.ds(tile * LANES, LANES)]
        for place in range(2):
            here = tile - used[0]
            out = level[place, here, 8 : 8 + BLOCK_ROWS, :] * (1.0 + band[taps // 2 : taps // 2 + 1])
            for tap in range(taps):
                if tap != taps // 2:
                    shifted = level[place, here, pl.ds(zero + 8 + tap - taps // 2, BLOCK_ROWS), :]
                    out = out + band[tap : tap + 1] * shifted
            scratch[place, :, pl.ds((tile - base) * LANES, LANES)] = out.astype(bf16).astype(f32)

    lane = lax.broadcasted_iota(jnp.int32, (BLOCK_ROWS, LANES), 1)
    bricks = BLOCK_ROWS // ROWS
    for place in range(2):
        amount = offset_ref[brick * 2 + place]
        weight = fraction_ref[brick * 2 + place]
        whole = amount // LANES
        part = amount % LANES
        near_mask = lane < part
        far_mask = lane < part + 1

        def turned(tile):
            start = (tile - base - whole) * LANES
            x = scratch[place, :, pl.ds(pl.multiple_of(start, LANES), LANES)]
            return (1.0 - weight) * pltpu.roll(x, part, 1), weight * pltpu.roll(x, (part + 1) % LANES, 1)

        last = turned(first - 1)
        for tile in range(first, first + count):
            now = turned(tile)
            mixed = jnp.where(near_mask, last[0], now[0]) + jnp.where(far_mask, last[1], now[1])
            last = now
            out_ref[:, place * ROWS : (place + 1) * ROWS, pl.ds((tile - first) * LANES, LANES)] = (
                mixed.reshape(bricks, ROWS, LANES).astype(bf16)
            )


def frame_side(raw, order, dark, gain, band, offset, fraction, lo, hi):
    _, frame_rows, columns = raw.shape
    steps = frame_rows // BLOCK_ROWS
    bricks = frame_rows // ROWS
    per = BLOCK_ROWS // 16
    last = frame_rows // 16 - 1
    smem = pl.BlockSpec(memory_space=pltpu.SMEM)
    first, count = lo // LANES, (hi - lo) // LANES
    if lo == 0:
        columns = hi

    def three(lead):
        zeros = (0,) * len(lead)
        return [
            pl.BlockSpec(lead + (16, columns), lambda i: zeros + (jnp.maximum(per * i - 1, 0), 0)),
            pl.BlockSpec(lead + (BLOCK_ROWS, columns), lambda i: zeros + (i, 0)),
            pl.BlockSpec(lead + (16, columns), lambda i: zeros + (jnp.minimum(per * i + per, last), 0)),
        ]

    return pl.pallas_call(
        functools.partial(frame_kernel, first, count),
        grid=(steps,),
        in_specs=[smem, smem, smem]
        + three((2,)) + three(()) + three(())
        + [pl.BlockSpec((band.shape[0], columns), lambda i: (0, 0))],
        out_specs=pl.BlockSpec((BLOCK_ROWS // ROWS, 2 * ROWS, hi - lo), lambda i: (i, 0, 0)),
        out_shape=jax.ShapeDtypeStruct((bricks, 2 * ROWS, hi - lo), jnp.bfloat16),
        scratch_shapes=[
            pltpu.VMEM((2, BLOCK_ROWS, (LEAD + count) * LANES), jnp.float32),
            pltpu.VMEM((2, min(first, LEAD) + count, BLOCK_ROWS + 16, LANES), jnp.float32),
        ],
        compiler_params=pltpu.CompilerParams(vmem_limit_bytes=VMEM if lo == 0 else LATER_VMEM),
        cost_estimate=pl.CostEstimate(
            flops=8_000_000_000, bytes_accessed=6_500_000, transcendentals=0
        ),
        name="frame_side",
    )(order, offset, fraction, raw, raw, raw, dark, dark, dark, gain, gain, gain, band)


def stages(planes, half):
    halo = 2 * ITERS * half
    total = planes + 2 * halo

    def cut(lo, hi, most):
        parts = -(-(hi - lo) // most)
        size = -(-(hi - lo) // (2 * parts)) * 2
        return [(at, min(size, hi - at)) for at in range(lo, hi, size)]

    inner, outer = [], []
    for stage in range(1, 2 * ITERS + 1):
        reach = stage * half
        lo, hi = halo + reach, total - halo - reach
        inner.append([cut(lo, hi, GROUP)])
        outer.append([cut(reach, lo, GROUP), cut(hi, total - reach, GROUP)])
    return inner, outer


def flat(stage):
    return [group for groups in stage for group in groups]


def bands_kernel(taps, lat_taps, plans, psf_ref, lateral_ref, index_ref, *outs):
    matrices, (tl_ref, tm_ref) = outs[:-2], outs[-2:]
    f32 = jnp.float32
    bf16 = jnp.bfloat16
    half = taps // 2
    width = SPAN * ROWS
    index = index_ref[...]
    raw = []
    for tap in range(taps):
        value = jnp.zeros(index.shape, f32)
        for kernel in range(psf_ref.shape[0]):
            value = jnp.where(index == kernel, psf_ref[kernel, tap], value)
        raw.append(value)
    total = functools.reduce(lambda a, b: a + b, raw)
    total = jnp.where(total > 0.0, total, 1.0)
    unit = [value / total for value in raw]
    row = lax.broadcasted_iota(jnp.int32, (width, width), 0)
    col = lax.broadcasted_iota(jnp.int32, (width, width), 1)

    def banded(start, gap, order):
        m = jnp.zeros((width, width), f32)
        for tap in range(taps):
            values = unit[tap][:, start * ROWS : start * ROWS + width]
            m = jnp.where(gap == ROWS * order(tap), values, m)
        return m

    for which, plan in enumerate(plans):
        slot = [0, 0]
        for number, stage in enumerate(plan):
            kind = number % 2
            target = matrices[2 * which + kind]
            for at, _ in flat(stage):
                if kind == 0:
                    m = banded(at, row - col, lambda tap: tap).T
                else:
                    m = banded(at - half, col - row, lambda tap: 2 * half - tap)
                target[slot[kind]] = m[: GROUP * ROWS].astype(bf16)
                slot[kind] += 1

    lateral_total = lateral_ref[0]
    for tap in range(1, lat_taps):
        lateral_total = lateral_total + lateral_ref[tap]
    k = lax.broadcasted_iota(jnp.int32, tl_ref.shape, 0)
    j = lax.broadcasted_iota(jnp.int32, tl_ref.shape, 1)
    place = k - LANES - j + lat_taps // 2
    forward = jnp.zeros(tl_ref.shape, f32)
    backward = jnp.zeros(tl_ref.shape, f32)
    for tap in range(lat_taps):
        forward = jnp.where(place == tap, lateral_ref[tap], forward)
        backward = jnp.where(place == lat_taps - 1 - tap, lateral_ref[tap], backward)
    scale = jnp.full((1, TILE), lateral_total, f32)
    tl_ref[...] = (forward / scale).astype(bf16)
    tm_ref[...] = (backward / scale).astype(bf16)


def bands(psf_bank, lateral_psf, band_index, planes, halo):
    plans = stages(planes, psf_bank.shape[1] // 2)
    spread = jnp.pad(band_index, (halo, halo + SPAN), constant_values=-1)
    first = lax.axis_index("cam") * planes
    length = planes + 2 * halo + SPAN
    mine = lax.dynamic_slice_in_dim(spread, first, length, 0)
    index = jnp.broadcast_to(mine[:, None], (length, ROWS)).reshape(1, length * ROWS)
    smem = pl.BlockSpec(memory_space=pltpu.SMEM)
    vmem = pl.BlockSpec(memory_space=pltpu.VMEM)
    counts = [
        sum(len(flat(stage)) for stage in plan[kind::2]) for plan in plans for kind in range(2)
    ]
    strip = jax.ShapeDtypeStruct((TILE + 2 * LANES, TILE), jnp.bfloat16)
    return pl.pallas_call(
        functools.partial(bands_kernel, psf_bank.shape[1], lateral_psf.shape[0], plans),
        in_specs=[smem, smem, vmem],
        out_specs=[vmem] * (len(counts) + 2),
        out_shape=[
            jax.ShapeDtypeStruct((n, GROUP * ROWS, SPAN * ROWS), jnp.bfloat16) for n in counts
        ]
        + [strip, strip],
        compiler_params=pltpu.CompilerParams(vmem_limit_bytes=BANDS_VMEM),
        cost_estimate=pl.CostEstimate(
            flops=2_000_000_000, bytes_accessed=2_000_000, transcendentals=0
        ),
        name="bands",
    )(psf_bank, lateral_psf, index)


def restore_kernel(plan, inside, half, counts, cut, *refs):
    parts = []
    for count in counts:
        parts.append(refs[:count])
        refs = refs[count:]
    g, gt, tl, tm = refs[:4]
    refs = refs[4:]
    f32 = jnp.float32
    bf16 = jnp.bfloat16
    halo = 2 * ITERS * half
    if not inside:
        q_in, e_in = refs[:2]
        refs = refs[2:]
    buffers = refs[-8:]
    mf, ef, mb, qb, pad, pad_back, done, sems = buffers
    if inside:
        canvas, q_out, e_out = refs[-11:-8]
    else:
        canvas = refs[-9]
    size, columns = mf.shape
    total = size // ROWS
    tiles = -(-columns // TILE)

    for buffer in (pad, pad_back):
        edge = jnp.zeros((buffer.shape[0], LANES), bf16)
        buffer[:, :LANES] = edge
        buffer[:, LANES + columns :] = edge

    at_column = 0
    reach = (2 * ITERS - 1) * half
    for part in parts:
        width = part[0].shape[-1] if part is parts[-1] else 2 * LANES
        skip = part[0].shape[-1] - width
        if inside:
            loads = [(part[0], 0, part[0].shape[0], halo)]
        else:
            low, own, high = part
            count = own.shape[0]
            loads = [
                (low, 0, low.shape[0], 0),
                (own, 0, reach // 2, halo),
                (own, count - reach // 2, count, total - halo - reach),
                (high, 0, high.shape[0], total - halo),
            ]
        for ref, lo, hi, plane in loads:
            rows = slice(plane * ROWS, plane * ROWS + (hi - lo) * ref.shape[1])
            for col in range(0, width, TILE):
                end = min(col + TILE, width)
                whole = ref[lo:hi, :, skip + col : skip + end].reshape(-1, end - col)
                there = slice(at_column + col, at_column + end)
                mb[rows, there] = whole
                mf[rows, there] = whole.astype(f32)
        at_column += width

    q_rows = slice((halo + half) * ROWS, (total - halo - half) * ROWS)
    e_width = half * (2 * ITERS - 2) * ROWS
    e_low = (halo + 2 * half) * ROWS
    e_high = (total - halo - 2 * half) * ROWS - e_width
    if not inside:
        q_height = halo * ROWS
        for q_from in (0, q_in.shape[0] - q_height):
            q_to = q_rows.start + q_from
            qb[q_to : q_to + q_height, :] = q_in[q_from : q_from + q_height, :]
        for e_from, e_to in ((0, e_low), (e_width, e_high)):
            e_first = e_in[e_from : e_from + e_width, :]
            ef[e_to : e_to + e_width, :] = e_first
            mb[e_to : e_to + e_width, :] = e_first.astype(bf16)

    copies = []
    base = canvas.shape[-1] - columns if cut else 0
    limit = canvas.shape[-1] if cut else columns - LANES
    top = ITERS * 2 * half

    def wide(tile):
        return min(TILE, columns - tile * TILE)

    def columns_of(tile):
        return slice(tile * TILE, tile * TILE + wide(tile))

    def within(tile):
        return slice(LANES + tile * TILE, LANES + tile * TILE + wide(tile))

    def around(tile):
        return slice(tile * TILE, tile * TILE + wide(tile) + 2 * LANES)

    def lateral(stage, source, matrix, tile):
        band = matrix[: wide(tile) + 2 * LANES, : wide(tile)]
        height = sum(count for _, count in flat(stage)) * ROWS
        whole = jnp.dot(source[:height, around(tile)], band, preferred_element_type=f32)
        start = 0
        for groups in stage:
            rows = rows_of(groups)
            stop = start + rows.stop - rows.start
            yield groups, rows, whole[start:stop]
            start = stop

    def rows_of(groups):
        return slice(groups[0][0] * ROWS, (groups[-1][0] + groups[-1][1]) * ROWS)

    def axial(matrices, skip, stage, source, target, tile):
        place = 0
        for number, (first, count) in enumerate(flat(stage)):
            low = (first - half) * ROWS
            high = (first + count + half) * ROWS
            r = jnp.dot(
                matrices[skip + number, : count * ROWS, : high - low],
                source[low:high, columns_of(tile)],
                preferred_element_type=f32,
            )
            target[place : place + count * ROWS, within(tile)] = r.astype(bf16)
            place += count * ROWS

    def calls(sweep):
        ahead, back = plan[2 * sweep], plan[2 * sweep + 1]
        skip_ahead = sum(len(flat(stage)) for stage in plan[0 : 2 * sweep : 2])
        skip_back = sum(len(flat(stage)) for stage in plan[1 : 2 * sweep : 2])
        final = sweep == ITERS - 1

        def ratio(tile):
            cols = columns_of(tile)
            for _, rows, blurred in lateral(ahead, pad, tl, tile):
                b = blurred + BACKGROUND
                guess = pl.reciprocal(b, approx=True)
                guess = guess * (2.0 - b * guess)
                qb[rows, cols] = (mf[rows, cols] * guess).astype(bf16)

        def update(tile):
            cols = columns_of(tile)
            for groups, rows, d in lateral(back, pad_back, tm, tile):
                e = (mf if sweep == 0 else ef)[rows, cols] * d
                if not final:
                    ef[rows, cols] = e
                    mb[rows, cols] = e.astype(bf16)
                    continue
                start = base + tile * TILE
                drop = cut if tile == 0 else 0
                keep = min(wide(tile), limit - start)
                if keep > drop:
                    first, count = groups[0][0] - top, e.shape[0] // ROWS
                    where = (slice(first, first + count), slice(None))
                    here = slice(tile * TILE + drop, tile * TILE + keep)
                    done[where + (here,)] = e.reshape(-1, ROWS, wide(tile))[:, :, drop:keep].astype(bf16)
                    copy = pltpu.make_async_copy(
                        done.at[where + (here,)],
                        canvas.at[where + (slice(start + drop, start + keep),)],
                        sems.at[len(copies)],
                    )
                    copy.start()
                    copies.append(copy)

        return (
            (0, functools.partial(axial, g, skip_ahead, ahead, mb, pad)),
            (2, ratio),
            (3, functools.partial(axial, gt, skip_back, back, qb, pad_back)),
            (5, update),
        )

    waves = [(6 * sweep + lag, call) for sweep in range(ITERS) for lag, call in calls(sweep)]
    for step in range(tiles + max(lag for lag, _ in waves)):
        for lag, call in waves:
            if 0 <= step - lag < tiles:
                call(step - lag)

    if inside:
        q_out[...] = qb[q_rows, :]
        e_out[:e_width, :] = ef[e_low : e_low + e_width, :]
        e_out[e_width:, :] = ef[e_high : e_high + e_width, :]
    for copy in copies:
        copy.wait()


def restore(parts, matrices, state, canvas, plan, inside, planes, half, columns):
    later = len(parts) > 1
    width = parts[-1][0].shape[-1] + (2 * LANES if later else 0)
    halo = 2 * ITERS * half
    height = (planes + 2 * halo) * ROWS
    bf16 = jnp.bfloat16
    vmem = pl.BlockSpec(memory_space=pltpu.VMEM)
    hbm = pl.BlockSpec(memory_space=pltpu.HBM)
    operands = [array for part in parts for array in part] + [*matrices, *state]
    specs = [vmem] * len(operands)
    aliases = {}
    if canvas is not None:
        aliases = {len(operands): 0}
        operands.append(canvas)
        specs.append(hbm)
    tallest = max(sum(count for _, count in flat(stage)) for stage in plan) * ROWS
    results = [jax.ShapeDtypeStruct((planes, ROWS, columns), bf16)]
    if inside:
        results += [
            jax.ShapeDtypeStruct(((planes - 2 * half) * ROWS, width), bf16),
            jax.ShapeDtypeStruct((2 * half * (2 * ITERS - 2) * ROWS, width), jnp.float32),
        ]
    return pl.pallas_call(
        functools.partial(
            restore_kernel, plan, inside, half, [len(part) for part in parts], LANES if later else 0
        ),
        in_specs=specs,
        out_specs=[hbm] + [vmem] * (len(results) - 1),
        out_shape=results,
        input_output_aliases=aliases,
        scratch_shapes=[
            pltpu.VMEM((height, width), jnp.float32),
            pltpu.VMEM((height, width), jnp.float32),
            pltpu.VMEM((height, width), bf16),
            pltpu.VMEM((height, width), bf16),
            pltpu.VMEM((tallest, width + 2 * LANES), bf16),
            pltpu.VMEM((tallest, width + 2 * LANES), bf16),
            pltpu.VMEM((planes, ROWS, width), bf16),
            pltpu.SemaphoreType.DMA((-(-width // TILE) * (1 if inside else 2),)),
        ],
        compiler_params=pltpu.CompilerParams(vmem_limit_bytes=RESTORE_VMEM),
        cost_estimate=pl.CostEstimate(
            flops=5_000_000_000, bytes_accessed=8_000_000, transcendentals=0
        ),
        name="inside" if inside else "ends",
    )(*operands)


def local(
    raw_frames,
    frame_order,
    dark_frame,
    flat_gain,
    stripe_band,
    shear_offset,
    shear_fraction,
    band_index,
    psf_bank,
    lateral_psf,
):
    half = psf_bank.shape[1] // 2
    planes = shear_offset.shape[0]
    columns = raw_frames.shape[-1]
    halo = 2 * ITERS * half
    plans = stages(planes, half)
    count = lax.axis_size("cam")
    forward = [(i, i + 1) for i in range(count - 1)]
    backward = [(i + 1, i) for i in range(count - 1)]
    *axial, forward_lateral, backward_lateral = bands(psf_bank, lateral_psf, band_index, planes, halo)
    matrices = [
        (*axial[2 * which : 2 * which + 2], forward_lateral, backward_lateral) for which in range(2)
    ]
    depth = halo // 2
    first_piece = frame_side(
        raw_frames, frame_order, dark_frame, flat_gain, stripe_band, shear_offset, shear_fraction, 0, SPLIT
    )
    first_piece, later_order = lax.optimization_barrier((first_piece, frame_order))
    second_piece = frame_side(
        raw_frames, later_order, dark_frame, flat_gain, stripe_band, shear_offset, shear_fraction,
        SPLIT, columns,
    )
    def exchange(piece):
        return lax.all_to_all(piece, "brick", split_axis=0, concat_axis=0, tiled=True)

    def with_halo(centre):
        low = lax.ppermute(centre[-depth:], "cam", forward)
        high = lax.ppermute(centre[:depth], "cam", backward)
        return low, centre, high

    def inside(parts, canvas):
        centres = [(centre,) for _, centre, _ in parts]
        canvas, *state = restore(
            centres, matrices[0], (), canvas, plans[0], True, planes, half, columns
        )
        return canvas, state

    def ends(parts, state, canvas):
        return restore(
            parts, matrices[1], state, canvas, plans[1], False, planes, half, columns
        )[0]

    first, second_piece, matrices = lax.optimization_barrier(
        (exchange(first_piece), second_piece, matrices)
    )
    first_part = with_halo(first)
    canvas, first_state = inside([first_part], None)
    second, first_state = lax.optimization_barrier((exchange(second_piece), first_state))
    second_part = with_halo(second)
    canvas, second_state = inside([first_part, second_part], canvas)
    canvas = ends([first_part], first_state, canvas)
    return ends([first_part, second_part], second_state, canvas)


def solution(mesh):
    placed = (
        P(("cam", "brick"), None, None),
        P(("cam", "brick"), None),
        P(),
        P(),
        P(),
        P("cam"),
        P("cam"),
        P(),
        P(),
        P(),
    )
    return jax.shard_map(
        local, mesh=mesh, in_specs=placed, out_specs=P("cam", "brick", None), check_vma=False
    )
```

```python
import functools

import jax
import jax.numpy as jnp
from jax import lax
from jax.experimental import pallas as pl
from jax.experimental.pallas import tpu as pltpu
from jax.sharding import PartitionSpec as P

SHEAR = 512
ITERS = 2
BACKGROUND = 1.0

LANES = 128
TILE = 256
ROWS = 8
BLOCK_ROWS = 128
LEAD = SHEAR // LANES + 1
SPLIT = 1024
VMEM = 60 * 1024 * 1024
BANDS_VMEM = 20 * 1024 * 1024
RESTORE_VMEM = 26 * 1024 * 1024
LATER_VMEM = 20 * 1024 * 1024
GROUP = 20
SPAN = 32


def frame_kernel(
    first, count,
    order_ref, offset_ref, fraction_ref,
    raw_prev, raw_main, raw_next,
    dark_prev, dark_main, dark_next,
    gain_prev, gain_main, gain_next,
    band_ref, out_ref, scratch, level,
):
    step = pl.program_id(0)
    steps = pl.num_programs(0)
    rows = BLOCK_ROWS + 16
    brick = lax.axis_index("brick")
    f32 = jnp.float32
    bf16 = jnp.bfloat16
    base = first - LEAD

    @pl.when(step == 0)
    def _():
        if base < 0:
            scratch[:, :, : -base * LANES] = jnp.zeros((2, BLOCK_ROWS, -base * LANES), f32)

    has_prev = (step > 0).astype(f32)
    has_next = (step < steps - 1).astype(f32)
    frames = [jnp.where(order_ref[0, 0] == place, 0, 1) for place in range(2)]

    used = range(max(base, 0), first + count)
    for tile in used:
        cols = pl.ds(tile * LANES, LANES)
        for part, keep, start in ((0, slice(8, 16), 0), (1, slice(None), 8), (2, slice(0, 8), rows - 8)):
            dark = (dark_prev, dark_main, dark_next)[part][:, cols].astype(f32)[keep]
            gain = (gain_prev, gain_main, gain_next)[part][:, cols].astype(f32)[keep]
            if part != 1:
                gain = gain * (has_prev, None, has_next)[part]
            raw = (raw_prev, raw_main, raw_next)[part]
            for place in range(2):
                f = (raw[frames[place], :, cols].astype(f32)[keep] - dark) * gain
                level[place, tile - used[0], start : start + f.shape[0], :] = f

    zero = jnp.minimum(step, 0)
    taps = band_ref.shape[0]
    for tile in used:
        band = band_ref[:, pl.ds(tile * LANES, LANES)]
        for place in range(2):
            here = tile - used[0]
            out = level[place, here, 8 : 8 + BLOCK_ROWS, :] * (1.0 + band[taps // 2 : taps // 2 + 1])
            for tap in range(taps):
                if tap != taps // 2:
                    shifted = level[place, here, pl.ds(zero + 8 + tap - taps // 2, BLOCK_ROWS), :]
                    out = out + band[tap : tap + 1] * shifted
            scratch[place, :, pl.ds((tile - base) * LANES, LANES)] = out.astype(bf16).astype(f32)

    lane = lax.broadcasted_iota(jnp.int32, (BLOCK_ROWS, LANES), 1)
    bricks = BLOCK_ROWS // ROWS
    for place in range(2):
        amount = offset_ref[brick * 2 + place]
        weight = fraction_ref[brick * 2 + place]
        whole = amount // LANES
        part = amount % LANES
        near_mask = lane < part
        far_mask = lane < part + 1

        def turned(tile):
            start = (tile - base - whole) * LANES
            x = scratch[place, :, pl.ds(pl.multiple_of(start, LANES), LANES)]
            return (1.0 - weight) * pltpu.roll(x, part, 1), weight * pltpu.roll(x, (part + 1) % LANES, 1)

        last = turned(first - 1)
        for tile in range(first, first + count):
            now = turned(tile)
            mixed = jnp.where(near_mask, last[0], now[0]) + jnp.where(far_mask, last[1], now[1])
            last = now
            out_ref[:, place * ROWS : (place + 1) * ROWS, pl.ds((tile - first) * LANES, LANES)] = (
                mixed.reshape(bricks, ROWS, LANES).astype(bf16)
            )


def frame_side(raw, order, dark, gain, band, offset, fraction, lo, hi):
    _, frame_rows, columns = raw.shape
    steps = frame_rows // BLOCK_ROWS
    bricks = frame_rows // ROWS
    per = BLOCK_ROWS // 16
    last = frame_rows // 16 - 1
    smem = pl.BlockSpec(memory_space=pltpu.SMEM)
    first, count = lo // LANES, (hi - lo) // LANES
    if lo == 0:
        columns = hi

    def three(lead):
        zeros = (0,) * len(lead)
        return [
            pl.BlockSpec(lead + (16, columns), lambda i: zeros + (jnp.maximum(per * i - 1, 0), 0)),
            pl.BlockSpec(lead + (BLOCK_ROWS, columns), lambda i: zeros + (i, 0)),
            pl.BlockSpec(lead + (16, columns), lambda i: zeros + (jnp.minimum(per * i + per, last), 0)),
        ]

    return pl.pallas_call(
        functools.partial(frame_kernel, first, count),
        grid=(steps,),
        in_specs=[smem, smem, smem]
        + three((2,)) + three(()) + three(())
        + [pl.BlockSpec((band.shape[0], columns), lambda i: (0, 0))],
        out_specs=pl.BlockSpec((BLOCK_ROWS // ROWS, 2 * ROWS, hi - lo), lambda i: (i, 0, 0)),
        out_shape=jax.ShapeDtypeStruct((bricks, 2 * ROWS, hi - lo), jnp.bfloat16),
        scratch_shapes=[
            pltpu.VMEM((2, BLOCK_ROWS, (LEAD + count) * LANES), jnp.float32),
            pltpu.VMEM((2, min(first, LEAD) + count, BLOCK_ROWS + 16, LANES), jnp.float32),
        ],
        compiler_params=pltpu.CompilerParams(vmem_limit_bytes=VMEM if lo == 0 else LATER_VMEM),
        cost_estimate=pl.CostEstimate(
            flops=8_000_000_000, bytes_accessed=6_500_000, transcendentals=0
        ),
        name="frame_side",
    )(order, offset, fraction, raw, raw, raw, dark, dark, dark, gain, gain, gain, band)


def stages(planes, half):
    halo = 2 * ITERS * half
    total = planes + 2 * halo

    def cut(lo, hi, most):
        parts = -(-(hi - lo) // most)
        size = -(-(hi - lo) // (2 * parts)) * 2
        return [(at, min(size, hi - at)) for at in range(lo, hi, size)]

    inner, outer = [], []
    for stage in range(1, 2 * ITERS + 1):
        reach = stage * half
        lo, hi = halo + reach, total - halo - reach
        inner.append([cut(lo, hi, GROUP)])
        outer.append([cut(reach, lo, GROUP), cut(hi, total - reach, GROUP)])
    return inner, outer


def flat(stage):
    return [group for groups in stage for group in groups]


def bands_kernel(taps, lat_taps, plans, psf_ref, lateral_ref, index_ref, *outs):
    matrices, (tl_ref, tm_ref) = outs[:-2], outs[-2:]
    f32 = jnp.float32
    bf16 = jnp.bfloat16
    half = taps // 2
    width = SPAN * ROWS
    index = index_ref[...]
    raw = []
    for tap in range(taps):
        value = jnp.zeros(index.shape, f32)
        for kernel in range(psf_ref.shape[0]):
            value = jnp.where(index == kernel, psf_ref[kernel, tap], value)
        raw.append(value)
    total = functools.reduce(lambda a, b: a + b, raw)
    total = jnp.where(total > 0.0, total, 1.0)
    unit = [value / total for value in raw]
    row = lax.broadcasted_iota(jnp.int32, (width, width), 0)
    col = lax.broadcasted_iota(jnp.int32, (width, width), 1)

    def banded(start, gap, order):
        m = jnp.zeros((width, width), f32)
        for tap in range(taps):
            values = unit[tap][:, start * ROWS : start * ROWS + width]
            m = jnp.where(gap == ROWS * order(tap), values, m)
        return m

    for which, plan in enumerate(plans):
        slot = [0, 0]
        for number, stage in enumerate(plan):
            kind = number % 2
            target = matrices[2 * which + kind]
            for at, _ in flat(stage):
                if kind == 0:
                    m = banded(at, row - col, lambda tap: tap).T
                else:
                    m = banded(at - half, col - row, lambda tap: 2 * half - tap)
                target[slot[kind]] = m[: GROUP * ROWS].astype(bf16)
                slot[kind] += 1

    lateral_total = lateral_ref[0]
    for tap in range(1, lat_taps):
        lateral_total = lateral_total + lateral_ref[tap]
    k = lax.broadcasted_iota(jnp.int32, tl_ref.shape, 0)
    j = lax.broadcasted_iota(jnp.int32, tl_ref.shape, 1)
    place = k - LANES - j + lat_taps // 2
    forward = jnp.zeros(tl_ref.shape, f32)
    backward = jnp.zeros(tl_ref.shape, f32)
    for tap in range(lat_taps):
        forward = jnp.where(place == tap, lateral_ref[tap], forward)
        backward = jnp.where(place == lat_taps - 1 - tap, lateral_ref[tap], backward)
    scale = jnp.full((1, TILE), lateral_total, f32)
    tl_ref[...] = (forward / scale).astype(bf16)
    tm_ref[...] = (backward / scale).astype(bf16)


def bands(psf_bank, lateral_psf, band_index, planes, halo):
    plans = stages(planes, psf_bank.shape[1] // 2)
    spread = jnp.pad(band_index, (halo, halo + SPAN), constant_values=-1)
    first = lax.axis_index("cam") * planes
    length = planes + 2 * halo + SPAN
    mine = lax.dynamic_slice_in_dim(spread, first, length, 0)
    index = jnp.broadcast_to(mine[:, None], (length, ROWS)).reshape(1, length * ROWS)
    smem = pl.BlockSpec(memory_space=pltpu.SMEM)
    vmem = pl.BlockSpec(memory_space=pltpu.VMEM)
    counts = [
        sum(len(flat(stage)) for stage in plan[kind::2]) for plan in plans for kind in range(2)
    ]
    strip = jax.ShapeDtypeStruct((TILE + 2 * LANES, TILE), jnp.bfloat16)
    return pl.pallas_call(
        functools.partial(bands_kernel, psf_bank.shape[1], lateral_psf.shape[0], plans),
        in_specs=[smem, smem, vmem],
        out_specs=[vmem] * (len(counts) + 2),
        out_shape=[
            jax.ShapeDtypeStruct((n, GROUP * ROWS, SPAN * ROWS), jnp.bfloat16) for n in counts
        ]
        + [strip, strip],
        compiler_params=pltpu.CompilerParams(vmem_limit_bytes=BANDS_VMEM),
        cost_estimate=pl.CostEstimate(
            flops=2_000_000_000, bytes_accessed=2_000_000, transcendentals=0
        ),
        name="bands",
    )(psf_bank, lateral_psf, index)


def restore_kernel(plan, inside, half, counts, cut, *refs):
    parts = []
    for count in counts:
        parts.append(refs[:count])
        refs = refs[count:]
    g, gt, tl, tm = refs[:4]
    refs = refs[4:]
    f32 = jnp.float32
    bf16 = jnp.bfloat16
    halo = 2 * ITERS * half
    if not inside:
        q_in, e_in = refs[:2]
        refs = refs[2:]
    buffers = refs[-8:]
    mf, ef, mb, qb, pad, pad_back, done, sems = buffers
    if inside:
        canvas, q_out, e_out = refs[-11:-8]
    else:
        canvas = refs[-9]
    size, columns = mf.shape
    total = size // ROWS
    tiles = -(-columns // TILE)

    for buffer in (pad, pad_back):
        edge = jnp.zeros((buffer.shape[0], LANES), bf16)
        buffer[:, :LANES] = edge
        buffer[:, LANES + columns :] = edge

    at_column = 0
    reach = (2 * ITERS - 1) * half
    for part in parts:
        width = part[0].shape[-1] if part is parts[-1] else 2 * LANES
        skip = part[0].shape[-1] - width
        if inside:
            loads = [(part[0], 0, part[0].shape[0], halo)]
        else:
            low, own, high = part
            count = own.shape[0]
            loads = [
                (low, 0, low.shape[0], 0),
                (own, 0, reach // 2, halo),
                (own, count - reach // 2, count, total - halo - reach),
                (high, 0, high.shape[0], total - halo),
            ]
        for ref, lo, hi, plane in loads:
            rows = slice(plane * ROWS, plane * ROWS + (hi - lo) * ref.shape[1])
            for col in range(0, width, TILE):
                end = min(col + TILE, width)
                whole = ref[lo:hi, :, skip + col : skip + end].reshape(-1, end - col)
                there = slice(at_column + col, at_column + end)
                mb[rows, there] = whole
                mf[rows, there] = whole.astype(f32)
        at_column += width

    q_rows = slice((halo + half) * ROWS, (total - halo - half) * ROWS)
    e_width = half * (2 * ITERS - 2) * ROWS
    e_low = (halo + 2 * half) * ROWS
    e_high = (total - halo - 2 * half) * ROWS - e_width
    if not inside:
        q_height = halo * ROWS
        for q_from in (0, q_in.shape[0] - q_height):
            q_to = q_rows.start + q_from
            qb[q_to : q_to + q_height, :] = q_in[q_from : q_from + q_height, :]
        for e_from, e_to in ((0, e_low), (e_width, e_high)):
            e_first = e_in[e_from : e_from + e_width, :]
            ef[e_to : e_to + e_width, :] = e_first
            mb[e_to : e_to + e_width, :] = e_first.astype(bf16)

    copies = []
    base = canvas.shape[-1] - columns if cut else 0
    limit = canvas.shape[-1] if cut else columns - LANES
    top = ITERS * 2 * half

    def wide(tile):
        return min(TILE, columns - tile * TILE)

    def columns_of(tile):
        return slice(tile * TILE, tile * TILE + wide(tile))

    def within(tile):
        return slice(LANES + tile * TILE, LANES + tile * TILE + wide(tile))

    def around(tile):
        return slice(tile * TILE, tile * TILE + wide(tile) + 2 * LANES)

    def lateral(stage, source, matrix, tile):
        band = matrix[: wide(tile) + 2 * LANES, : wide(tile)]
        height = sum(count for _, count in flat(stage)) * ROWS
        whole = jnp.dot(source[:height, around(tile)], band, preferred_element_type=f32)
        start = 0
        for groups in stage:
            rows = rows_of(groups)
            stop = start + rows.stop - rows.start
            yield groups, rows, whole[start:stop]
            start = stop

    def rows_of(groups):
        return slice(groups[0][0] * ROWS, (groups[-1][0] + groups[-1][1]) * ROWS)

    def axial(matrices, skip, stage, source, target, tile):
        place = 0
        for number, (first, count) in enumerate(flat(stage)):
            low = (first - half) * ROWS
            high = (first + count + half) * ROWS
            r = jnp.dot(
                matrices[skip + number, : count * ROWS, : high - low],
                source[low:high, columns_of(tile)],
                preferred_element_type=f32,
            )
            target[place : place + count * ROWS, within(tile)] = r.astype(bf16)
            place += count * ROWS

    def calls(sweep):
        ahead, back = plan[2 * sweep], plan[2 * sweep + 1]
        skip_ahead = sum(len(flat(stage)) for stage in plan[0 : 2 * sweep : 2])
        skip_back = sum(len(flat(stage)) for stage in plan[1 : 2 * sweep : 2])
        final = sweep == ITERS - 1

        def ratio(tile):
            cols = columns_of(tile)
            for _, rows, blurred in lateral(ahead, pad, tl, tile):
                b = blurred + BACKGROUND
                guess = pl.reciprocal(b, approx=True)
                guess = guess * (2.0 - b * guess)
                qb[rows, cols] = (mf[rows, cols] * guess).astype(bf16)

        def update(tile):
            cols = columns_of(tile)
            for groups, rows, d in lateral(back, pad_back, tm, tile):
                e = (mf if sweep == 0 else ef)[rows, cols] * d
                if not final:
                    ef[rows, cols] = e
                    mb[rows, cols] = e.astype(bf16)
                    continue
                start = base + tile * TILE
                drop = cut if tile == 0 else 0
                keep = min(wide(tile), limit - start)
                if keep > drop:
                    first, count = groups[0][0] - top, e.shape[0] // ROWS
                    where = (slice(first, first + count), slice(None))
                    here = slice(tile * TILE + drop, tile * TILE + keep)
                    done[where + (here,)] = e.reshape(-1, ROWS, wide(tile))[:, :, drop:keep].astype(bf16)
                    copy = pltpu.make_async_copy(
                        done.at[where + (here,)],
                        canvas.at[where + (slice(start + drop, start + keep),)],
                        sems.at[len(copies)],
                    )
                    copy.start()
                    copies.append(copy)

        return (
            (0, functools.partial(axial, g, skip_ahead, ahead, mb, pad)),
            (2, ratio),
            (3, functools.partial(axial, gt, skip_back, back, qb, pad_back)),
            (5, update),
        )

    waves = [(6 * sweep + lag, call) for sweep in range(ITERS) for lag, call in calls(sweep)]
    for step in range(tiles + max(lag for lag, _ in waves)):
        for lag, call in waves:
            if 0 <= step - lag < tiles:
                call(step - lag)

    if inside:
        q_out[...] = qb[q_rows, :]
        e_out[:e_width, :] = ef[e_low : e_low + e_width, :]
        e_out[e_width:, :] = ef[e_high : e_high + e_width, :]
    for copy in copies:
        copy.wait()


def restore(parts, matrices, state, canvas, plan, inside, planes, half, columns):
    later = len(parts) > 1
    width = parts[-1][0].shape[-1] + (2 * LANES if later else 0)
    halo = 2 * ITERS * half
    height = (planes + 2 * halo) * ROWS
    bf16 = jnp.bfloat16
    vmem = pl.BlockSpec(memory_space=pltpu.VMEM)
    hbm = pl.BlockSpec(memory_space=pltpu.HBM)
    operands = [array for part in parts for array in part] + [*matrices, *state]
    specs = [vmem] * len(operands)
    aliases = {}
    if canvas is not None:
        aliases = {len(operands): 0}
        operands.append(canvas)
        specs.append(hbm)
    tallest = max(sum(count for _, count in flat(stage)) for stage in plan) * ROWS
    results = [jax.ShapeDtypeStruct((planes, ROWS, columns), bf16)]
    if inside:
        results += [
            jax.ShapeDtypeStruct(((planes - 2 * half) * ROWS, width), bf16),
            jax.ShapeDtypeStruct((2 * half * (2 * ITERS - 2) * ROWS, width), jnp.float32),
        ]
    return pl.pallas_call(
        functools.partial(
            restore_kernel, plan, inside, half, [len(part) for part in parts], LANES if later else 0
        ),
        in_specs=specs,
        out_specs=[hbm] + [vmem] * (len(results) - 1),
        out_shape=results,
        input_output_aliases=aliases,
        scratch_shapes=[
            pltpu.VMEM((height, width), jnp.float32),
            pltpu.VMEM((height, width), jnp.float32),
            pltpu.VMEM((height, width), bf16),
            pltpu.VMEM((height, width), bf16),
            pltpu.VMEM((tallest, width + 2 * LANES), bf16),
            pltpu.VMEM((tallest, width + 2 * LANES), bf16),
            pltpu.VMEM((planes, ROWS, width), bf16),
            pltpu.SemaphoreType.DMA((-(-width // TILE) * (1 if inside else 2),)),
        ],
        compiler_params=pltpu.CompilerParams(vmem_limit_bytes=RESTORE_VMEM),
        cost_estimate=pl.CostEstimate(
            flops=5_000_000_000, bytes_accessed=8_000_000, transcendentals=0
        ),
        name="inside" if inside else "ends",
    )(*operands)


def local(
    raw_frames,
    frame_order,
    dark_frame,
    flat_gain,
    stripe_band,
    shear_offset,
    shear_fraction,
    band_index,
    psf_bank,
    lateral_psf,
):
    half = psf_bank.shape[1] // 2
    planes = shear_offset.shape[0]
    columns = raw_frames.shape[-1]
    halo = 2 * ITERS * half
    plans = stages(planes, half)
    count = lax.axis_size("cam")
    forward = [(i, i + 1) for i in range(count - 1)]
    backward = [(i + 1, i) for i in range(count - 1)]
    *axial, forward_lateral, backward_lateral = bands(psf_bank, lateral_psf, band_index, planes, halo)
    matrices = [
        (*axial[2 * which : 2 * which + 2], forward_lateral, backward_lateral) for which in range(2)
    ]
    depth = halo // 2
    first_piece = frame_side(
        raw_frames, frame_order, dark_frame, flat_gain, stripe_band, shear_offset, shear_fraction, 0, SPLIT
    )
    first_piece, later_order = lax.optimization_barrier((first_piece, frame_order))
    second_piece = frame_side(
        raw_frames, later_order, dark_frame, flat_gain, stripe_band, shear_offset, shear_fraction,
        SPLIT, columns,
    )
    def exchange(piece):
        return lax.all_to_all(piece, "brick", split_axis=0, concat_axis=0, tiled=True)

    def with_halo(centre):
        low = lax.ppermute(centre[-depth:], "cam", forward)
        high = lax.ppermute(centre[:depth], "cam", backward)
        return low, centre, high

    def inside(parts, canvas):
        centres = [(centre,) for _, centre, _ in parts]
        canvas, *state = restore(
            centres, matrices[0], (), canvas, plans[0], True, planes, half, columns
        )
        return canvas, state

    def ends(parts, state, canvas):
        return restore(
            parts, matrices[1], state, canvas, plans[1], False, planes, half, columns
        )[0]

    first, second_piece, matrices = lax.optimization_barrier(
        (exchange(first_piece), second_piece, matrices)
    )
    first_part = with_halo(first)
    canvas, first_state = inside([first_part], None)
    second, first_state = lax.optimization_barrier((exchange(second_piece), first_state))
    second_part = with_halo(second)
    canvas, second_state = inside([first_part, second_part], canvas)
    canvas = ends([first_part], first_state, canvas)
    return ends([first_part, second_part], second_state, canvas)


def solution(mesh):
    placed = (
        P(("cam", "brick"), None, None),
        P(("cam", "brick"), None),
        P(),
        P(),
        P(),
        P("cam"),
        P("cam"),
        P(),
        P(),
        P(),
    )
    return jax.shard_map(
        local, mesh=mesh, in_specs=placed, out_specs=P("cam", "brick", None), check_vma=False
    )
```

```python
import functools

import jax
import jax.numpy as jnp
from jax import lax
from jax.experimental import pallas as pl
from jax.experimental.pallas import tpu as pltpu
from jax.sharding import PartitionSpec as P

SHEAR = 512
ITERS = 2
BACKGROUND = 1.0

LANES = 128
TILE = 256
ROWS = 8
BLOCK_ROWS = 128
LEAD = SHEAR // LANES + 1
SPLIT = 1152
VMEM = 60 * 1024 * 1024
BANDS_VMEM = 20 * 1024 * 1024
RESTORE_VMEM = 26 * 1024 * 1024
LATER_VMEM = 20 * 1024 * 1024
GROUP = 24
SPAN = 36


def frame_kernel(
    first, count,
    order_ref, offset_ref, fraction_ref,
    raw_prev, raw_main, raw_next,
    dark_prev, dark_main, dark_next,
    gain_prev, gain_main, gain_next,
    band_ref, out_ref, scratch, level,
):
    step = pl.program_id(0)
    steps = pl.num_programs(0)
    rows = BLOCK_ROWS + 16
    brick = lax.axis_index("brick")
    f32 = jnp.float32
    bf16 = jnp.bfloat16
    base = first - LEAD

    @pl.when(step == 0)
    def _():
        if base < 0:
            scratch[:, :, : -base * LANES] = jnp.zeros((2, BLOCK_ROWS, -base * LANES), f32)

    has_prev = (step > 0).astype(f32)
    has_next = (step < steps - 1).astype(f32)
    frames = [jnp.where(order_ref[0, 0] == place, 0, 1) for place in range(2)]

    used = range(max(base, 0), first + count)
    for tile in used:
        cols = pl.ds(tile * LANES, LANES)
        for part, keep, start in ((0, slice(8, 16), 0), (1, slice(None), 8), (2, slice(0, 8), rows - 8)):
            dark = (dark_prev, dark_main, dark_next)[part][:, cols].astype(f32)[keep]
            gain = (gain_prev, gain_main, gain_next)[part][:, cols].astype(f32)[keep]
            if part != 1:
                gain = gain * (has_prev, None, has_next)[part]
            raw = (raw_prev, raw_main, raw_next)[part]
            for place in range(2):
                f = (raw[frames[place], :, cols].astype(f32)[keep] - dark) * gain
                level[place, tile - used[0], start : start + f.shape[0], :] = f

    zero = jnp.minimum(step, 0)
    taps = band_ref.shape[0]
    for tile in used:
        band = band_ref[:, pl.ds(tile * LANES, LANES)]
        for place in range(2):
            here = tile - used[0]
            out = level[place, here, 8 : 8 + BLOCK_ROWS, :] * (1.0 + band[taps // 2 : taps // 2 + 1])
            for tap in range(taps):
                if tap != taps // 2:
                    shifted = level[place, here, pl.ds(zero + 8 + tap - taps // 2, BLOCK_ROWS), :]
                    out = out + band[tap : tap + 1] * shifted
            scratch[place, :, pl.ds((tile - base) * LANES, LANES)] = out.astype(bf16).astype(f32)

    lane = lax.broadcasted_iota(jnp.int32, (BLOCK_ROWS, LANES), 1)
    bricks = BLOCK_ROWS // ROWS
    for place in range(2):
        amount = offset_ref[brick * 2 + place]
        weight = fraction_ref[brick * 2 + place]
        whole = amount // LANES
        part = amount % LANES
        near_mask = lane < part
        far_mask = lane < part + 1

        def turned(tile):
            start = (tile - base - whole) * LANES
            x = scratch[place, :, pl.ds(pl.multiple_of(start, LANES), LANES)]
            return (1.0 - weight) * pltpu.roll(x, part, 1), weight * pltpu.roll(x, (part + 1) % LANES, 1)

        last = turned(first - 1)
        for tile in range(first, first + count):
            now = turned(tile)
            mixed = jnp.where(near_mask, last[0], now[0]) + jnp.where(far_mask, last[1], now[1])
            last = now
            out_ref[:, place * ROWS : (place + 1) * ROWS, pl.ds((tile - first) * LANES, LANES)] = (
                mixed.reshape(bricks, ROWS, LANES).astype(bf16)
            )


def frame_side(raw, order, dark, gain, band, offset, fraction, lo, hi):
    _, frame_rows, columns = raw.shape
    steps = frame_rows // BLOCK_ROWS
    bricks = frame_rows // ROWS
    per = BLOCK_ROWS // 16
    last = frame_rows // 16 - 1
    smem = pl.BlockSpec(memory_space=pltpu.SMEM)
    first, count = lo // LANES, (hi - lo) // LANES
    if lo == 0:
        columns = hi

    def three(lead):
        zeros = (0,) * len(lead)
        return [
            pl.BlockSpec(lead + (16, columns), lambda i: zeros + (jnp.maximum(per * i - 1, 0), 0)),
            pl.BlockSpec(lead + (BLOCK_ROWS, columns), lambda i: zeros + (i, 0)),
            pl.BlockSpec(lead + (16, columns), lambda i: zeros + (jnp.minimum(per * i + per, last), 0)),
        ]

    return pl.pallas_call(
        functools.partial(frame_kernel, first, count),
        grid=(steps,),
        in_specs=[smem, smem, smem]
        + three((2,)) + three(()) + three(())
        + [pl.BlockSpec((band.shape[0], columns), lambda i: (0, 0))],
        out_specs=pl.BlockSpec((BLOCK_ROWS // ROWS, 2 * ROWS, hi - lo), lambda i: (i, 0, 0)),
        out_shape=jax.ShapeDtypeStruct((bricks, 2 * ROWS, hi - lo), jnp.bfloat16),
        scratch_shapes=[
            pltpu.VMEM((2, BLOCK_ROWS, (LEAD + count) * LANES), jnp.float32),
            pltpu.VMEM((2, min(first, LEAD) + count, BLOCK_ROWS + 16, LANES), jnp.float32),
        ],
        compiler_params=pltpu.CompilerParams(vmem_limit_bytes=VMEM if lo == 0 else LATER_VMEM),
        cost_estimate=pl.CostEstimate(
            flops=8_000_000_000, bytes_accessed=6_500_000, transcendentals=0
        ),
        name="frame_side",
    )(order, offset, fraction, raw, raw, raw, dark, dark, dark, gain, gain, gain, band)


def stages(planes, half):
    halo = 2 * ITERS * half
    total = planes + 2 * halo

    def cut(lo, hi, most):
        parts = -(-(hi - lo) // most)
        size = -(-(hi - lo) // (2 * parts)) * 2
        return [(at, min(size, hi - at)) for at in range(lo, hi, size)]

    inner, outer = [], []
    for stage in range(1, 2 * ITERS + 1):
        reach = stage * half
        lo, hi = halo + reach, total - halo - reach
        inner.append([cut(lo, hi, GROUP)])
        outer.append([cut(reach, lo, GROUP), cut(hi, total - reach, GROUP)])
    return inner, outer


def flat(stage):
    return [group for groups in stage for group in groups]


def bands_kernel(taps, lat_taps, plans, psf_ref, lateral_ref, index_ref, *outs):
    matrices, (tl_ref, tm_ref) = outs[:-2], outs[-2:]
    f32 = jnp.float32
    bf16 = jnp.bfloat16
    half = taps // 2
    width = SPAN * ROWS
    index = index_ref[...]
    raw = []
    for tap in range(taps):
        value = jnp.zeros(index.shape, f32)
        for kernel in range(psf_ref.shape[0]):
            value = jnp.where(index == kernel, psf_ref[kernel, tap], value)
        raw.append(value)
    total = functools.reduce(lambda a, b: a + b, raw)
    total = jnp.where(total > 0.0, total, 1.0)
    unit = [value / total for value in raw]
    row = lax.broadcasted_iota(jnp.int32, (width, width), 0)
    col = lax.broadcasted_iota(jnp.int32, (width, width), 1)

    def banded(start, gap, order):
        m = jnp.zeros((width, width), f32)
        for tap in range(taps):
            values = unit[tap][:, start * ROWS : start * ROWS + width]
            m = jnp.where(gap == ROWS * order(tap), values, m)
        return m

    for which, plan in enumerate(plans):
        slot = [0, 0]
        for number, stage in enumerate(plan):
            kind = number % 2
            target = matrices[2 * which + kind]
            for at, _ in flat(stage):
                if kind == 0:
                    m = banded(at, row - col, lambda tap: tap).T
                else:
                    m = banded(at - half, col - row, lambda tap: 2 * half - tap)
                target[slot[kind]] = m[: GROUP * ROWS].astype(bf16)
                slot[kind] += 1

    lateral_total = lateral_ref[0]
    for tap in range(1, lat_taps):
        lateral_total = lateral_total + lateral_ref[tap]
    k = lax.broadcasted_iota(jnp.int32, tl_ref.shape, 0)
    j = lax.broadcasted_iota(jnp.int32, tl_ref.shape, 1)
    place = k - LANES - j + lat_taps // 2
    forward = jnp.zeros(tl_ref.shape, f32)
    backward = jnp.zeros(tl_ref.shape, f32)
    for tap in range(lat_taps):
        forward = jnp.where(place == tap, lateral_ref[tap], forward)
        backward = jnp.where(place == lat_taps - 1 - tap, lateral_ref[tap], backward)
    scale = jnp.full((1, TILE), lateral_total, f32)
    tl_ref[...] = (forward / scale).astype(bf16)
    tm_ref[...] = (backward / scale).astype(bf16)


def bands(psf_bank, lateral_psf, band_index, planes, halo):
    plans = stages(planes, psf_bank.shape[1] // 2)
    spread = jnp.pad(band_index, (halo, halo + SPAN), constant_values=-1)
    first = lax.axis_index("cam") * planes
    length = planes + 2 * halo + SPAN
    mine = lax.dynamic_slice_in_dim(spread, first, length, 0)
    index = jnp.broadcast_to(mine[:, None], (length, ROWS)).reshape(1, length * ROWS)
    smem = pl.BlockSpec(memory_space=pltpu.SMEM)
    vmem = pl.BlockSpec(memory_space=pltpu.VMEM)
    counts = [
        sum(len(flat(stage)) for stage in plan[kind::2]) for plan in plans for kind in range(2)
    ]
    strip = jax.ShapeDtypeStruct((TILE + 2 * LANES, TILE), jnp.bfloat16)
    return pl.pallas_call(
        functools.partial(bands_kernel, psf_bank.shape[1], lateral_psf.shape[0], plans),
        in_specs=[smem, smem, vmem],
        out_specs=[vmem] * (len(counts) + 2),
        out_shape=[
            jax.ShapeDtypeStruct((n, GROUP * ROWS, SPAN * ROWS), jnp.bfloat16) for n in counts
        ]
        + [strip, strip],
        compiler_params=pltpu.CompilerParams(vmem_limit_bytes=BANDS_VMEM),
        cost_estimate=pl.CostEstimate(
            flops=2_000_000_000, bytes_accessed=2_000_000, transcendentals=0
        ),
        name="bands",
    )(psf_bank, lateral_psf, index)


def restore_kernel(plan, inside, half, counts, cut, *refs):
    parts = []
    for count in counts:
        parts.append(refs[:count])
        refs = refs[count:]
    g, gt, tl, tm = refs[:4]
    refs = refs[4:]
    f32 = jnp.float32
    bf16 = jnp.bfloat16
    halo = 2 * ITERS * half
    if not inside:
        q_in, e_in = refs[:2]
        refs = refs[2:]
    buffers = refs[-8:]
    mf, ef, mb, qb, pad, pad_back, done, sems = buffers
    if inside:
        canvas, q_out, e_out = refs[-11:-8]
    else:
        canvas = refs[-9]
    size, columns = mf.shape
    total = size // ROWS
    tiles = -(-columns // TILE)

    for buffer in (pad, pad_back):
        edge = jnp.zeros((buffer.shape[0], LANES), bf16)
        buffer[:, :LANES] = edge
        buffer[:, LANES + columns :] = edge

    at_column = 0
    reach = (2 * ITERS - 1) * half
    for part in parts:
        width = part[0].shape[-1] if part is parts[-1] else 2 * LANES
        skip = part[0].shape[-1] - width
        if inside:
            loads = [(part[0], 0, part[0].shape[0], halo)]
        else:
            low, own, high = part
            count = own.shape[0]
            loads = [
                (low, 0, low.shape[0], 0),
                (own, 0, reach // 2, halo),
                (own, count - reach // 2, count, total - halo - reach),
                (high, 0, high.shape[0], total - halo),
            ]
        for ref, lo, hi, plane in loads:
            rows = slice(plane * ROWS, plane * ROWS + (hi - lo) * ref.shape[1])
            for col in range(0, width, TILE):
                end = min(col + TILE, width)
                whole = ref[lo:hi, :, skip + col : skip + end].reshape(-1, end - col)
                there = slice(at_column + col, at_column + end)
                mb[rows, there] = whole
                mf[rows, there] = whole.astype(f32)
        at_column += width

    q_rows = slice((halo + half) * ROWS, (total - halo - half) * ROWS)
    e_width = half * (2 * ITERS - 2) * ROWS
    e_low = (halo + 2 * half) * ROWS
    e_high = (total - halo - 2 * half) * ROWS - e_width
    if not inside:
        q_height = halo * ROWS
        for q_from in (0, q_in.shape[0] - q_height):
            q_to = q_rows.start + q_from
            qb[q_to : q_to + q_height, :] = q_in[q_from : q_from + q_height, :]
        for e_from, e_to in ((0, e_low), (e_width, e_high)):
            e_first = e_in[e_from : e_from + e_width, :]
            ef[e_to : e_to + e_width, :] = e_first
            mb[e_to : e_to + e_width, :] = e_first.astype(bf16)

    copies = []
    base = canvas.shape[-1] - columns if cut else 0
    limit = canvas.shape[-1] if cut else columns - LANES
    top = ITERS * 2 * half

    def wide(tile):
        return min(TILE, columns - tile * TILE)

    def columns_of(tile):
        return slice(tile * TILE, tile * TILE + wide(tile))

    def within(tile):
        return slice(LANES + tile * TILE, LANES + tile * TILE + wide(tile))

    def around(tile):
        return slice(tile * TILE, tile * TILE + wide(tile) + 2 * LANES)

    def lateral(stage, source, matrix, tile):
        band = matrix[: wide(tile) + 2 * LANES, : wide(tile)]
        height = sum(count for _, count in flat(stage)) * ROWS
        whole = jnp.dot(source[:height, around(tile)], band, preferred_element_type=f32)
        start = 0
        for groups in stage:
            rows = rows_of(groups)
            stop = start + rows.stop - rows.start
            yield groups, rows, whole[start:stop]
            start = stop

    def rows_of(groups):
        return slice(groups[0][0] * ROWS, (groups[-1][0] + groups[-1][1]) * ROWS)

    def axial(matrices, skip, stage, source, target, tile):
        place = 0
        for number, (first, count) in enumerate(flat(stage)):
            low = (first - half) * ROWS
            high = (first + count + half) * ROWS
            r = jnp.dot(
                matrices[skip + number, : count * ROWS, : high - low],
                source[low:high, columns_of(tile)],
                preferred_element_type=f32,
            )
            target[place : place + count * ROWS, within(tile)] = r.astype(bf16)
            place += count * ROWS

    def calls(sweep):
        ahead, back = plan[2 * sweep], plan[2 * sweep + 1]
        skip_ahead = sum(len(flat(stage)) for stage in plan[0 : 2 * sweep : 2])
        skip_back = sum(len(flat(stage)) for stage in plan[1 : 2 * sweep : 2])
        final = sweep == ITERS - 1

        def ratio(tile):
            cols = columns_of(tile)
            for _, rows, blurred in lateral(ahead, pad, tl, tile):
                b = blurred + BACKGROUND
                guess = pl.reciprocal(b, approx=True)
                guess = guess * (2.0 - b * guess)
                qb[rows, cols] = (mf[rows, cols] * guess).astype(bf16)

        def update(tile):
            cols = columns_of(tile)
            for groups, rows, d in lateral(back, pad_back, tm, tile):
                e = (mf if sweep == 0 else ef)[rows, cols] * d
                if not final:
                    ef[rows, cols] = e
                    mb[rows, cols] = e.astype(bf16)
                    continue
                start = base + tile * TILE
                drop = cut if tile == 0 else 0
                keep = min(wide(tile), limit - start)
                if keep > drop:
                    first, count = groups[0][0] - top, e.shape[0] // ROWS
                    where = (slice(first, first + count), slice(None))
                    here = slice(tile * TILE + drop, tile * TILE + keep)
                    done[where + (here,)] = e.reshape(-1, ROWS, wide(tile))[:, :, drop:keep].astype(bf16)
                    copy = pltpu.make_async_copy(
                        done.at[where + (here,)],
                        canvas.at[where + (slice(start + drop, start + keep),)],
                        sems.at[len(copies)],
                    )
                    copy.start()
                    copies.append(copy)

        return (
            (0, functools.partial(axial, g, skip_ahead, ahead, mb, pad)),
            (2, ratio),
            (3, functools.partial(axial, gt, skip_back, back, qb, pad_back)),
            (5, update),
        )

    waves = [(6 * sweep + lag, call) for sweep in range(ITERS) for lag, call in calls(sweep)]
    for step in range(tiles + max(lag for lag, _ in waves)):
        for lag, call in waves:
            if 0 <= step - lag < tiles:
                call(step - lag)

    if inside:
        q_out[...] = qb[q_rows, :]
        e_out[:e_width, :] = ef[e_low : e_low + e_width, :]
        e_out[e_width:, :] = ef[e_high : e_high + e_width, :]
    for copy in copies:
        copy.wait()


def restore(parts, matrices, state, canvas, plan, inside, planes, half, columns):
    later = len(parts) > 1
    width = parts[-1][0].shape[-1] + (2 * LANES if later else 0)
    halo = 2 * ITERS * half
    height = (planes + 2 * halo) * ROWS
    bf16 = jnp.bfloat16
    vmem = pl.BlockSpec(memory_space=pltpu.VMEM)
    hbm = pl.BlockSpec(memory_space=pltpu.HBM)
    operands = [array for part in parts for array in part] + [*matrices, *state]
    specs = [vmem] * len(operands)
    aliases = {}
    if canvas is not None:
        aliases = {len(operands): 0}
        operands.append(canvas)
        specs.append(hbm)
    tallest = max(sum(count for _, count in flat(stage)) for stage in plan) * ROWS
    results = [jax.ShapeDtypeStruct((planes, ROWS, columns), bf16)]
    if inside:
        results += [
            jax.ShapeDtypeStruct(((planes - 2 * half) * ROWS, width), bf16),
            jax.ShapeDtypeStruct((2 * half * (2 * ITERS - 2) * ROWS, width), jnp.float32),
        ]
    return pl.pallas_call(
        functools.partial(
            restore_kernel, plan, inside, half, [len(part) for part in parts], LANES if later else 0
        ),
        in_specs=specs,
        out_specs=[hbm] + [vmem] * (len(results) - 1),
        out_shape=results,
        input_output_aliases=aliases,
        scratch_shapes=[
            pltpu.VMEM((height, width), jnp.float32),
            pltpu.VMEM((height, width), jnp.float32),
            pltpu.VMEM((height, width), bf16),
            pltpu.VMEM((height, width), bf16),
            pltpu.VMEM((tallest, width + 2 * LANES), bf16),
            pltpu.VMEM((tallest, width + 2 * LANES), bf16),
            pltpu.VMEM((planes, ROWS, width), bf16),
            pltpu.SemaphoreType.DMA((-(-width // TILE) * (1 if inside else 2),)),
        ],
        compiler_params=pltpu.CompilerParams(vmem_limit_bytes=RESTORE_VMEM),
        cost_estimate=pl.CostEstimate(
            flops=5_000_000_000, bytes_accessed=8_000_000, transcendentals=0
        ),
        name="inside" if inside else "ends",
    )(*operands)


def local(
    raw_frames,
    frame_order,
    dark_frame,
    flat_gain,
    stripe_band,
    shear_offset,
    shear_fraction,
    band_index,
    psf_bank,
    lateral_psf,
):
    half = psf_bank.shape[1] // 2
    planes = shear_offset.shape[0]
    columns = raw_frames.shape[-1]
    halo = 2 * ITERS * half
    plans = stages(planes, half)
    count = lax.axis_size("cam")
    forward = [(i, i + 1) for i in range(count - 1)]
    backward = [(i + 1, i) for i in range(count - 1)]
    *axial, forward_lateral, backward_lateral = bands(psf_bank, lateral_psf, band_index, planes, halo)
    matrices = [
        (*axial[2 * which : 2 * which + 2], forward_lateral, backward_lateral) for which in range(2)
    ]
    depth = halo // 2
    first_piece = frame_side(
        raw_frames, frame_order, dark_frame, flat_gain, stripe_band, shear_offset, shear_fraction, 0, SPLIT
    )
    first_piece, later_order = lax.optimization_barrier((first_piece, frame_order))
    second_piece = frame_side(
        raw_frames, later_order, dark_frame, flat_gain, stripe_band, shear_offset, shear_fraction,
        SPLIT, columns,
    )
    def exchange(piece):
        return lax.all_to_all(piece, "brick", split_axis=0, concat_axis=0, tiled=True)

    def with_halo(centre):
        low = lax.ppermute(centre[-depth:], "cam", forward)
        high = lax.ppermute(centre[:depth], "cam", backward)
        return low, centre, high

    def inside(parts, canvas):
        centres = [(centre,) for _, centre, _ in parts]
        canvas, *state = restore(
            centres, matrices[0], (), canvas, plans[0], True, planes, half, columns
        )
        return canvas, state

    def ends(parts, state, canvas):
        return restore(
            parts, matrices[1], state, canvas, plans[1], False, planes, half, columns
        )[0]

    first, second_piece, matrices = lax.optimization_barrier(
        (exchange(first_piece), second_piece, matrices)
    )
    first_part = with_halo(first)
    canvas, first_state = inside([first_part], None)
    second, first_state = lax.optimization_barrier((exchange(second_piece), first_state))
    second_part = with_halo(second)
    canvas, second_state = inside([first_part, second_part], canvas)
    canvas = ends([first_part], first_state, canvas)
    return ends([first_part, second_part], second_state, canvas)


def solution(mesh):
    placed = (
        P(("cam", "brick"), None, None),
        P(("cam", "brick"), None),
        P(),
        P(),
        P(),
        P("cam"),
        P("cam"),
        P(),
        P(),
        P(),
    )
    return jax.shard_map(
        local, mesh=mesh, in_specs=placed, out_specs=P("cam", "brick", None), check_vma=False
    )
```
